32 devices in a mesh: seq: 8 (over y, x, core), mp: 4 (over z).
Axes of the slice: x: 2, y: 2, z: 4, core: 2. Of those that a mesh axis runs over, the one named last changes fastest.
Arguments:
- normed: bfloat16 [4096, 2048], P('seq'), may hold values from -40 to 40
- out_cotangent: bfloat16 [4096, 2048], P('seq'), may hold values from -6 to 6
- segments: int32 [4096], replicated, may hold values from 0 to 15, never falling along the last dimension, each value on 1 to 512 neighbouring positions
- band_mask: int32 [32, 4], P('seq'), may hold values 0 or 1
- query_weight: bfloat16 [2048, 2048], P(None, 'mp'), may hold values from -0.125 to 0.125
- key_value_weight: bfloat16 [2048, 8, 128], P(None, 'mp'), may hold values from -0.125 to 0.125
- out_weight: bfloat16 [2048, 2048], P('mp'), may hold values from -0.125 to 0.125
Outputs:
- context: bfloat16 [4096, 2048], P('seq', 'mp')
- input_grad: bfloat16 [4096, 2048], P('seq', 'mp')
- key_value_gradient: float32 [2048, 8, 128], P(None, 'mp')
The draws below stay inside these ranges and needn't reach their ends.
Inputs may be any that keep to these rules, and one draw needn't show every extreme that they name: `segments`: document ids never fall along the sequence; each document holds 1 to 512 tokens, one exactly 512.
All inputs are finite; a program needn't handle non-finite values. No bound on the sum of `band_mask` on one device may be relied on, other than what follows from the above.
Results may differ from the reference program's by a relative error of at most 0.039.
The reference program's roundings to bfloat16 on the way count: a program that leaves them out, or rounds other values in their place, can miss the bound.
Values may be sent and summed in bfloat16 or wider, within the bound.
A program may use at most 64 MiB of HBM per device.

```python
import math
import jax
import jax.numpy as jnp
import numpy as np
from jax import lax

MODEL_DIM = 2048
QUERY_HEADS = 32
KEY_VALUE_HEADS = 8
HEAD_DIM = 64
BAND_BLOCK = 128
TOK_DEV = 512
TOKENS = 4096
N_MP = 4


def draw_normed(key, part):
    first_key = jax.random.fold_in(key, 0)
    row_group = jnp.arange(TOKENS, dtype=jnp.int32) // TOK_DEV % 16
    column_group = jnp.arange(MODEL_DIM, dtype=jnp.int32) * 16 // MODEL_DIM
    heavy = jnp.where(row_group[:, None] == column_group[None, :], 3.0, 1.0).astype(jnp.float32)
    values = jax.random.normal(first_key, (TOKENS, MODEL_DIM), jnp.float32)
    return jnp.clip(values * heavy, -40.0, 40.0).astype(jnp.bfloat16)


def set_ends(entries, stream_key, smallest, top_value):
    spot = [jax.random.randint(jax.random.fold_in(stream_key, axis), (), 0, length) for axis, length in enumerate(entries.shape)]
    longest = entries.shape.index(max(entries.shape))
    neighbour = spot[:longest] + [(spot[longest] + 1) % entries.shape[longest]] + spot[longest + 1:]
    return entries.at[tuple(spot)].set(smallest).at[tuple(neighbour)].set(top_value)


def steps_of(key, extent, cuts, least, largest):
    loudness, own = 1.0, jax.random.fold_in(key, 6)
    for dim, parts in cuts:
        draws = jnp.exp(jax.random.uniform(jax.random.fold_in(own, dim), (parts,), jnp.float32, least / len(cuts), largest / len(cuts)))
        loudness = loudness * jnp.repeat(draws, extent[dim] // parts).reshape([-1 if axis == dim else 1 for axis in range(len(extent))])
    return loudness


def split_up(number_of, total, limit, slope):
    weights = [(1 << 20) // math.isqrt(standing ** slope) + 1 for standing in range(2, number_of + 1)]
    surplus, counts = total - limit - (number_of - 1), [1] * (number_of - 1)
    while surplus > 0:
        free = [i for i in range(number_of - 1) if counts[i] < limit]
        whole, left = sum([weights[i] for i in free]), surplus
        for i in free:
            more = min(limit - counts[i], max(1, left * weights[i] // whole), surplus)
            counts[i] = counts[i] + more
            surplus = surplus - more
    return np.array([limit] + counts)


def uneven_parts(own_key, count, total, limit, lean):
    if count == 2:
        one = jax.random.randint(own_key, (), max(1, total - limit), min(limit, total - 1) + 1)
        return jnp.stack([one, total - one])
    sizes = jnp.asarray(split_up(count, total, limit, lean), jnp.int32)
    pairs = (count - 1) // 2
    giver, sink = sizes[1:1 + 2 * pairs:2], sizes[2:2 + 2 * pairs:2]
    slack = jnp.minimum(giver - 1, limit - sink)
    shifted = jax.random.randint(jax.random.fold_in(own_key, 1), (pairs,), 0, 1 << 20) % (slack + 1)
    sizes = sizes.at[1:1 + 2 * pairs:2].set(giver - shifted).at[2:2 + 2 * pairs:2].set(sink + shifted)
    return sizes[jax.random.permutation(jax.random.fold_in(own_key, 2), count)]


def scatter_about(stream_key, extent, deviation, bound, shards=(), held_as=jnp.bfloat16):
    level = steps_of(stream_key, extent, shards, -0.22, 0.18) if shards else 1.0
    drawn = jax.random.normal(stream_key, extent, jnp.float32) * deviation * level
    return jnp.minimum(jnp.maximum(drawn, -bound), bound).astype(held_as)


def setup_inputs(seed: int = 0) -> dict:
    splits = jax.random.split(jax.random.key(seed), 8)
    normed = draw_normed(jax.random.fold_in(splits[7], 71), 0)
    out_cotangent = scatter_about(splits[1], (TOKENS, MODEL_DIM), 1.0, 6.0, ((0, 8),))
    segments = jnp.searchsorted(jnp.cumsum(uneven_parts(splits[2], TOKENS // (2 * BAND_BLOCK), TOKENS, 4 * BAND_BLOCK, 2)), jnp.arange(TOKENS), side="right").astype(jnp.int32)
    band_mask = set_ends((jax.random.randint(splits[3], (TOKENS // BAND_BLOCK, 4), 0, 4) < 3).astype(jnp.int32), jax.random.fold_in(splits[3], 1), 0, 1)
    query_weight = scatter_about(splits[4], (MODEL_DIM, QUERY_HEADS * HEAD_DIM), MODEL_DIM ** -0.5, 0.125, ((1, 4),))
    key_value_weight = scatter_about(splits[5], (MODEL_DIM, KEY_VALUE_HEADS, 2 * HEAD_DIM), MODEL_DIM ** -0.5, 0.125, ((1, 4),))
    out_weight = scatter_about(splits[6], (QUERY_HEADS * HEAD_DIM, MODEL_DIM), (QUERY_HEADS * HEAD_DIM) ** -0.5, 0.125, ((0, 4),))
    return dict(normed=normed, out_cotangent=out_cotangent, segments=segments, band_mask=band_mask, query_weight=query_weight, key_value_weight=key_value_weight, out_weight=out_weight)


neg_fill = -1e+30

def band_allowed(rel_block, mask_cols):
    in_band = rel_block == 0
    in_band = in_band | (rel_block == -2) & (mask_cols[0] == 1)
    in_band = in_band | (rel_block == -1) & (mask_cols[1] == 1)
    in_band = in_band | (rel_block == 1) & (mask_cols[2] == 1)
    in_band = in_band | (rel_block == 2) & (mask_cols[3] == 1)
    return in_band

def reference(normed, out_cotangent, segments, band_mask, query_weight, key_value_weight, out_weight):
    query_group_width = QUERY_HEADS // KEY_VALUE_HEADS
    score_scale = 1.0 / math.sqrt(HEAD_DIM)
    margin = 2 * BAND_BLOCK
    window_rows = BAND_BLOCK + 2 * margin
    key_value_columns = KEY_VALUE_HEADS * 2 * HEAD_DIM
    kv_pair = key_value_weight.reshape(MODEL_DIM, key_value_columns)
    query_vectors = jnp.dot(normed, query_weight, preferred_element_type=jnp.float32).astype(jnp.bfloat16)
    keyval = jnp.dot(normed, kv_pair, preferred_element_type=jnp.float32).astype(jnp.bfloat16)
    context_gradient = jnp.dot(out_cotangent, out_weight.T, preferred_element_type=jnp.float32).astype(jnp.bfloat16)
    key_value_padded = jnp.concatenate([jnp.zeros((margin, key_value_columns), jnp.bfloat16), keyval, jnp.zeros((margin, key_value_columns), jnp.bfloat16)], 0)
    doc_padded = jnp.concatenate([jnp.full((margin,), -1, jnp.int32), segments.astype(jnp.int32), jnp.full((margin,), -1, jnp.int32)], 0)
    key_block = jnp.arange(window_rows, dtype=jnp.int32) // BAND_BLOCK - 2

    def one_block(grad_acc, block_index):
        first_row_index = (block_index * BAND_BLOCK).astype(jnp.int32)
        query_row_block = lax.dynamic_slice_in_dim(query_vectors, first_row_index, BAND_BLOCK, 0).astype(jnp.float32).reshape(BAND_BLOCK, KEY_VALUE_HEADS, query_group_width, HEAD_DIM)
        context_gradient_rows = lax.dynamic_slice_in_dim(context_gradient, first_row_index, BAND_BLOCK, 0).astype(jnp.float32).reshape(BAND_BLOCK, KEY_VALUE_HEADS, query_group_width, HEAD_DIM)
        key_value_rows = lax.dynamic_slice_in_dim(key_value_padded, first_row_index, window_rows, 0).astype(jnp.float32).reshape(window_rows, KEY_VALUE_HEADS, 2 * HEAD_DIM)
        key_rows = key_value_rows[..., :HEAD_DIM]
        value_rows = key_value_rows[..., HEAD_DIM:]
        query_docs = lax.dynamic_slice_in_dim(segments.astype(jnp.int32), first_row_index, BAND_BLOCK, 0)
        key_docs = lax.dynamic_slice_in_dim(doc_padded, first_row_index, window_rows, 0)
        mask_row = lax.dynamic_index_in_dim(band_mask, block_index.astype(jnp.int32), 0, keepdims=False)
        in_band = band_allowed(key_block, mask_row)
        allowed = in_band[None, :] & (query_docs[:, None] == key_docs[None, :])
        scores = jnp.einsum('qhgd,khd->hgqk', query_row_block, key_rows) * score_scale
        masked = jnp.where(allowed, scores, neg_fill)
        row_max = lax.optimization_barrier(jnp.max(masked, axis=-1, keepdims=True))
        row_sum = lax.optimization_barrier(jnp.sum(jnp.exp(masked - row_max), axis=-1, keepdims=True))
        log_norm = row_max + jnp.log(row_sum)
        soft_weights = jnp.exp(masked - log_norm)
        weights_half = lax.optimization_barrier(soft_weights.astype(jnp.bfloat16)).astype(jnp.float32)
        context_rows = jnp.einsum('hgqk,khd->qhgd', weights_half, value_rows).astype(jnp.bfloat16)
        context_full = lax.optimization_barrier(context_rows).astype(jnp.float32)
        delta = jnp.einsum('qhgd,qhgd->hgq', context_gradient_rows, context_full)
        d_prob = jnp.einsum('qhgd,khd->hgqk', context_gradient_rows, value_rows)
        d_score = (soft_weights * (d_prob - delta[..., None]) * score_scale).astype(jnp.bfloat16)
        d_score = lax.optimization_barrier(d_score).astype(jnp.float32)
        d_query_rows = jnp.einsum('hgqk,khd->qhgd', d_score, key_rows).astype(jnp.bfloat16)
        d_key = jnp.einsum('hgqk,qhgd->khd', d_score, query_row_block)
        d_value = jnp.einsum('hgqk,qhgd->khd', weights_half, context_gradient_rows)
        d_pair = jnp.concatenate([d_key, d_value], -1).reshape(window_rows, key_value_columns)
        current = lax.dynamic_slice_in_dim(grad_acc, first_row_index, window_rows, 0)
        grad_acc = lax.dynamic_update_slice_in_dim(grad_acc, current + d_pair, first_row_index, 0)
        return (grad_acc, (context_rows.reshape(BAND_BLOCK, QUERY_HEADS * HEAD_DIM), d_query_rows.reshape(BAND_BLOCK, QUERY_HEADS * HEAD_DIM)))
    grad_start = jnp.zeros((TOKENS + 2 * margin, key_value_columns), jnp.float32)
    block_ids = jnp.arange(TOKENS // BAND_BLOCK, dtype=jnp.int32)
    grad_acc, (context_all, d_query_all) = lax.scan(one_block, grad_start, block_ids)
    context = context_all.reshape(TOKENS, QUERY_HEADS * HEAD_DIM)
    d_query = d_query_all.reshape(TOKENS, QUERY_HEADS * HEAD_DIM)
    key_value_gradient_half = grad_acc[margin:margin + TOKENS].astype(jnp.bfloat16)
    query_cols = QUERY_HEADS * HEAD_DIM // N_MP
    pair_cols = key_value_columns // N_MP
    input_total = jnp.zeros((TOKENS, MODEL_DIM), jnp.float32)
    for member in range(N_MP):
        part_query = jnp.dot(d_query[:, member * query_cols:(member + 1) * query_cols], query_weight[:, member * query_cols:(member + 1) * query_cols].T, preferred_element_type=jnp.float32)
        part_pair = jnp.dot(key_value_gradient_half[:, member * pair_cols:(member + 1) * pair_cols], kv_pair[:, member * pair_cols:(member + 1) * pair_cols].T, preferred_element_type=jnp.float32)
        rounded = lax.optimization_barrier((part_query + part_pair).astype(jnp.bfloat16))
        input_total = input_total + rounded.astype(jnp.float32)
    input_grad = input_total.astype(jnp.bfloat16)
    key_value_gradient = jnp.dot(normed.T, key_value_gradient_half, preferred_element_type=jnp.float32).reshape(MODEL_DIM, KEY_VALUE_HEADS, 2 * HEAD_DIM)
    return (context, input_grad, key_value_gradient)
```

```python
import functools

import jax
import jax.numpy as jnp
from jax import lax
from jax.experimental import pallas as pl
from jax.experimental.pallas import tpu as pltpu
from jax.sharding import PartitionSpec as P

QUERY_HEADS = 32
KEY_VALUE_HEADS = 8
GROUP = QUERY_HEADS // KEY_VALUE_HEADS
HEAD_DIM = 64
BLOCK = 128
MARGIN = 2 * BLOCK
WINDOW = BLOCK + 2 * MARGIN
SCALE = 0.125
AHEAD = 2

MESH = pl.DeviceIdType.MESH
NT = (((1,), (1,)), ((), ()))
f32 = jnp.float32
bf16 = jnp.bfloat16
ANY = pl.BlockSpec(memory_space=pl.ANY)
VMEM = pl.BlockSpec(memory_space=pltpu.VMEM)
SMEM = pl.BlockSpec(memory_space=pltpu.SMEM)


def side_by_side(x):
    return jnp.concatenate([x[h * HEAD_DIM : (h + 1) * HEAD_DIM] for h in range(GROUP)], axis=1)


def stacked(x):
    return jnp.concatenate([x[:, h * BLOCK : (h + 1) * BLOCK] for h in range(GROUP)], axis=0)


def fused_kernel(n, m, sum_seq, x_hbm, oc_hbm, wq_hbm, wkv_hbm, wo_hbm, seg_ref, band_ref,
                 ctx_hbm, ig_ref, kvg_hbm, ctx_ref, raw, wide_raw, x_ref, oc_ref, wq_ref, wkv_ref, wo_ref, q_ref, dc_ref,
                 kvx, kdocs, bias, grad, halo, hin, dq_ref, dkv, part, inb, ls, os, ks, kr, hs, hr, rs, rr,
                 *rest):
    if sum_seq:
        (gt, gsum, sib, quart, got, mine, mix, piece, sib2,
         ss, sr, qs, qr, gs, gr, fs, fr) = rest
    tok, kvc = dkv.shape
    blocks = tok // BLOCK
    kv_heads = kvc // (2 * HEAD_DIM)
    wide = GROUP * HEAD_DIM
    loads = [
        pltpu.make_async_copy(src, dst, ls.at[i])
        for i, (src, dst) in enumerate(
            ((wkv_hbm, raw), (x_hbm, x_ref), (wq_hbm, wq_ref), (oc_hbm, oc_ref), (wo_hbm, wo_ref))
        )
    ]
    for cp in loads:
        cp.start()
    ch = part.shape[2]
    me = lax.axis_index("seq")
    z = lax.axis_index("mp")
    core = me % 2
    sibling = me + 1 - 2 * core
    chip = me // 2
    chips = n // 2

    def seq_dev(i):
        return (i, z)

    def mp_dev(i):
        return (me, i)

    barrier = pltpu.get_barrier_semaphore()
    has_left, has_right = me > 0, me < n - 1
    has_down, has_up = z > 0, z < m - 1

    def greet(dev):
        pl.semaphore_signal(barrier, inc=1, device_id=dev, device_id_type=MESH)

    for there, dev in (
        (has_left, seq_dev(me - 1)),
        (has_right, seq_dev(me + 1)),
        (has_down, mp_dev(z - 1)),
        (has_up, mp_dev(z + 1)),
    ):
        @pl.when(there)
        def _():
            greet(dev)
    if sum_seq:
        for k in range(1, chips):
            greet(seq_dev(((chip + k) % chips) * 2 + core))
    peers = chips - 1 if sum_seq else 0
    for there in (has_left, has_right, has_down, has_up):
        peers = peers + there.astype(jnp.int32)
    pl.semaphore_wait(barrier, peers)

    def remote(src, dst, send, recv, dev):
        return pltpu.make_async_remote_copy(
            src_ref=src, dst_ref=dst, send_sem=send, recv_sem=recv, device_id=dev,
            device_id_type=MESH)

    loads[0].wait()
    span = wide_raw.shape[0] // kv_heads

    @pl.loop(0, wkv_ref.shape[0] // span)
    def _(i):
        wide_raw[...] = raw[pl.ds(pl.multiple_of(i * span * kv_heads, 256), span * kv_heads), :].astype(f32)
        for g in range(kv_heads):
            wkv_ref[pl.ds(pl.multiple_of(i * span, 256), span), g * 128 : (g + 1) * 128] = (
                wide_raw[pl.ds(g, span, stride=kv_heads), :].astype(bf16)
            )

    loads[1].wait()

    @pl.loop(0, tok // 256)
    def _(i):
        r = pl.ds(pl.multiple_of(i * 256, 256), 256)
        ro = pl.ds(pl.multiple_of(i * 256 + MARGIN, 256), 256)
        kvx[ro, :] = jnp.dot(x_ref[r, :], wkv_ref[...], preferred_element_type=f32).astype(bf16)

    before, after = pl.ds(0, MARGIN), pl.ds(MARGIN + tok, MARGIN)
    kv_left = remote(kvx.at[pl.ds(MARGIN, MARGIN)], kvx.at[after], ks.at[0], kr.at[0], seq_dev(me - 1))
    kv_right = remote(kvx.at[pl.ds(tok, MARGIN)], kvx.at[before], ks.at[1], kr.at[1], seq_dev(me + 1))
    pl.when(has_left)(kv_left.start)
    pl.when(has_right)(kv_right.start)

    for kb in range(blocks + 4):
        row = me * blocks + kb - 2
        inside = (row >= 0) & (row < n * blocks)
        docs = seg_ref[pl.ds(jnp.clip(row, 0, n * blocks - 1), 1), :]
        docs = jnp.where(inside, docs, -1)
        kdocs[kb] = jnp.transpose(jnp.broadcast_to(docs, (BLOCK, BLOCK)))

    @pl.loop(0, blocks)
    def _(b):
        qdoc = seg_ref[pl.ds(me * blocks + b, 1), :]
        for o in range(5):
            same = kdocs[b + o] == qdoc
            if o != 2:
                same = same & (band_ref[b, o if o < 2 else o - 1] == 1)
            bias[b, o * BLOCK : (o + 1) * BLOCK, :] = jnp.where(same, 0.0, -1e30).astype(f32)

    grad[...] = jnp.zeros_like(grad)
    loads[2].wait()

    @pl.loop(0, tok // 256)
    def _(i):
        r = pl.ds(pl.multiple_of(i * 256, 256), 256)
        q_ref[r, :] = jnp.dot(x_ref[r, :], wq_ref[...], preferred_element_type=f32).astype(bf16)

    loads[3].wait()
    loads[4].wait()

    @pl.loop(0, tok // 256)
    def _(i):
        r = pl.ds(pl.multiple_of(i * 256, 256), 256)
        dc_ref[r, :] = lax.dot_general(
            oc_ref[r, :], wo_ref[...], NT, preferred_element_type=f32
        ).astype(bf16)

    @pl.when(jnp.logical_not(has_left))
    def _():
        kvx[before, :] = jnp.zeros((MARGIN, kvc), bf16)
        for g in range(kv_heads):
            hin[1, g] = jnp.zeros(hin.shape[2:], bf16)

    @pl.when(jnp.logical_not(has_right))
    def _():
        kvx[after, :] = jnp.zeros((MARGIN, kvc), bf16)
        for g in range(kv_heads):
            hin[0, g] = jnp.zeros(hin.shape[2:], bf16)

    pl.when(has_left)(kv_right.wait_recv)
    pl.when(has_right)(kv_left.wait_recv)

    halos = []
    for g in range(kv_heads):
        cols = slice(g * wide, (g + 1) * wide)
        kcols = slice(g * 2 * HEAD_DIM, (g + 1) * 2 * HEAD_DIM)

        @pl.loop(0, blocks)
        def _(b):
            first = pl.multiple_of(b * BLOCK, BLOCK)
            qt = side_by_side(jnp.transpose(q_ref[pl.ds(first, BLOCK), cols] * SCALE))
            dct = side_by_side(jnp.transpose(dc_ref[pl.ds(first, BLOCK), cols]))
            zero = jnp.zeros_like(qt)
            qz = jnp.concatenate([qt, zero], axis=0)
            dcz = jnp.concatenate([zero, dct], axis=0)
            kv = kvx[pl.ds(first, WINDOW), kcols]
            kvt = jnp.transpose(kv)
            s = jnp.dot(kv, qz, preferred_element_type=f32)
            s = s + jnp.concatenate([bias[b]] * GROUP, axis=1)
            p = jnp.exp(s - jnp.max(s, axis=0, keepdims=True))
            w = p * (1.0 / jnp.sum(p, axis=0, keepdims=True))
            wh = w.astype(bf16)
            ctx = jnp.dot(kvt[HEAD_DIM:], wh, preferred_element_type=f32).astype(bf16)
            delta = jnp.sum(dct.astype(f32) * ctx.astype(f32), axis=0, keepdims=True)
            dp = jnp.dot(kv, dcz, preferred_element_type=f32)
            ds = (w * (dp - delta)).astype(bf16)
            dq = jnp.dot(kvt[:HEAD_DIM], ds, preferred_element_type=f32) * SCALE
            ctx_ref[pl.ds(first, BLOCK), cols] = jnp.transpose(stacked(ctx))
            dq_ref[pl.ds(first, BLOCK), cols] = jnp.transpose(stacked(dq.astype(bf16)))
            d_kv = lax.dot_general(ds, qz, NT, preferred_element_type=f32)
            d_kv = d_kv + lax.dot_general(wh, dcz, NT, preferred_element_type=f32)
            grad[pl.ds(first, WINDOW), kcols] += d_kv

        halo[0, g] = grad[:MARGIN, kcols].astype(bf16)
        halo[1, g] = grad[MARGIN + tok :, kcols].astype(bf16)
        to_left = remote(halo.at[0, g], hin.at[0, g], hs.at[0, g], hr.at[0, g], seq_dev(me - 1))
        to_right = remote(halo.at[1, g], hin.at[1, g], hs.at[1, g], hr.at[1, g], seq_dev(me + 1))
        pl.when(has_left)(to_left.start)
        pl.when(has_right)(to_right.start)
        halos.append((to_left, to_right))

    leave = [pltpu.make_async_copy(ctx_ref, ctx_hbm, os.at[0])]
    leave[0].start()
    zero = jnp.zeros((tok - MARGIN, 2 * HEAD_DIM), f32)
    for g, (to_left, to_right) in enumerate(halos):
        kcols = slice(g * 2 * HEAD_DIM, (g + 1) * 2 * HEAD_DIM)
        pl.when(has_left)(to_right.wait_recv)
        pl.when(has_right)(to_left.wait_recv)
        dkv[:, kcols] = (
            grad[MARGIN : MARGIN + tok, kcols]
            + jnp.concatenate([hin[1, g].astype(f32), zero], axis=0)
            + jnp.concatenate([zero, hin[0, g].astype(f32)], axis=0)
        ).astype(bf16)

    def to_up(c):
        return remote(part.at[c], inb.at[c], rs.at[c], rr.at[c], mp_dev(z + 1))

    def to_down(c):
        slot = jnp.where(c == z - 1, m, c)
        return remote(part.at[c], inb.at[slot], rs.at[c], rr.at[slot], mp_dev(z - 1))

    low = z < m // 2

    @pl.loop(0, m)
    def _(t):
        c = jnp.where(low, m - 1 - t, t)
        rows = pl.ds(pl.multiple_of(c * ch, ch), ch)

        @pl.loop(0, tok // 256)
        def _(i):
            r = pl.ds(pl.multiple_of(i * 256, 256), 256)
            part[c, r, :] = (
                lax.dot_general(dq_ref[r, :], wq_ref[rows, :], NT, preferred_element_type=f32)
                + lax.dot_general(dkv[r, :], wkv_ref[rows, :], NT, preferred_element_type=f32)
            ).astype(bf16)

        @pl.when((z == 0) & (c > z))
        def _():
            to_up(c).start()

        @pl.when((z == m - 1) & (c < z))
        def _():
            to_down(c).start()

    def arrived(slot):
        remote(part.at[0], inb.at[slot], rs.at[0], rr.at[slot], mp_dev(z)).wait_recv()

    def add_in(c, slot):
        arrived(slot)

        @pl.loop(0, tok // 128)
        def _(i):
            r = pl.ds(pl.multiple_of(i * 128, 128), 128)
            part[c, r, :] = (part[c, r, :].astype(f32) + inb[slot, r, :].astype(f32)).astype(bf16)

    inner = (z > 0) & (z < m - 1)

    def up_step(c):
        @pl.when(inner & (c > z))
        def _():
            add_in(c, c)
            to_up(c).start()

    def down_step(c):
        @pl.when(inner & (c < z))
        def _():
            add_in(c, c)
            to_down(c).start()

    def chain_steps(first, last):
        @pl.when(low)
        def _():
            @pl.loop(first, last)
            def _(t):
                up_step(m - 1 - t)
                down_step(t)

        @pl.when(jnp.logical_not(low))
        def _():
            @pl.loop(first, last)
            def _(t):
                down_step(t)
                up_step(m - 1 - t)

    if sum_seq:
        pw = gt.shape[3]
        pr = pw * kv_heads
        dkvt = jnp.transpose(dkv[...])
        for k in range(2):
            half = (1 - core) if k == 0 else core

            @pl.loop(0, chips)
            def _(j):
                cols = pl.ds(pl.multiple_of((2 * j + half) * pw, pw), pw)
                prod = jnp.dot(dkvt, x_ref[:, cols], preferred_element_type=f32)
                if k == 0:
                    gt[0, j] = prod.astype(bf16)
                else:
                    gsum[j] = prod

            if k == 0:
                swap = remote(gt.at[0], sib, ss, sr, seq_dev(sibling))
                swap.start()
        swap.wait_recv()

        def other(k):
            return (chip + k) % chips

        sends = []
        for k in range(1, chips):
            j = other(k)
            gt[1, j] = (gsum[j] + sib[j].astype(f32)).astype(bf16)
            cp = remote(gt.at[1, j], quart.at[k], qs.at[k], qr.at[k], seq_dev(j * 2 + core))
            cp.start()
            sends.append(cp)
        mine[...] = gsum[chip] + sib[chip].astype(f32)
        swap.wait_send()

        @pl.when(low)
        def _():
            up_step(m - 1)

        @pl.when(jnp.logical_not(low))
        def _():
            down_step(0)

        for cp in sends:
            cp.wait_recv()
        for k in range(1, chips):
            mine[...] += quart[k].astype(f32)
        for cp in sends:
            cp.wait_send()
        done = jnp.transpose(mine[...])
        for g in range(kv_heads):
            kcols = slice(g * 2 * HEAD_DIM, (g + 1) * 2 * HEAD_DIM)
            mix[pl.ds(g, pw, stride=kv_heads), :] = done[:, kcols]
        piece[...] = mix[...].astype(bf16)
        sends = []
        for k in range(1, chips):
            cp = remote(piece, got.at[k], gs.at[k], gr.at[k], seq_dev(other(k) * 2 + core))
            cp.start()
            sends.append(cp)

        @pl.when(low)
        def _():
            down_step(0)

        @pl.when(jnp.logical_not(low))
        def _():
            up_step(m - 1)

        chain_steps(1, m)
        got[0] = piece[...]
        for cp in sends:
            cp.wait()
        swap = remote(got, sib2, fs, fr, seq_dev(sibling))
        swap.start()
        for k in range(chips):
            src = (chip + chips - k) % chips
            rows = pl.ds(pl.multiple_of((2 * src + core) * pr, pr), pr)
            leave.append(pltpu.make_async_copy(got.at[k], kvg_hbm.at[rows], os.at[1 + k]))
            leave[-1].start()
        swap.wait_recv()
        for k in range(chips):
            src = (chip + chips - k) % chips
            rows = pl.ds(pl.multiple_of((2 * src + 1 - core) * pr, pr), pr)
            leave.append(pltpu.make_async_copy(sib2.at[k], kvg_hbm.at[rows], os.at[1 + chips + k]))
            leave[-1].start()
        swap.wait_send()
    else:
        leave.append(pltpu.make_async_copy(dkv, kvg_hbm, os.at[1]))
        leave[1].start()
        chain_steps(0, m)

    @pl.when(has_down)
    def _():
        arrived(z)

    @pl.when(jnp.logical_not(has_down))
    def _():
        inb[0] = jnp.zeros(inb.shape[1:], bf16)

    @pl.when(has_up)
    def _():
        arrived(m)

    @pl.when(jnp.logical_not(has_up))
    def _():
        inb[m] = jnp.zeros(inb.shape[1:], bf16)

    @pl.loop(0, tok // 128)
    def _(i):
        r = pl.ds(pl.multiple_of(i * 128, 128), 128)
        ig_ref[r, :] = (
            part[z, r, :].astype(f32) + inb[z, r, :].astype(f32) + inb[m, r, :].astype(f32)
        ).astype(bf16)

    @pl.loop(0, m)
    def _(c):
        @pl.when(c > z)
        def _():
            to_up(c).wait_send()

        @pl.when(c < z)
        def _():
            to_down(c).wait_send()

    for cp in leave:
        cp.wait()
    pl.when(has_left)(kv_left.wait_send)
    pl.when(has_right)(kv_right.wait_send)
    for to_left, to_right in halos:
        pl.when(has_left)(to_left.wait_send)
        pl.when(has_right)(to_right.wait_send)


def relay_kernel(n, ag, x_hbm, oc_hbm, wq_hbm, wkv_hbm, wo_hbm, seg_ref, band_ref,
                 ctx_hbm, ig_ref, kvg_hbm, ctx_ref, raw, wide_raw, x_ref, oc_ref, wall, wo_ref, q_ref, dc_ref,
                 kvx, kdocs, bias, grad, halo, hin, dall, wx, dout, dx, snd, rcv, tout, rin,
                 gt, gsum, sib, quart, got, mine, mix, piece, sib2,
                 ls, os, ks, kr, hs, hr, ss, sr, qs, qr, gs, gr, fs, fr,
                 zhs, zhr, zas, zar, pls, plr, pfs, pfr, pss, psr,
                 oqs, oqr, oks, okr, xqs, xqr, xks, xkr, rss, rsr, tos, tor):
    tok, qc = q_ref.shape
    kvc = kvx.shape[1]
    ch = wall.shape[0] // 4
    blocks = tok // BLOCK
    kv_heads = kvc // (2 * HEAD_DIM)
    wide = GROUP * HEAD_DIM
    pair = 2 * HEAD_DIM
    held = ag * BLOCK
    me = lax.axis_index("seq")
    z = lax.axis_index("mp")
    core = me % 2
    sibling = me + 1 - 2 * core
    chip = me // 2
    chips = n // 2
    pr = ch // n
    outer = (z == 0) | (z == 3)
    inner = jnp.logical_not(outer)
    partner = jnp.where(outer, jnp.where(z == 0, 1, 2), jnp.where(z == 1, 0, 3))
    facing = 3 - z
    facing_partner = 3 - partner

    loads = [
        pltpu.make_async_copy(src, dst, ls.at[i])
        for i, (src, dst) in enumerate((
            (wkv_hbm, raw),
            (x_hbm, x_ref),
            (wq_hbm, wall.at[:, pl.ds(0, qc)]),
            (oc_hbm, oc_ref),
            (wo_hbm, wo_ref),
        ))
    ]
    for cp in loads:
        cp.start()

    def seq_dev(i):
        return (i, z)

    def mp_dev(i):
        return (me, i)

    barrier = pltpu.get_barrier_semaphore()
    has_left, has_right = me > 0, me < n - 1
    has_down, has_up = z > 0, z < 3

    def greet(dev):
        pl.semaphore_signal(barrier, inc=1, device_id=dev, device_id_type=MESH)

    for there, dev in (
        (has_left, seq_dev(me - 1)),
        (has_right, seq_dev(me + 1)),
        (has_down, mp_dev(z - 1)),
        (has_up, mp_dev(z + 1)),
    ):
        @pl.when(there)
        def _():
            greet(dev)
    for k in range(1, chips):
        greet(seq_dev(((chip + k) % chips) * 2 + core))
    peers = chips - 1
    for there in (has_left, has_right, has_down, has_up):
        peers = peers + there.astype(jnp.int32)
    pl.semaphore_wait(barrier, peers)

    def remote(src, dst, send, recv, dev):
        return pltpu.make_async_remote_copy(
            src_ref=src, dst_ref=dst, send_sem=send, recv_sem=recv, device_id=dev,
            device_id_type=MESH)

    qcols, kvcols = pl.ds(0, qc), pl.ds(qc, kvc)

    def rows_of(c):
        return pl.ds(pl.multiple_of(c * ch + me * pr, pr), pr)

    sent_chunks = (partner, facing_partner, facing)
    zh = [[], []]
    for j, c in enumerate(sent_chunks):
        zh[0].append(remote(wq_hbm.at[rows_of(c), :], wx.at[j, chip, core, :, qcols], zhs.at[0, j], zhr.at[0, j], mp_dev(partner)))
        zh[1].append(remote(wall.at[rows_of(c), kvcols], wx.at[j, chip, core, :, kvcols], zhs.at[1, j], zhr.at[1, j], mp_dev(partner)))
    za = [[], [], []]
    if ag:
        for j, c in enumerate((facing, facing_partner)):
            za[0].append(remote(wq_hbm.at[rows_of(c), :], wx.at[3 + j, chip, core, :, qcols], zas.at[0, j], zar.at[0, j], mp_dev(facing)))
            za[1].append(remote(wall.at[rows_of(c), kvcols], wx.at[3 + j, chip, core, :, kvcols], zas.at[1, j], zar.at[1, j], mp_dev(facing)))
            za[2].append(remote(wx.at[1 + j, chip, core], wx.at[5 + j, chip, core], zas.at[2, j], zar.at[2, j], mp_dev(facing)))

    def each(cps, what):
        for cp in cps:
            getattr(cp, what)()

    @pl.when(outer)
    def _():
        each(zh[0], "start")

    @pl.when(inner)
    def _():
        each(za[0], "start")

    xchip, ychip = chip + 1 - 2 * (chip % 2), (chip + 2) % chips
    dchip = (xchip + 2) % chips
    sets = ((0, 3), (3, 2), (5, 2)) if ag else ((0, 3),)
    half = pr // 2
    to_x, to_y, via_x, via_y, to_sib = [], [], [], [], []
    for i, (first, count) in enumerate(sets):
        ksl = pl.ds(first, count)
        own = wx.at[ksl, chip, core]
        to_x.append(remote(own, own, pls.at[0, i], plr.at[0, i], seq_dev(xchip * 2 + core)))
        to_y.append(remote(own, own, pls.at[1, i], plr.at[1, i], seq_dev(ychip * 2 + core)))
        lo = wx.at[ksl, xchip, core, pl.ds(0, half)]
        hi = wx.at[ksl, ychip, core, pl.ds(half, half)]
        via_y.append(remote(lo, lo, pfs.at[0, i], pfr.at[0, i], seq_dev(ychip * 2 + core)))
        via_x.append(remote(hi, hi, pfs.at[1, i], pfr.at[1, i], seq_dev(xchip * 2 + core)))
        row = []
        for j, c in enumerate((chip, xchip, ychip, dchip)):
            part = wx.at[ksl, c, core]
            row.append(remote(part, part, pss.at[i, j], psr.at[i, j], seq_dev(sibling)))
        to_sib.append(row)

    def plane_start(i):
        to_x[i].start()
        to_y[i].start()
        to_sib[i][0].start()

    def plane_wait_x(i):
        first, count = sets[i]
        dst = wx.at[pl.ds(first, count), xchip, core]
        remote(dst, dst, pls.at[0, i], plr.at[0, i], seq_dev(sibling)).wait_recv()

    def plane_wait_y(i):
        first, count = sets[i]
        dst = wx.at[pl.ds(first, count), ychip, core]
        remote(dst, dst, pls.at[1, i], plr.at[1, i], seq_dev(sibling)).wait_recv()

    def plane_relay(i):
        plane_wait_x(i)
        via_y[i].start()
        to_sib[i][1].start()
        plane_wait_y(i)
        via_x[i].start()
        to_sib[i][2].start()

    def plane_pair(i):
        first, count = sets[i]
        for f, s in enumerate((pl.ds(0, half), pl.ds(half, half))):
            dst = wx.at[pl.ds(first, count), dchip, core, s]
            remote(dst, dst, pfs.at[f, i], pfr.at[f, i], seq_dev(sibling)).wait_recv()
        to_sib[i][3].start()

    def plane_done(i):
        first, count = sets[i]
        for j, c in enumerate((chip, xchip, ychip, dchip)):
            dst = wx.at[pl.ds(first, count), c, 1 - core]
            remote(dst, dst, pss.at[i, j], psr.at[i, j], seq_dev(sibling)).wait_recv()

    loads[0].wait()
    span = wide_raw.shape[0] // kv_heads

    @pl.loop(0, wall.shape[0] // span)
    def _(i):
        wide_raw[...] = raw[pl.ds(pl.multiple_of(i * span * kv_heads, 256), span * kv_heads), :].astype(f32)
        for g in range(kv_heads):
            wall[pl.ds(pl.multiple_of(i * span, 256), span), qc + g * 128 : qc + (g + 1) * 128] = (
                wide_raw[pl.ds(g, span, stride=kv_heads), :].astype(bf16)
            )

    loads[1].wait()

    @pl.loop(0, tok // 256)
    def _(i):
        r = pl.ds(pl.multiple_of(i * 256, 256), 256)
        ro = pl.ds(pl.multiple_of(i * 256 + MARGIN, 256), 256)
        kvx[ro, :] = jnp.dot(x_ref[r, :], wall[:, qc:], preferred_element_type=f32).astype(bf16)

    before, after = pl.ds(0, MARGIN), pl.ds(MARGIN + tok, MARGIN)
    kv_left = remote(kvx.at[pl.ds(MARGIN, MARGIN)], kvx.at[after], ks.at[0], kr.at[0], seq_dev(me - 1))
    kv_right = remote(kvx.at[pl.ds(tok, MARGIN)], kvx.at[before], ks.at[1], kr.at[1], seq_dev(me + 1))
    pl.when(has_left)(kv_left.start)
    pl.when(has_right)(kv_right.start)

    @pl.when(outer)
    def _():
        each(zh[1], "start")

    @pl.when(inner)
    def _():
        each(za[1], "start")

    for kb in range(blocks + 4):
        row = me * blocks + kb - 2
        inside = (row >= 0) & (row < n * blocks)
        docs = seg_ref[pl.ds(jnp.clip(row, 0, n * blocks - 1), 1), :]
        docs = jnp.where(inside, docs, -1)
        kdocs[kb] = jnp.transpose(jnp.broadcast_to(docs, (BLOCK, BLOCK)))

    @pl.loop(0, blocks)
    def _(b):
        qdoc = seg_ref[pl.ds(me * blocks + b, 1), :]
        for o in range(5):
            same = kdocs[b + o] == qdoc
            if o != 2:
                same = same & (band_ref[b, o if o < 2 else o - 1] == 1)
            bias[b, o * BLOCK : (o + 1) * BLOCK, :] = jnp.where(same, 0.0, -1e30).astype(f32)

    grad[...] = jnp.zeros_like(grad)
    loads[2].wait()

    @pl.loop(0, tok // 256)
    def _(i):
        r = pl.ds(pl.multiple_of(i * 256, 256), 256)
        q_ref[r, :] = jnp.dot(x_ref[r, :], wall[:, :qc], preferred_element_type=f32).astype(bf16)

    loads[3].wait()
    loads[4].wait()

    @pl.loop(0, tok // 256)
    def _(i):
        r = pl.ds(pl.multiple_of(i * 256, 256), 256)
        dc_ref[r, :] = lax.dot_general(
            oc_ref[r, :], wo_ref[...], NT, preferred_element_type=f32
        ).astype(bf16)

    @pl.when(jnp.logical_not(has_left))
    def _():
        kvx[before, :] = jnp.zeros((MARGIN, kvc), bf16)
        for g in range(kv_heads):
            hin[1, g] = jnp.zeros(hin.shape[2:], bf16)

    @pl.when(jnp.logical_not(has_right))
    def _():
        kvx[after, :] = jnp.zeros((MARGIN, kvc), bf16)
        for g in range(kv_heads):
            hin[0, g] = jnp.zeros(hin.shape[2:], bf16)

    @pl.when(inner)
    def _():
        each(zh[0], "wait_recv")
        each(zh[1], "wait_recv")
        plane_start(0)
        each(za[2], "start")
        each(za[0], "wait_recv")
        each(za[1], "wait_recv")
        plane_start(1)

    pl.when(has_left)(kv_right.wait_recv)
    pl.when(has_right)(kv_left.wait_recv)

    def block_rows(b):
        return pl.ds(pl.multiple_of(b * BLOCK, BLOCK), BLOCK)

    def dq_out(g, b):
        at = (block_rows(b), pl.ds(g * wide, wide))
        return remote(dall.at[at], dout.at[at], oqs.at[g, b], oqr.at[g, b], mp_dev(partner))

    def dq_across(which, g, b):
        at = (block_rows(b), pl.ds(g * wide, wide))
        src = dall.at[at] if which == 0 else dout.at[at]
        return remote(src, dx.at[(which,) + at], xqs.at[which, g, b], xqr.at[which, g, b], mp_dev(facing))

    def dkv_cols(g):
        return pl.ds(qc + g * pair, pair)

    def dkv_out(g, early):
        rows = pl.ds(0, held) if early else pl.ds(held, tok - held)
        at = (rows, dkv_cols(g))
        i = 1 if early else 0
        return remote(dall.at[at], dout.at[at], oks.at[g, i], okr.at[g, i], mp_dev(partner))

    def dkv_across(which, g):
        at = (pl.ds(0, held), dkv_cols(g))
        src = dall.at[at] if which == 0 else dout.at[at]
        return remote(src, dx.at[(which,) + at], xks.at[which, g], xkr.at[which, g], mp_dev(facing))

    def halo_left(g):
        return remote(halo.at[0, g], hin.at[0, g], hs.at[0, g], hr.at[0, g], seq_dev(me - 1))

    def halo_right(g):
        return remote(halo.at[1, g], hin.at[1, g], hs.at[1, g], hr.at[1, g], seq_dev(me + 1))

    def finish_late(g):
        pl.when(has_right)(halo_left(g).wait_recv)
        dall[held:, qc + g * pair : qc + (g + 1) * pair] = (
            grad[MARGIN + held : MARGIN + tok, g * pair : (g + 1) * pair] + hin[0, g].astype(f32)
        ).astype(bf16)
        pl.when(outer)(dkv_out(g, False).start)

    def finish_early(g):
        pl.when(has_left)(halo_right(g).wait_recv)
        dall[:held, qc + g * pair : qc + (g + 1) * pair] = (
            grad[MARGIN : MARGIN + held, g * pair : (g + 1) * pair] + hin[1, g].astype(f32)
        ).astype(bf16)
        pl.when(outer)(dkv_out(g, True).start)
        pl.when(inner)(dkv_across(0, g).start)

    for g in range(kv_heads):
        cols = slice(g * wide, (g + 1) * wide)
        kcols = slice(g * pair, (g + 1) * pair)

        @pl.loop(0, blocks)
        def _(b):
            first = pl.multiple_of(b * BLOCK, BLOCK)
            qt = side_by_side(jnp.transpose(q_ref[pl.ds(first, BLOCK), cols] * SCALE))
            dct = side_by_side(jnp.transpose(dc_ref[pl.ds(first, BLOCK), cols]))
            zero = jnp.zeros_like(qt)
            qz = jnp.concatenate([qt, zero], axis=0)
            dcz = jnp.concatenate([zero, dct], axis=0)
            kv = kvx[pl.ds(first, WINDOW), kcols]
            kvt = jnp.transpose(kv)
            s = jnp.dot(kv, qz, preferred_element_type=f32)
            s = s + jnp.concatenate([bias[b]] * GROUP, axis=1)
            p = jnp.exp(s - jnp.max(s, axis=0, keepdims=True))
            w = p * (1.0 / jnp.sum(p, axis=0, keepdims=True))
            wh = w.astype(bf16)
            ctx = jnp.dot(kvt[HEAD_DIM:], wh, preferred_element_type=f32).astype(bf16)
            delta = jnp.sum(dct.astype(f32) * ctx.astype(f32), axis=0, keepdims=True)
            dp = jnp.dot(kv, dcz, preferred_element_type=f32)
            ds = (w * (dp - delta)).astype(bf16)
            dq = jnp.dot(kvt[:HEAD_DIM], ds, preferred_element_type=f32) * SCALE
            ctx_ref[pl.ds(first, BLOCK), cols] = jnp.transpose(stacked(ctx))
            dall[pl.ds(first, BLOCK), cols] = jnp.transpose(stacked(dq.astype(bf16)))
            d_kv = lax.dot_general(ds, qz, NT, preferred_element_type=f32)
            d_kv = d_kv + lax.dot_general(wh, dcz, NT, preferred_element_type=f32)
            grad[pl.ds(first, WINDOW), kcols] += d_kv

            @pl.when(outer)
            def _():
                dq_out(g, b).start()

            @pl.when(inner & (b < ag))
            def _():
                dq_across(0, g, b).start()

            @pl.when(inner & (b >= 2) & (b < ag + 2))
            def _():
                dq_out(g, b - 2).wait_recv()
                dq_across(1, g, b - 2).start()

            @pl.when(b == 1)
            def _():
                halo[0, g] = grad[:MARGIN, kcols].astype(bf16)
                pl.when(has_left)(halo_left(g).start)

            if g == 1:
                @pl.when(inner & (b == 0))
                def _():
                    plane_relay(0)
                    each(za[2], "wait_recv")
                    plane_start(2)

                @pl.when(b == 1)
                def _():
                    finish_early(0)
                    finish_late(0)

                @pl.when(inner & (b == blocks - 1))
                def _():
                    plane_relay(1)

        halo[1, g] = grad[MARGIN + tok :, kcols].astype(bf16)
        pl.when(has_right)(halo_right(g).start)

    leave = [pltpu.make_async_copy(ctx_ref, ctx_hbm, os.at[0])]
    leave[0].start()
    finish_late(1)

    @pl.when(inner)
    def _():
        dkv_out(0, True).wait_recv()
        dkv_across(1, 0).start()

    finish_early(1)
    pl.when(inner)(functools.partial(plane_pair, 0))

    pw = gt.shape[3]
    gr_rows = pw * kv_heads
    dkvt = jnp.transpose(dall[:, qc:])
    for k in range(2):
        part = (1 - core) if k == 0 else core

        @pl.loop(0, chips)
        def _(j):
            cols = pl.ds(pl.multiple_of((2 * j + part) * pw, pw), pw)
            prod = jnp.dot(dkvt, x_ref[:, cols], preferred_element_type=f32)
            if k == 0:
                gt[0, j] = prod.astype(bf16)
            else:
                gsum[j] = prod

        if k == 0:
            swap = remote(gt.at[0], sib, ss, sr, seq_dev(sibling))
            swap.start()

    def chunk(c):
        return pl.ds(pl.multiple_of(c * ch, ch), ch)

    def times_own(r, c):
        return lax.dot_general(dall[r, :], wall[chunk(c), :], NT, preferred_element_type=f32)

    def times_sent(d, k):
        return lax.dot_general(d, wx[k].reshape(ch, qc + kvc), NT, preferred_element_type=f32)

    tile = 256 if ag % 2 == 0 else 128
    summed = tok - held

    def sum_piece(slot, i):
        at = (slot, pl.ds(i * BLOCK, BLOCK))
        return remote(snd.at[at], rcv.at[at], rss.at[slot, i], rsr.at[slot, i], mp_dev(facing))

    def out_piece(i):
        at = block_rows(i)
        return remote(tout.at[at], rin.at[at], tos.at[i], tor.at[i], mp_dev(partner))

    steps = tile // BLOCK

    @pl.when(inner)
    def _():
        for g in range(kv_heads):
            for b in range(ag, blocks):
                dq_out(g, b).wait_recv()
            dkv_out(g, False).wait_recv()
        plane_done(0)
        for slot in (1, 0):
            c = facing_partner if slot == 1 else facing
            for t in range(summed // tile):
                r = slice(held + t * tile, held + (t + 1) * tile)
                snd[slot, t * tile : (t + 1) * tile, :] = (
                    times_own(r, c) + times_sent(dout[r, :], slot + 1)
                ).astype(bf16)
                for i in range(t * steps, (t + 1) * steps):
                    sum_piece(slot, i).start()
            if slot == 1:
                dkv_out(1, True).wait_recv()
                dkv_across(1, 1).start()
                plane_relay(2)
                plane_pair(1)

    swap.wait_recv()

    def other(k):
        return (chip + k) % chips

    sends = []
    for k in range(1, chips):
        j = other(k)
        gt[1, j] = (gsum[j] + sib[j].astype(f32)).astype(bf16)
        cp = remote(gt.at[1, j], quart.at[k], qs.at[k], qr.at[k], seq_dev(j * 2 + core))
        cp.start()
        sends.append(cp)
    mine[...] = gsum[chip] + sib[chip].astype(f32)
    swap.wait_send()

    @pl.when(inner)
    def _():
        for i in range(summed // BLOCK):
            r = slice(held + i * BLOCK, held + (i + 1) * BLOCK)
            own = times_own(r, partner)
            sum_piece(1, i).wait_recv()
            tout[r, :] = (own + rcv[1, i * BLOCK : (i + 1) * BLOCK, :].astype(f32)).astype(bf16)
            out_piece(ag + i).start()

    for cp in sends:
        cp.wait_recv()
    for k in range(1, chips):
        mine[...] += quart[k].astype(f32)
    for cp in sends:
        cp.wait_send()
    done = jnp.transpose(mine[...])
    for g in range(kv_heads):
        kcols = slice(g * pair, (g + 1) * pair)
        mix[pl.ds(g, pw, stride=kv_heads), :] = done[:, kcols]
    piece[...] = mix[...].astype(bf16)
    sends = []
    for k in range(1, chips):
        cp = remote(piece, got.at[k], gs.at[k], gr.at[k], seq_dev(other(k) * 2 + core))
        cp.start()
        sends.append(cp)

    if ag:
        @pl.when(inner)
        def _():
            for which in range(2):
                for g in range(kv_heads):
                    for b in range(ag):
                        dq_across(which, g, b).wait_recv()
                    dkv_across(which, g).wait_recv()
            plane_pair(2)
            plane_done(1)
            plane_done(2)
            for t in range(held // tile):
                r = slice(t * tile, (t + 1) * tile)
                tout[r, :] = (
                    times_own(r, partner) + times_sent(dx[0, r, :], 4) + times_sent(dx[1, r, :], 6)
                ).astype(bf16)
                for i in range(t * steps, (t + 1) * steps):
                    out_piece(i).start()
            for t in range(held // tile):
                r = slice(t * tile, (t + 1) * tile)
                ig_ref[r, :] = (
                    times_own(r, z) + times_sent(dout[r, :], 0)
                    + times_sent(dx[0, r, :], 3) + times_sent(dx[1, r, :], 5)
                ).astype(bf16)

    got[0] = piece[...]
    for cp in sends:
        cp.wait()
    swap = remote(got, sib2, fs, fr, seq_dev(sibling))
    swap.start()
    for k in range(chips):
        src = (chip + chips - k) % chips
        rows = pl.ds(pl.multiple_of((2 * src + core) * gr_rows, gr_rows), gr_rows)
        leave.append(pltpu.make_async_copy(got.at[k], kvg_hbm.at[rows], os.at[1 + k]))
        leave[-1].start()
    swap.wait_recv()
    for k in range(chips):
        src = (chip + chips - k) % chips
        rows = pl.ds(pl.multiple_of((2 * src + 1 - core) * gr_rows, gr_rows), gr_rows)
        leave.append(pltpu.make_async_copy(sib2.at[k], kvg_hbm.at[rows], os.at[1 + chips + k]))
        leave[-1].start()
    swap.wait_send()

    @pl.when(inner)
    def _():
        for t in range(summed // tile):
            for i in range(t * steps, (t + 1) * steps):
                sum_piece(0, i).wait_recv()
            r = slice(held + t * tile, held + (t + 1) * tile)
            ig_ref[r, :] = (
                times_own(r, z) + times_sent(dout[r, :], 0)
                + rcv[0, t * tile : (t + 1) * tile, :].astype(f32)
            ).astype(bf16)

    @pl.when(outer)
    def _():
        order = list(range(ag, blocks)) + list(range(ag))
        for i in order:
            r = slice(i * BLOCK, (i + 1) * BLOCK)
            own = times_own(r, z)
            out_piece(i).wait_recv()
            ig_ref[r, :] = (own + rin[r, :].astype(f32)).astype(bf16)

    @pl.when(outer)
    def _():
        for g in range(kv_heads):
            for b in range(blocks):
                dq_out(g, b).wait_send()
            dkv_out(g, False).wait_send()
            if ag:
                dkv_out(g, True).wait_send()
        each(zh[0], "wait_send")
        each(zh[1], "wait_send")

    @pl.when(inner)
    def _():
        for which in range(2 if ag else 0):
            for g in range(kv_heads):
                for b in range(ag):
                    dq_across(which, g, b).wait_send()
                dkv_across(which, g).wait_send()
        for slot in range(2):
            for i in range(blocks - ag):
                sum_piece(slot, i).wait_send()
        for i in range(blocks):
            out_piece(i).wait_send()
        for group in za:
            each(group, "wait_send")
        for group in (to_x, to_y, via_x, via_y, *to_sib):
            each(group, "wait_send")

    for cp in leave:
        cp.wait()
    pl.when(has_left)(kv_left.wait_send)
    pl.when(has_right)(kv_right.wait_send)
    for g in range(kv_heads):
        pl.when(has_left)(halo_left(g).wait_send)
        pl.when(has_right)(halo_right(g).wait_send)


def write_kernel(ctx_hbm, ig_hbm, kvg_hbm, ctx_out, ig_out, kvg_out, half, full, ctx_mid, ig_mid, ins, outs):
    pieces, rows = half.shape[0], half.shape[1]
    loads, stores = [], []
    for i in range(pieces):
        loads.append(pltpu.make_async_copy(kvg_hbm.at[pl.ds(i * rows, rows)], half.at[i], ins.at[i]))
        stores.append(pltpu.make_async_copy(full.at[i], kvg_out.at[pl.ds(i * rows, rows)], outs.at[i]))
        loads[i].start()
    for i, (src, mid, dst) in enumerate(((ctx_hbm, ctx_mid, ctx_out), (ig_hbm, ig_mid, ig_out))):
        loads.append(pltpu.make_async_copy(src, mid, ins.at[pieces + i]))
        stores.append(pltpu.make_async_copy(mid, dst, outs.at[pieces + i]))
        loads[-1].start()
    for i in range(pieces):
        loads[i].wait()
        full[i] = half[i].astype(f32)
        stores[i].start()
    for i in range(pieces, pieces + 2):
        loads[i].wait()
        stores[i].start()
    for cp in stores:
        cp.wait()


def written(*arrays):
    pieces = 4
    rows, lanes = arrays[2].shape[0] // pieces, arrays[2].shape[1]
    return pl.pallas_call(
        write_kernel,
        out_shape=[
            jax.ShapeDtypeStruct(a.shape, t) for a, t in zip(arrays, (bf16, bf16, f32))
        ],
        in_specs=[ANY] * 3,
        out_specs=[ANY] * 3,
        scratch_shapes=[
            pltpu.VMEM((pieces, rows, lanes), bf16),
            pltpu.VMEM((pieces, rows, lanes), f32),
            pltpu.VMEM(arrays[0].shape, bf16),
            pltpu.VMEM(arrays[1].shape, bf16),
            pltpu.SemaphoreType.DMA((pieces + 2,)),
            pltpu.SemaphoreType.DMA((pieces + 2,)),
        ],
        compiler_params=pltpu.CompilerParams(vmem_limit_bytes=60 * 2**20),
        name="write",
    )(*arrays)


def local(n, m, normed, out_cotangent, segments, band_mask, query_weight, key_value_weight, out_weight):
    tok, width = normed.shape
    qc = query_weight.shape[1]
    kv_heads = key_value_weight.shape[1]
    pair = 2 * HEAD_DIM
    kvc = kv_heads * pair
    wkv = key_value_weight.reshape(width * kv_heads, pair)
    blocks = tok // BLOCK
    ch = width // m
    pw = width // n
    sum_seq = n % 2 == 0 and n * 128 <= width and width % (n * 128) == 0
    chips = n // 2
    dma = pltpu.SemaphoreType.DMA
    vmem = pltpu.VMEM
    relay = n == 8 and m == 4 and kv_heads == 2 and tok == 4 * BLOCK and sum_seq
    scratch = [
        vmem((tok, qc), bf16),
        vmem((width * kv_heads, pair), bf16),
        vmem((256 * kv_heads, pair), f32),
        vmem((tok, width), bf16),
        vmem((tok, width), bf16),
        vmem((width, qc), bf16),
        vmem((width, kvc), bf16),
        vmem((qc, width), bf16),
        vmem((tok, qc), bf16),
        vmem((tok, qc), bf16),
        vmem((tok + 2 * MARGIN, kvc), bf16),
        vmem((blocks + 4, BLOCK, BLOCK), jnp.int32),
        vmem((blocks, WINDOW, BLOCK), f32),
        vmem((tok + 2 * MARGIN, kvc), f32),
        vmem((2, kv_heads, MARGIN, pair), bf16),
        vmem((2, kv_heads, MARGIN, pair), bf16),
        vmem((tok, qc), bf16),
        vmem((tok, kvc), bf16),
        vmem((m, tok, ch), bf16),
        vmem((m + 1, tok, ch), bf16),
        dma((5,)),
        dma((1 + n,)),
        dma((2,)),
        dma((2,)),
        dma((2, kv_heads)),
        dma((2, kv_heads)),
        dma((m,)),
        dma((m + 1,)),
    ]
    if sum_seq:
        kvg_shape = (width * kv_heads, pair)
        if not relay:
            scratch += [
                vmem((2, chips, kvc, pw), bf16),
                vmem((chips, kvc, pw), f32),
                vmem((chips, kvc, pw), bf16),
                vmem((chips, kvc, pw), bf16),
                vmem((chips, pw * kv_heads, pair), bf16),
                vmem((kvc, pw), f32),
                vmem((pw * kv_heads, pair), f32),
                vmem((pw * kv_heads, pair), bf16),
                vmem((chips, pw * kv_heads, pair), bf16),
                dma, dma, dma((chips,)), dma((chips,)), dma((chips,)), dma((chips,)), dma, dma,
            ]
    else:
        kvg_shape = (tok, kvc)
    ag = AHEAD
    held = ag * BLOCK
    relay_scratch = [
        vmem((tok, qc), bf16),
        vmem((width * kv_heads, pair), bf16),
        vmem((256 * kv_heads, pair), f32),
        vmem((tok, width), bf16),
        vmem((tok, width), bf16),
        vmem((width, qc + kvc), bf16),
        vmem((qc, width), bf16),
        vmem((tok, qc), bf16),
        vmem((tok, qc), bf16),
        vmem((tok + 2 * MARGIN, kvc), bf16),
        vmem((blocks + 4, BLOCK, BLOCK), jnp.int32),
        vmem((blocks, WINDOW, BLOCK), f32),
        vmem((tok + 2 * MARGIN, kvc), f32),
        vmem((2, kv_heads, MARGIN, pair), bf16),
        vmem((2, kv_heads, MARGIN, pair), bf16),
        vmem((tok, qc + kvc), bf16),
        vmem((7 if ag else 3, max(chips, 1), 2, max(ch // n, 8), qc + kvc), bf16),
        vmem((tok, qc + kvc), bf16),
        vmem((2, max(held, BLOCK), qc + kvc), bf16),
        vmem((2, max(tok - held, BLOCK), ch), bf16),
        vmem((2, max(tok - held, BLOCK), ch), bf16),
        vmem((tok, ch), bf16),
        vmem((tok, ch), bf16),
        vmem((2, chips, kvc, pw), bf16),
        vmem((chips, kvc, pw), f32),
        vmem((chips, kvc, pw), bf16),
        vmem((chips, kvc, pw), bf16),
        vmem((chips, pw * kv_heads, pair), bf16),
        vmem((kvc, pw), f32),
        vmem((pw * kv_heads, pair), f32),
        vmem((pw * kv_heads, pair), bf16),
        vmem((chips, pw * kv_heads, pair), bf16),
        dma((5,)),
        dma((1 + n,)),
        dma((2,)),
        dma((2,)),
        dma((2, kv_heads)),
        dma((2, kv_heads)),
        dma, dma, dma((chips,)), dma((chips,)), dma((chips,)), dma((chips,)), dma, dma,
        dma((2, 3)), dma((2, 3)),
        dma((3, 2)), dma((3, 2)),
        dma((2, 3)), dma((2, 3)),
        dma((2, 3)), dma((2, 3)),
        dma((3, 4)), dma((3, 4)),
        dma((kv_heads, blocks)), dma((kv_heads, blocks)),
        dma((kv_heads, 2)), dma((kv_heads, 2)),
        dma((2, kv_heads, blocks)), dma((2, kv_heads, blocks)),
        dma((2, kv_heads)), dma((2, kv_heads)),
        dma((2, blocks)), dma((2, blocks)),
        dma((blocks,)), dma((blocks,)),
    ]
    if relay:
        scratch = relay_scratch
        body = functools.partial(relay_kernel, n, ag)
    else:
        body = functools.partial(fused_kernel, n, m, sum_seq)
    context, input_grad, other = pl.pallas_call(
        body,
        out_shape=[
            jax.ShapeDtypeStruct((tok, qc), bf16),
            jax.ShapeDtypeStruct((tok, ch), bf16),
            jax.ShapeDtypeStruct(kvg_shape, bf16),
        ],
        in_specs=[ANY] * 5 + [VMEM, SMEM],
        out_specs=[ANY, VMEM, ANY],
        scratch_shapes=scratch,
        compiler_params=pltpu.CompilerParams(
            vmem_limit_bytes=56 * 2**20, collective_id=0, has_side_effects=True
        ),
        name="fused",
    )(normed, out_cotangent, query_weight, wkv, out_weight, segments.reshape(-1, BLOCK), band_mask)
    if sum_seq:
        context, input_grad, kv_grad = written(context, input_grad, other)
    else:
        kv_grad = lax.dot_general(normed, other, (((0,), (0,)), ((), ())), preferred_element_type=f32)
        kv_grad = lax.psum(kv_grad, "seq")
    return context, input_grad, kv_grad.reshape(width, kv_heads, pair)


def solution(mesh):
    placed = (
        P("seq", None),
        P("seq", None),
        P(),
        P("seq", None),
        P(None, "mp"),
        P(None, "mp", None),
        P("mp", None),
    )
    return jax.shard_map(
        functools.partial(local, mesh.shape["seq"], mesh.shape["mp"]),
        mesh=mesh,
        in_specs=placed,
        out_specs=(P("seq", "mp"), P("seq", "mp"), P(None, "mp", None)),
        check_vma=False,
    )
```

```python
import functools

import jax
import jax.numpy as jnp
from jax import lax
from jax.experimental import pallas as pl
from jax.experimental.pallas import tpu as pltpu
from jax.sharding import PartitionSpec as P

QUERY_HEADS = 32
KEY_VALUE_HEADS = 8
GROUP = QUERY_HEADS // KEY_VALUE_HEADS
HEAD_DIM = 64
BLOCK = 128
MARGIN = 2 * BLOCK
WINDOW = BLOCK + 2 * MARGIN
SCALE = 0.125
AHEAD = 2

MESH = pl.DeviceIdType.MESH
NT = (((1,), (1,)), ((), ()))
f32 = jnp.float32
bf16 = jnp.bfloat16
ANY = pl.BlockSpec(memory_space=pl.ANY)
VMEM = pl.BlockSpec(memory_space=pltpu.VMEM)
SMEM = pl.BlockSpec(memory_space=pltpu.SMEM)


def side_by_side(x):
    return jnp.concatenate([x[h * HEAD_DIM : (h + 1) * HEAD_DIM] for h in range(GROUP)], axis=1)


def stacked(x):
    return jnp.concatenate([x[:, h * BLOCK : (h + 1) * BLOCK] for h in range(GROUP)], axis=0)


def fused_kernel(n, m, sum_seq, x_hbm, oc_hbm, wq_hbm, wkv_hbm, wo_hbm, seg_ref, band_ref,
                 ctx_hbm, ig_ref, kvg_hbm, ctx_ref, raw, wide_raw, x_ref, oc_ref, wq_ref, wkv_ref, wo_ref, q_ref, dc_ref,
                 kvx, kdocs, bias, grad, halo, hin, dq_ref, dkv, part, inb, ls, os, ks, kr, hs, hr, rs, rr,
                 *rest):
    if sum_seq:
        (gt, gsum, sib, quart, got, mine, mix, piece, sib2,
         ss, sr, qs, qr, gs, gr, fs, fr) = rest
    tok, kvc = dkv.shape
    blocks = tok // BLOCK
    kv_heads = kvc // (2 * HEAD_DIM)
    wide = GROUP * HEAD_DIM
    loads = [
        pltpu.make_async_copy(src, dst, ls.at[i])
        for i, (src, dst) in enumerate(
            ((wkv_hbm, raw), (x_hbm, x_ref), (wq_hbm, wq_ref), (oc_hbm, oc_ref), (wo_hbm, wo_ref))
        )
    ]
    for cp in loads:
        cp.start()
    ch = part.shape[2]
    me = lax.axis_index("seq")
    z = lax.axis_index("mp")
    core = me % 2
    sibling = me + 1 - 2 * core
    chip = me // 2
    chips = n // 2

    def seq_dev(i):
        return (i, z)

    def mp_dev(i):
        return (me, i)

    barrier = pltpu.get_barrier_semaphore()
    has_left, has_right = me > 0, me < n - 1
    has_down, has_up = z > 0, z < m - 1

    def greet(dev):
        pl.semaphore_signal(barrier, inc=1, device_id=dev, device_id_type=MESH)

    for there, dev in (
        (has_left, seq_dev(me - 1)),
        (has_right, seq_dev(me + 1)),
        (has_down, mp_dev(z - 1)),
        (has_up, mp_dev(z + 1)),
    ):
        @pl.when(there)
        def _():
            greet(dev)
    if sum_seq:
        for k in range(1, chips):
            greet(seq_dev(((chip + k) % chips) * 2 + core))
    peers = chips - 1 if sum_seq else 0
    for there in (has_left, has_right, has_down, has_up):
        peers = peers + there.astype(jnp.int32)
    pl.semaphore_wait(barrier, peers)

    def remote(src, dst, send, recv, dev):
        return pltpu.make_async_remote_copy(
            src_ref=src, dst_ref=dst, send_sem=send, recv_sem=recv, device_id=dev,
            device_id_type=MESH)

    loads[0].wait()
    span = wide_raw.shape[0] // kv_heads

    @pl.loop(0, wkv_ref.shape[0] // span)
    def _(i):
        wide_raw[...] = raw[pl.ds(pl.multiple_of(i * span * kv_heads, 256), span * kv_heads), :].astype(f32)
        for g in range(kv_heads):
            wkv_ref[pl.ds(pl.multiple_of(i * span, 256), span), g * 128 : (g + 1) * 128] = (
                wide_raw[pl.ds(g, span, stride=kv_heads), :].astype(bf16)
            )

    loads[1].wait()

    @pl.loop(0, tok // 256)
    def _(i):
        r = pl.ds(pl.multiple_of(i * 256, 256), 256)
        ro = pl.ds(pl.multiple_of(i * 256 + MARGIN, 256), 256)
        kvx[ro, :] = jnp.dot(x_ref[r, :], wkv_ref[...], preferred_element_type=f32).astype(bf16)

    before, after = pl.ds(0, MARGIN), pl.ds(MARGIN + tok, MARGIN)
    kv_left = remote(kvx.at[pl.ds(MARGIN, MARGIN)], kvx.at[after], ks.at[0], kr.at[0], seq_dev(me - 1))
    kv_right = remote(kvx.at[pl.ds(tok, MARGIN)], kvx.at[before], ks.at[1], kr.at[1], seq_dev(me + 1))
    pl.when(has_left)(kv_left.start)
    pl.when(has_right)(kv_right.start)

    for kb in range(blocks + 4):
        row = me * blocks + kb - 2
        inside = (row >= 0) & (row < n * blocks)
        docs = seg_ref[pl.ds(jnp.clip(row, 0, n * blocks - 1), 1), :]
        docs = jnp.where(inside, docs, -1)
        kdocs[kb] = jnp.transpose(jnp.broadcast_to(docs, (BLOCK, BLOCK)))

    @pl.loop(0, blocks)
    def _(b):
        qdoc = seg_ref[pl.ds(me * blocks + b, 1), :]
        for o in range(5):
            same = kdocs[b + o] == qdoc
            if o != 2:
                same = same & (band_ref[b, o if o < 2 else o - 1] == 1)
            bias[b, o * BLOCK : (o + 1) * BLOCK, :] = jnp.where(same, 0.0, -1e30).astype(f32)

    grad[...] = jnp.zeros_like(grad)
    loads[2].wait()

    @pl.loop(0, tok // 256)
    def _(i):
        r = pl.ds(pl.multiple_of(i * 256, 256), 256)
        q_ref[r, :] = jnp.dot(x_ref[r, :], wq_ref[...], preferred_element_type=f32).astype(bf16)

    loads[3].wait()
    loads[4].wait()

    @pl.loop(0, tok // 256)
    def _(i):
        r = pl.ds(pl.multiple_of(i * 256, 256), 256)
        dc_ref[r, :] = lax.dot_general(
            oc_ref[r, :], wo_ref[...], NT, preferred_element_type=f32
        ).astype(bf16)

    @pl.when(jnp.logical_not(has_left))
    def _():
        kvx[before, :] = jnp.zeros((MARGIN, kvc), bf16)
        for g in range(kv_heads):
            hin[1, g] = jnp.zeros(hin.shape[2:], bf16)

    @pl.when(jnp.logical_not(has_right))
    def _():
        kvx[after, :] = jnp.zeros((MARGIN, kvc), bf16)
        for g in range(kv_heads):
            hin[0, g] = jnp.zeros(hin.shape[2:], bf16)

    pl.when(has_left)(kv_right.wait_recv)
    pl.when(has_right)(kv_left.wait_recv)

    halos = []
    for g in range(kv_heads):
        cols = slice(g * wide, (g + 1) * wide)
        kcols = slice(g * 2 * HEAD_DIM, (g + 1) * 2 * HEAD_DIM)

        @pl.loop(0, blocks)
        def _(b):
            first = pl.multiple_of(b * BLOCK, BLOCK)
            qt = side_by_side(jnp.transpose(q_ref[pl.ds(first, BLOCK), cols] * SCALE))
            dct = side_by_side(jnp.transpose(dc_ref[pl.ds(first, BLOCK), cols]))
            zero = jnp.zeros_like(qt)
            qz = jnp.concatenate([qt, zero], axis=0)
            dcz = jnp.concatenate([zero, dct], axis=0)
            kv = kvx[pl.ds(first, WINDOW), kcols]
            kvt = jnp.transpose(kv)
            s = jnp.dot(kv, qz, preferred_element_type=f32)
            s = s + jnp.concatenate([bias[b]] * GROUP, axis=1)
            p = jnp.exp(s - jnp.max(s, axis=0, keepdims=True))
            w = p * (1.0 / jnp.sum(p, axis=0, keepdims=True))
            wh = w.astype(bf16)
            ctx = jnp.dot(kvt[HEAD_DIM:], wh, preferred_element_type=f32).astype(bf16)
            delta = jnp.sum(dct.astype(f32) * ctx.astype(f32), axis=0, keepdims=True)
            dp = jnp.dot(kv, dcz, preferred_element_type=f32)
            ds = (w * (dp - delta)).astype(bf16)
            dq = jnp.dot(kvt[:HEAD_DIM], ds, preferred_element_type=f32) * SCALE
            ctx_ref[pl.ds(first, BLOCK), cols] = jnp.transpose(stacked(ctx))
            dq_ref[pl.ds(first, BLOCK), cols] = jnp.transpose(stacked(dq.astype(bf16)))
            d_kv = lax.dot_general(ds, qz, NT, preferred_element_type=f32)
            d_kv = d_kv + lax.dot_general(wh, dcz, NT, preferred_element_type=f32)
            grad[pl.ds(first, WINDOW), kcols] += d_kv

        halo[0, g] = grad[:MARGIN, kcols].astype(bf16)
        halo[1, g] = grad[MARGIN + tok :, kcols].astype(bf16)
        to_left = remote(halo.at[0, g], hin.at[0, g], hs.at[0, g], hr.at[0, g], seq_dev(me - 1))
        to_right = remote(halo.at[1, g], hin.at[1, g], hs.at[1, g], hr.at[1, g], seq_dev(me + 1))
        pl.when(has_left)(to_left.start)
        pl.when(has_right)(to_right.start)
        halos.append((to_left, to_right))

    leave = [pltpu.make_async_copy(ctx_ref, ctx_hbm, os.at[0])]
    leave[0].start()
    zero = jnp.zeros((tok - MARGIN, 2 * HEAD_DIM), f32)
    for g, (to_left, to_right) in enumerate(halos):
        kcols = slice(g * 2 * HEAD_DIM, (g + 1) * 2 * HEAD_DIM)
        pl.when(has_left)(to_right.wait_recv)
        pl.when(has_right)(to_left.wait_recv)
        dkv[:, kcols] = (
            grad[MARGIN : MARGIN + tok, kcols]
            + jnp.concatenate([hin[1, g].astype(f32), zero], axis=0)
            + jnp.concatenate([zero, hin[0, g].astype(f32)], axis=0)
        ).astype(bf16)

    def to_up(c):
        return remote(part.at[c], inb.at[c], rs.at[c], rr.at[c], mp_dev(z + 1))

    def to_down(c):
        slot = jnp.where(c == z - 1, m, c)
        return remote(part.at[c], inb.at[slot], rs.at[c], rr.at[slot], mp_dev(z - 1))

    low = z < m // 2

    @pl.loop(0, m)
    def _(t):
        c = jnp.where(low, m - 1 - t, t)
        rows = pl.ds(pl.multiple_of(c * ch, ch), ch)

        @pl.loop(0, tok // 256)
        def _(i):
            r = pl.ds(pl.multiple_of(i * 256, 256), 256)
            part[c, r, :] = (
                lax.dot_general(dq_ref[r, :], wq_ref[rows, :], NT, preferred_element_type=f32)
                + lax.dot_general(dkv[r, :], wkv_ref[rows, :], NT, preferred_element_type=f32)
            ).astype(bf16)

        @pl.when((z == 0) & (c > z))
        def _():
            to_up(c).start()

        @pl.when((z == m - 1) & (c < z))
        def _():
            to_down(c).start()

    def arrived(slot):
        remote(part.at[0], inb.at[slot], rs.at[0], rr.at[slot], mp_dev(z)).wait_recv()

    def add_in(c, slot):
        arrived(slot)

        @pl.loop(0, tok // 128)
        def _(i):
            r = pl.ds(pl.multiple_of(i * 128, 128), 128)
            part[c, r, :] = (part[c, r, :].astype(f32) + inb[slot, r, :].astype(f32)).astype(bf16)

    inner = (z > 0) & (z < m - 1)

    def up_step(c):
        @pl.when(inner & (c > z))
        def _():
            add_in(c, c)
            to_up(c).start()

    def down_step(c):
        @pl.when(inner & (c < z))
        def _():
            add_in(c, c)
            to_down(c).start()

    def chain_steps(first, last):
        @pl.when(low)
        def _():
            @pl.loop(first, last)
            def _(t):
                up_step(m - 1 - t)
                down_step(t)

        @pl.when(jnp.logical_not(low))
        def _():
            @pl.loop(first, last)
            def _(t):
                down_step(t)
                up_step(m - 1 - t)

    if sum_seq:
        pw = gt.shape[3]
        pr = pw * kv_heads
        dkvt = jnp.transpose(dkv[...])
        for k in range(2):
            half = (1 - core) if k == 0 else core

            @pl.loop(0, chips)
            def _(j):
                cols = pl.ds(pl.multiple_of((2 * j + half) * pw, pw), pw)
                prod = jnp.dot(dkvt, x_ref[:, cols], preferred_element_type=f32)
                if k == 0:
                    gt[0, j] = prod.astype(bf16)
                else:
                    gsum[j] = prod

            if k == 0:
                swap = remote(gt.at[0], sib, ss, sr, seq_dev(sibling))
                swap.start()
        swap.wait_recv()

        def other(k):
            return (chip + k) % chips

        sends = []
        for k in range(1, chips):
            j = other(k)
            gt[1, j] = (gsum[j] + sib[j].astype(f32)).astype(bf16)
            cp = remote(gt.at[1, j], quart.at[k], qs.at[k], qr.at[k], seq_dev(j * 2 + core))
            cp.start()
            sends.append(cp)
        mine[...] = gsum[chip] + sib[chip].astype(f32)
        swap.wait_send()

        @pl.when(low)
        def _():
            up_step(m - 1)

        @pl.when(jnp.logical_not(low))
        def _():
            down_step(0)

        for cp in sends:
            cp.wait_recv()
        for k in range(1, chips):
            mine[...] += quart[k].astype(f32)
        for cp in sends:
            cp.wait_send()
        done = jnp.transpose(mine[...])
        for g in range(kv_heads):
            kcols = slice(g * 2 * HEAD_DIM, (g + 1) * 2 * HEAD_DIM)
            mix[pl.ds(g, pw, stride=kv_heads), :] = done[:, kcols]
        piece[...] = mix[...].astype(bf16)
        sends = []
        for k in range(1, chips):
            cp = remote(piece, got.at[k], gs.at[k], gr.at[k], seq_dev(other(k) * 2 + core))
            cp.start()
            sends.append(cp)

        @pl.when(low)
        def _():
            down_step(0)

        @pl.when(jnp.logical_not(low))
        def _():
            up_step(m - 1)

        chain_steps(1, m)
        got[0] = piece[...]
        for cp in sends:
            cp.wait()
        swap = remote(got, sib2, fs, fr, seq_dev(sibling))
        swap.start()
        for k in range(chips):
            src = (chip + chips - k) % chips
            rows = pl.ds(pl.multiple_of((2 * src + core) * pr, pr), pr)
            leave.append(pltpu.make_async_copy(got.at[k], kvg_hbm.at[rows], os.at[1 + k]))
            leave[-1].start()
        swap.wait_recv()
        for k in range(chips):
            src = (chip + chips - k) % chips
            rows = pl.ds(pl.multiple_of((2 * src + 1 - core) * pr, pr), pr)
            leave.append(pltpu.make_async_copy(sib2.at[k], kvg_hbm.at[rows], os.at[1 + chips + k]))
            leave[-1].start()
        swap.wait_send()
    else:
        leave.append(pltpu.make_async_copy(dkv, kvg_hbm, os.at[1]))
        leave[1].start()
        chain_steps(0, m)

    @pl.when(has_down)
    def _():
        arrived(z)

    @pl.when(jnp.logical_not(has_down))
    def _():
        inb[0] = jnp.zeros(inb.shape[1:], bf16)

    @pl.when(has_up)
    def _():
        arrived(m)

    @pl.when(jnp.logical_not(has_up))
    def _():
        inb[m] = jnp.zeros(inb.shape[1:], bf16)

    @pl.loop(0, tok // 128)
    def _(i):
        r = pl.ds(pl.multiple_of(i * 128, 128), 128)
        ig_ref[r, :] = (
            part[z, r, :].astype(f32) + inb[z, r, :].astype(f32) + inb[m, r, :].astype(f32)
        ).astype(bf16)

    @pl.loop(0, m)
    def _(c):
        @pl.when(c > z)
        def _():
            to_up(c).wait_send()

        @pl.when(c < z)
        def _():
            to_down(c).wait_send()

    for cp in leave:
        cp.wait()
    pl.when(has_left)(kv_left.wait_send)
    pl.when(has_right)(kv_right.wait_send)
    for to_left, to_right in halos:
        pl.when(has_left)(to_left.wait_send)
        pl.when(has_right)(to_right.wait_send)


def relay_kernel(n, ag, x_hbm, oc_hbm, wq_hbm, wkv_hbm, wo_hbm, seg_ref, band_ref,
                 ctx_hbm, ig_ref, kvg_hbm, ctx_ref, raw, wide_raw, x_ref, oc_ref, wall, wo_ref, q_ref, dc_ref,
                 kvx, kdocs, bias, grad, halo, hin, dall, wx, dout, dx, snd, rcv, tout, rin, part,
                 gt, gsum, sib, quart, got, mine, mix, piece, sib2,
                 ls, os, ks, kr, hs, hr, ss, sr, qs, qr, gs, gr, fs, fr,
                 zhs, zhr, zas, zar, pls, plr, pfs, pfr, pss, psr,
                 oqs, oqr, oks, okr, xqs, xqr, xks, xkr, rss, rsr, tos, tor, fas, far):
    tok, qc = q_ref.shape
    kvc = kvx.shape[1]
    ch = wall.shape[0] // 4
    blocks = tok // BLOCK
    kv_heads = kvc // (2 * HEAD_DIM)
    wide = GROUP * HEAD_DIM
    pair = 2 * HEAD_DIM
    held = ag * BLOCK
    me = lax.axis_index("seq")
    z = lax.axis_index("mp")
    core = me % 2
    sibling = me + 1 - 2 * core
    chip = me // 2
    chips = n // 2
    pr = ch // n
    outer = (z == 0) | (z == 3)
    inner = jnp.logical_not(outer)
    partner = jnp.where(outer, jnp.where(z == 0, 1, 2), jnp.where(z == 1, 0, 3))
    facing = 3 - z
    facing_partner = 3 - partner

    loads = [
        pltpu.make_async_copy(src, dst, ls.at[i])
        for i, (src, dst) in enumerate((
            (wkv_hbm, raw),
            (x_hbm, x_ref),
            (wq_hbm, wall.at[:, pl.ds(0, qc)]),
            (oc_hbm, oc_ref),
            (wo_hbm, wo_ref),
        ))
    ]
    for cp in loads:
        cp.start()

    def seq_dev(i):
        return (i, z)

    def mp_dev(i):
        return (me, i)

    barrier = pltpu.get_barrier_semaphore()
    has_left, has_right = me > 0, me < n - 1
    has_down, has_up = z > 0, z < 3

    def greet(dev):
        pl.semaphore_signal(barrier, inc=1, device_id=dev, device_id_type=MESH)

    for there, dev in (
        (has_left, seq_dev(me - 1)),
        (has_right, seq_dev(me + 1)),
        (has_down, mp_dev(z - 1)),
        (has_up, mp_dev(z + 1)),
    ):
        @pl.when(there)
        def _():
            greet(dev)
    for k in range(1, chips):
        greet(seq_dev(((chip + k) % chips) * 2 + core))
    peers = chips - 1
    for there in (has_left, has_right, has_down, has_up):
        peers = peers + there.astype(jnp.int32)
    pl.semaphore_wait(barrier, peers)

    def remote(src, dst, send, recv, dev):
        return pltpu.make_async_remote_copy(
            src_ref=src, dst_ref=dst, send_sem=send, recv_sem=recv, device_id=dev,
            device_id_type=MESH)

    qcols, kvcols = pl.ds(0, qc), pl.ds(qc, kvc)

    def rows_of(c):
        return pl.ds(pl.multiple_of(c * ch + me * pr, pr), pr)

    sent_chunks = (facing_partner, facing)
    zh = [[], []]
    for j, c in enumerate(sent_chunks):
        zh[0].append(remote(wq_hbm.at[rows_of(c), :], wx.at[j, chip, core, :, qcols], zhs.at[0, j], zhr.at[0, j], mp_dev(partner)))
        zh[1].append(remote(wall.at[rows_of(c), kvcols], wx.at[j, chip, core, :, kvcols], zhs.at[1, j], zhr.at[1, j], mp_dev(partner)))
    za = [[], [], []]
    if ag:
        za.append([])
        for j, c in enumerate((facing_partner, facing)):
            za[0].append(remote(wq_hbm.at[rows_of(c), :], wx.at[(2, 4)[j], chip, core, :, qcols], zas.at[0, j], zar.at[0, j], mp_dev(facing)))
            za[1].append(remote(wall.at[rows_of(c), kvcols], wx.at[(2, 4)[j], chip, core, :, kvcols], zas.at[1, j], zar.at[1, j], mp_dev(facing)))
            for i, cols in enumerate((qcols, kvcols)):
                za[2 + i].append(remote(
                    wx.at[1 - j, chip, core, :, cols], wx.at[(3, 5)[j], chip, core, :, cols],
                    zas.at[2 + i, j], zar.at[2 + i, j], mp_dev(facing)))

    def each(cps, what):
        for cp in cps:
            getattr(cp, what)()

    @pl.when(outer)
    def _():
        each(zh[0], "start")

    @pl.when(inner)
    def _():
        each(za[0], "start")

    xchip, ychip = chip + 1 - 2 * (chip % 2), (chip + 2) % chips
    dchip = (xchip + 2) % chips
    sets = ((0, 2), (2, 2), (4, 2))
    half = pr // 2
    to_x, to_y, via_x, via_y, to_sib = [], [], [], [], []
    for i, (first, count) in enumerate(sets):
        ksl = pl.ds(first, count)
        own = wx.at[ksl, chip, core]
        to_x.append(remote(own, own, pls.at[0, i], plr.at[0, i], seq_dev(xchip * 2 + core)))
        to_y.append(remote(own, own, pls.at[1, i], plr.at[1, i], seq_dev(ychip * 2 + core)))
        lo = wx.at[ksl, xchip, core, pl.ds(0, half)]
        hi = wx.at[ksl, ychip, core, pl.ds(half, half)]
        via_y.append(remote(lo, lo, pfs.at[0, i], pfr.at[0, i], seq_dev(ychip * 2 + core)))
        via_x.append(remote(hi, hi, pfs.at[1, i], pfr.at[1, i], seq_dev(xchip * 2 + core)))
        row = []
        for j, c in enumerate((chip, xchip, ychip, dchip)):
            block = wx.at[ksl, c, core]
            row.append(remote(block, block, pss.at[i, j], psr.at[i, j], seq_dev(sibling)))
        to_sib.append(row)

    def plane_start(i):
        to_x[i].start()
        to_y[i].start()
        to_sib[i][0].start()

    def plane_wait_x(i):
        first, count = sets[i]
        dst = wx.at[pl.ds(first, count), xchip, core]
        remote(dst, dst, pls.at[0, i], plr.at[0, i], seq_dev(sibling)).wait_recv()

    def plane_wait_y(i):
        first, count = sets[i]
        dst = wx.at[pl.ds(first, count), ychip, core]
        remote(dst, dst, pls.at[1, i], plr.at[1, i], seq_dev(sibling)).wait_recv()

    def plane_relay(i):
        plane_wait_x(i)
        via_y[i].start()
        to_sib[i][1].start()
        plane_wait_y(i)
        via_x[i].start()
        to_sib[i][2].start()

    def plane_pair(i):
        first, count = sets[i]
        for f, s in enumerate((pl.ds(0, half), pl.ds(half, half))):
            dst = wx.at[pl.ds(first, count), dchip, core, s]
            remote(dst, dst, pfs.at[f, i], pfr.at[f, i], seq_dev(sibling)).wait_recv()
        to_sib[i][3].start()

    def plane_done(i):
        first, count = sets[i]
        for j, c in enumerate((chip, xchip, ychip, dchip)):
            dst = wx.at[pl.ds(first, count), c, 1 - core]
            remote(dst, dst, pss.at[i, j], psr.at[i, j], seq_dev(sibling)).wait_recv()

    loads[0].wait()
    span = wide_raw.shape[0] // kv_heads

    @pl.loop(0, wall.shape[0] // span)
    def _(i):
        wide_raw[...] = raw[pl.ds(pl.multiple_of(i * span * kv_heads, 256), span * kv_heads), :].astype(f32)
        for g in range(kv_heads):
            wall[pl.ds(pl.multiple_of(i * span, 256), span), qc + g * 128 : qc + (g + 1) * 128] = (
                wide_raw[pl.ds(g, span, stride=kv_heads), :].astype(bf16)
            )

    @pl.when(outer)
    def _():
        each(zh[1], "start")

    @pl.when(inner)
    def _():
        each(za[1], "start")

    loads[1].wait()

    @pl.loop(0, tok // 256)
    def _(i):
        r = pl.ds(pl.multiple_of(i * 256, 256), 256)
        ro = pl.ds(pl.multiple_of(i * 256 + MARGIN, 256), 256)
        kvx[ro, :] = jnp.dot(x_ref[r, :], wall[:, qc:], preferred_element_type=f32).astype(bf16)

    before, after = pl.ds(0, MARGIN), pl.ds(MARGIN + tok, MARGIN)
    kv_left = remote(kvx.at[pl.ds(MARGIN, MARGIN)], kvx.at[after], ks.at[0], kr.at[0], seq_dev(me - 1))
    kv_right = remote(kvx.at[pl.ds(tok, MARGIN)], kvx.at[before], ks.at[1], kr.at[1], seq_dev(me + 1))
    pl.when(has_left)(kv_left.start)
    pl.when(has_right)(kv_right.start)

    for kb in range(blocks + 4):
        row = me * blocks + kb - 2
        inside = (row >= 0) & (row < n * blocks)
        docs = seg_ref[pl.ds(jnp.clip(row, 0, n * blocks - 1), 1), :]
        docs = jnp.where(inside, docs, -1)
        kdocs[kb] = jnp.transpose(jnp.broadcast_to(docs, (BLOCK, BLOCK)))

    @pl.loop(0, blocks)
    def _(b):
        qdoc = seg_ref[pl.ds(me * blocks + b, 1), :]
        for o in range(5):
            same = kdocs[b + o] == qdoc
            if o != 2:
                same = same & (band_ref[b, o if o < 2 else o - 1] == 1)
            bias[b, o * BLOCK : (o + 1) * BLOCK, :] = jnp.where(same, 0.0, -1e30).astype(f32)

    grad[...] = jnp.zeros_like(grad)
    loads[2].wait()

    @pl.when(inner)
    def _():
        each(zh[0], "wait_recv")
        each(za[2], "start")

    @pl.loop(0, tok // 256)
    def _(i):
        r = pl.ds(pl.multiple_of(i * 256, 256), 256)
        q_ref[r, :] = jnp.dot(x_ref[r, :], wall[:, :qc], preferred_element_type=f32).astype(bf16)

    @pl.when(inner)
    def _():
        each(zh[1], "wait_recv")
        each(za[3], "start")
        plane_start(0)

    loads[3].wait()
    loads[4].wait()

    @pl.loop(0, tok // 256)
    def _(i):
        r = pl.ds(pl.multiple_of(i * 256, 256), 256)
        dc_ref[r, :] = lax.dot_general(
            oc_ref[r, :], wo_ref[...], NT, preferred_element_type=f32
        ).astype(bf16)

    @pl.when(jnp.logical_not(has_left))
    def _():
        kvx[before, :] = jnp.zeros((MARGIN, kvc), bf16)
        for g in range(kv_heads):
            hin[1, g] = jnp.zeros(hin.shape[2:], bf16)

    @pl.when(jnp.logical_not(has_right))
    def _():
        kvx[after, :] = jnp.zeros((MARGIN, kvc), bf16)
        for g in range(kv_heads):
            hin[0, g] = jnp.zeros(hin.shape[2:], bf16)

    pl.when(has_left)(kv_right.wait_recv)
    pl.when(has_right)(kv_left.wait_recv)

    def block_rows(b):
        return pl.ds(pl.multiple_of(b * BLOCK, BLOCK), BLOCK)

    def dq_out(g, b):
        at = (block_rows(b), pl.ds(g * wide, wide))
        return remote(dall.at[at], dout.at[at], oqs.at[g, b], oqr.at[g, b], mp_dev(partner))

    def dq_across(which, g, b):
        at = (block_rows(b), pl.ds(g * wide, wide))
        src = dall.at[at] if which == 0 else dout.at[at]
        return remote(src, dx.at[(which,) + at], xqs.at[which, g, b], xqr.at[which, g, b], mp_dev(facing))

    def dkv_cols(g):
        return pl.ds(qc + g * pair, pair)

    def dkv_out(g, early):
        rows = pl.ds(0, held) if early else pl.ds(held, tok - held)
        at = (rows, dkv_cols(g))
        i = 1 if early else 0
        return remote(dall.at[at], dout.at[at], oks.at[g, i], okr.at[g, i], mp_dev(partner))

    def dkv_across(which, g):
        at = (pl.ds(0, held), dkv_cols(g))
        src = dall.at[at] if which == 0 else dout.at[at]
        return remote(src, dx.at[(which,) + at], xks.at[which, g], xkr.at[which, g], mp_dev(facing))

    def dkv_rest_across(g):
        at = (pl.ds(held, tok - held), dkv_cols(g))
        return remote(dout.at[at], dx.at[(1,) + at], xks.at[2, g], xkr.at[2, g], mp_dev(facing))

    def halo_left(g):
        return remote(halo.at[0, g], hin.at[0, g], hs.at[0, g], hr.at[0, g], seq_dev(me - 1))

    def halo_right(g):
        return remote(halo.at[1, g], hin.at[1, g], hs.at[1, g], hr.at[1, g], seq_dev(me + 1))

    def finish_late(g):
        pl.when(has_right)(halo_left(g).wait_recv)
        dall[held:, qc + g * pair : qc + (g + 1) * pair] = (
            grad[MARGIN + held : MARGIN + tok, g * pair : (g + 1) * pair] + hin[0, g].astype(f32)
        ).astype(bf16)
        pl.when(outer)(dkv_out(g, False).start)

    def finish_early(g):
        pl.when(has_left)(halo_right(g).wait_recv)
        dall[:held, qc + g * pair : qc + (g + 1) * pair] = (
            grad[MARGIN : MARGIN + held, g * pair : (g + 1) * pair] + hin[1, g].astype(f32)
        ).astype(bf16)
        pl.when(outer)(dkv_out(g, True).start)
        pl.when(inner)(dkv_across(0, g).start)

    for g in range(kv_heads):
        cols = slice(g * wide, (g + 1) * wide)
        kcols = slice(g * pair, (g + 1) * pair)

        @pl.loop(0, blocks)
        def _(b):
            first = pl.multiple_of(b * BLOCK, BLOCK)
            qt = side_by_side(jnp.transpose(q_ref[pl.ds(first, BLOCK), cols] * SCALE))
            dct = side_by_side(jnp.transpose(dc_ref[pl.ds(first, BLOCK), cols]))
            zero = jnp.zeros_like(qt)
            qz = jnp.concatenate([qt, zero], axis=0)
            dcz = jnp.concatenate([zero, dct], axis=0)
            kv = kvx[pl.ds(first, WINDOW), kcols]
            kvt = jnp.transpose(kv)
            s = jnp.dot(kv, qz, preferred_element_type=f32)
            s = s + jnp.concatenate([bias[b]] * GROUP, axis=1)
            p = jnp.exp(s - jnp.max(s, axis=0, keepdims=True))
            w = p * (1.0 / jnp.sum(p, axis=0, keepdims=True))
            wh = w.astype(bf16)
            ctx = jnp.dot(kvt[HEAD_DIM:], wh, preferred_element_type=f32).astype(bf16)
            delta = jnp.sum(dct.astype(f32) * ctx.astype(f32), axis=0, keepdims=True)
            dp = jnp.dot(kv, dcz, preferred_element_type=f32)
            ds = (w * (dp - delta)).astype(bf16)
            dq = jnp.dot(kvt[:HEAD_DIM], ds, preferred_element_type=f32) * SCALE
            ctx_ref[pl.ds(first, BLOCK), cols] = jnp.transpose(stacked(ctx))
            dall[pl.ds(first, BLOCK), cols] = jnp.transpose(stacked(dq.astype(bf16)))
            d_kv = lax.dot_general(ds, qz, NT, preferred_element_type=f32)
            d_kv = d_kv + lax.dot_general(wh, dcz, NT, preferred_element_type=f32)
            grad[pl.ds(first, WINDOW), kcols] += d_kv

            @pl.when(outer)
            def _():
                dq_out(g, b).start()

            @pl.when(inner & (b < ag))
            def _():
                dq_across(0, g, b).start()

            @pl.when(inner & (b >= 2) & (b < ag + 2))
            def _():
                dq_out(g, b - 2).wait_recv()
                dq_across(1, g, b - 2).start()

            @pl.when(b == 1)
            def _():
                halo[0, g] = grad[:MARGIN, kcols].astype(bf16)
                pl.when(has_left)(halo_left(g).start)

            if g == 0:
                @pl.when(inner & (b == 1))
                def _():
                    each(za[0] + za[1] + za[2] + za[3], "wait_recv")
                    plane_start(1)

                @pl.when(inner & (b == blocks - 1))
                def _():
                    plane_relay(0)

            if g == 1:
                @pl.when(inner & (b == 1))
                def _():
                    plane_relay(1)

                @pl.when(b == 1)
                def _():
                    finish_early(0)
                    finish_late(0)

                @pl.when(inner & (b == blocks - 1))
                def _():
                    plane_pair(0)

        halo[1, g] = grad[MARGIN + tok :, kcols].astype(bf16)
        pl.when(has_right)(halo_right(g).start)

    def chunk(c):
        return pl.ds(pl.multiple_of(c * ch, ch), ch)

    def times_own(r, c):
        return lax.dot_general(dall[r, :], wall[chunk(c), :], NT, preferred_element_type=f32)

    def times_sent(d, k):
        return lax.dot_general(d, wx[k].reshape(ch, qc + kvc), NT, preferred_element_type=f32)

    summed = tok - held
    last = kv_heads - 1

    def sum_piece(slot, i):
        at = (slot, pl.ds(i * BLOCK, BLOCK))
        return remote(snd.at[at], rcv.at[at], rss.at[slot, i], rsr.at[slot, i], mp_dev(facing))

    def out_piece(i):
        at = block_rows(i)
        return remote(tout.at[at], rin.at[at], tos.at[i], tor.at[i], mp_dev(partner))

    early, late = slice(0, held), slice(held, tok)
    cut = qc + kvc - pair

    leave = [pltpu.make_async_copy(ctx_ref, ctx_hbm, os.at[0])]
    leave[0].start()
    finish_late(1)

    @pl.when(inner)
    def _():
        dkv_out(0, True).wait_recv()
        dkv_across(1, 0).start()
        for j, c in enumerate((facing_partner, facing, partner, z)):
            part[j] = times_own(late, c)

    @pl.when(outer)
    def _():
        tout[late, :] = times_own(late, partner).astype(bf16)
        part[3] = times_own(late, z)

    finish_early(1)

    @pl.when(inner)
    def _():
        plane_start(2)
        plane_pair(1)
        part[4] = times_own(early, partner)
        part[5] = times_own(early, z)

    @pl.when(outer)
    def _():
        tout[early, :] = times_own(early, partner).astype(bf16)
        part[5] = times_own(early, z)
        dkv_out(last, False).wait_send()
        dkv_out(last, True).wait_send()
        for i in range(blocks):
            out_piece(i).start()

    pw = gt.shape[3]
    gr_rows = pw * kv_heads
    dkvt = jnp.transpose(dall[:, qc:])
    for k in range(2):
        own_half = (1 - core) if k == 0 else core

        @pl.loop(0, chips)
        def _(j):
            cols = pl.ds(pl.multiple_of((2 * j + own_half) * pw, pw), pw)
            prod = jnp.dot(dkvt, x_ref[:, cols], preferred_element_type=f32)
            if k == 0:
                gt[0, j] = prod.astype(bf16)
            else:
                gsum[j] = prod

        if k == 0:
            swap = remote(gt.at[0], sib, ss, sr, seq_dev(sibling))
            swap.start()

    def times_cut(d, k):
        return lax.dot_general(
            d, wx[k, :, :, :, :cut].reshape(ch, cut), NT, preferred_element_type=f32)

    def rest_on():
        src = dx.at[1, :, pl.ds(cut, pair)]
        return remote(src, src, fas.at[0], far.at[0], mp_dev(partner))

    def rest_rows_on():
        src = wx.at[3, :, :, :, pl.ds(cut, pair)]
        return remote(src, src, fas.at[1], far.at[1], mp_dev(partner))

    @pl.when(inner)
    def _():
        for g in range(last):
            dkv_out(g, False).wait_recv()
        plane_done(0)
        for b in range(ag, blocks):
            for g in range(kv_heads):
                dq_out(g, b).wait_recv()
            i = b - ag
            r = slice(b * BLOCK, (b + 1) * BLOCK)
            snd[1, i * BLOCK : (i + 1) * BLOCK, :] = (
                part[0, i * BLOCK : (i + 1) * BLOCK, :] + times_cut(dout[r, :cut], 1)
            ).astype(bf16)
            sum_piece(1, i).start()
        plane_done(1)
        rest_rows_on().start()
        for which in range(2):
            for g in range(kv_heads):
                for b in range(ag):
                    dq_across(which, g, b).wait_recv()
                if which == 0 or g < last:
                    dkv_across(which, g).wait_recv()
        tout[early, :] = (
            part[4] + times_sent(dx[0, early, :], 2) + times_cut(dx[1, early, :cut], 3)
        ).astype(bf16)
        for i in range(ag):
            out_piece(i).start()

    swap.wait_recv()

    def other(k):
        return (chip + k) % chips

    sends = []
    for k in range(1, chips):
        j = other(k)
        gt[1, j] = (gsum[j] + sib[j].astype(f32)).astype(bf16)
        cp = remote(gt.at[1, j], quart.at[k], qs.at[k], qr.at[k], seq_dev(j * 2 + core))
        cp.start()
        sends.append(cp)
    mine[...] = gsum[chip] + sib[chip].astype(f32)
    swap.wait_send()

    @pl.when(inner)
    def _():
        plane_relay(2)
        dkv_out(last, False).wait_recv()
        dkv_rest_across(last).start()
        dkv_out(last, True).wait_recv()
        dkv_across(1, last).start()
        snd[0] = (part[1] + times_sent(dout[late, :], 0)).astype(bf16)
        for i in range(blocks - ag):
            sum_piece(0, i).start()

    @pl.when(inner)
    def _():
        for i in range(summed // BLOCK):
            r = slice(held + i * BLOCK, held + (i + 1) * BLOCK)
            p = slice(i * BLOCK, (i + 1) * BLOCK)
            sum_piece(1, i).wait_recv()
            tout[r, :] = (part[2, p, :] + rcv[1, p, :].astype(f32)).astype(bf16)
            out_piece(ag + i).start()

    for cp in sends:
        cp.wait_recv()
    for k in range(1, chips):
        mine[...] += quart[k].astype(f32)
    for cp in sends:
        cp.wait_send()
    done = jnp.transpose(mine[...])
    for g in range(kv_heads):
        kcols = slice(g * pair, (g + 1) * pair)
        mix[pl.ds(g, pw, stride=kv_heads), :] = done[:, kcols]
    piece[...] = mix[...].astype(bf16)
    sends = []
    for k in range(1, chips):
        cp = remote(piece, got.at[k], gs.at[k], gr.at[k], seq_dev(other(k) * 2 + core))
        cp.start()
        sends.append(cp)

    @pl.when(inner)
    def _():
        dkv_across(1, last).wait_recv()
        dkv_rest_across(last).wait_recv()
        rest_on().start()
        plane_pair(2)
        plane_done(2)
        for i in range(ag):
            out_piece(i).wait_recv()
        ig_ref[early, :] = (
            part[5] + rin[early, :].astype(f32)
            + times_sent(dx[0, early, :], 4) + times_sent(dx[1, early, :], 5)
        ).astype(bf16)

    got[0] = piece[...]
    for cp in sends:
        cp.wait()
    swap = remote(got, sib2, fs, fr, seq_dev(sibling))
    swap.start()
    for k in range(chips):
        src = (chip + chips - k) % chips
        rows = pl.ds(pl.multiple_of((2 * src + core) * gr_rows, gr_rows), gr_rows)
        leave.append(pltpu.make_async_copy(got.at[k], kvg_hbm.at[rows], os.at[1 + k]))
        leave[-1].start()
    swap.wait_recv()
    for k in range(chips):
        src = (chip + chips - k) % chips
        rows = pl.ds(pl.multiple_of((2 * src + 1 - core) * gr_rows, gr_rows), gr_rows)
        leave.append(pltpu.make_async_copy(sib2.at[k], kvg_hbm.at[rows], os.at[1 + chips + k]))
        leave[-1].start()
    swap.wait_send()

    @pl.when(inner)
    def _():
        for i in range(ag, blocks):
            out_piece(i).wait_recv()
        for i in range(summed // BLOCK):
            sum_piece(0, i).wait_recv()
        ig_ref[late, :] = (part[3] + rin[late, :].astype(f32) + rcv[0].astype(f32)).astype(bf16)

    @pl.when(outer)
    def _():
        rest_rows_on().wait_recv()
        for i in range(blocks):
            out_piece(i).wait_recv()
        rest_on().wait_recv()
        for r, mine_part in ((early, part[5]), (late, part[3])):
            far_part = lax.dot_general(
                dx[1, r, cut:], wx[3, :, :, :, cut:].reshape(ch, pair), NT, preferred_element_type=f32)
            ig_ref[r, :] = (mine_part + far_part + rin[r, :].astype(f32)).astype(bf16)

    @pl.when(outer)
    def _():
        for g in range(kv_heads):
            for b in range(blocks):
                dq_out(g, b).wait_send()
            if g < last:
                dkv_out(g, False).wait_send()
                dkv_out(g, True).wait_send()
        each(zh[0], "wait_send")
        each(zh[1], "wait_send")

    @pl.when(inner)
    def _():
        for which in range(2 if ag else 0):
            for g in range(kv_heads):
                for b in range(ag):
                    dq_across(which, g, b).wait_send()
                dkv_across(which, g).wait_send()
        dkv_rest_across(last).wait_send()
        rest_on().wait_send()
        rest_rows_on().wait_send()
        for slot in range(2):
            for i in range(blocks - ag):
                sum_piece(slot, i).wait_send()
        for group in za:
            each(group, "wait_send")
        for group in (to_x, to_y, via_x, via_y, *to_sib):
            each(group, "wait_send")

    for i in range(blocks):
        out_piece(i).wait_send()
    for cp in leave:
        cp.wait()
    pl.when(has_left)(kv_left.wait_send)
    pl.when(has_right)(kv_right.wait_send)
    for g in range(kv_heads):
        pl.when(has_left)(halo_left(g).wait_send)
        pl.when(has_right)(halo_right(g).wait_send)


def write_kernel(ctx_hbm, ig_hbm, kvg_hbm, ctx_out, ig_out, kvg_out, half, full, ctx_mid, ig_mid, ins, outs):
    pieces, rows = half.shape[0], half.shape[1]
    loads, stores = [], []
    for i in range(pieces):
        loads.append(pltpu.make_async_copy(kvg_hbm.at[pl.ds(i * rows, rows)], half.at[i], ins.at[i]))
        stores.append(pltpu.make_async_copy(full.at[i], kvg_out.at[pl.ds(i * rows, rows)], outs.at[i]))
        loads[i].start()
    for i, (src, mid, dst) in enumerate(((ctx_hbm, ctx_mid, ctx_out), (ig_hbm, ig_mid, ig_out))):
        loads.append(pltpu.make_async_copy(src, mid, ins.at[pieces + i]))
        stores.append(pltpu.make_async_copy(mid, dst, outs.at[pieces + i]))
        loads[-1].start()
    for i in range(pieces):
        loads[i].wait()
        full[i] = half[i].astype(f32)
        stores[i].start()
    for i in range(pieces, pieces + 2):
        loads[i].wait()
        stores[i].start()
    for cp in stores:
        cp.wait()


def written(*arrays):
    pieces = 4
    rows, lanes = arrays[2].shape[0] // pieces, arrays[2].shape[1]
    return pl.pallas_call(
        write_kernel,
        out_shape=[
            jax.ShapeDtypeStruct(a.shape, t) for a, t in zip(arrays, (bf16, bf16, f32))
        ],
        in_specs=[ANY] * 3,
        out_specs=[ANY] * 3,
        scratch_shapes=[
            pltpu.VMEM((pieces, rows, lanes), bf16),
            pltpu.VMEM((pieces, rows, lanes), f32),
            pltpu.VMEM(arrays[0].shape, bf16),
            pltpu.VMEM(arrays[1].shape, bf16),
            pltpu.SemaphoreType.DMA((pieces + 2,)),
            pltpu.SemaphoreType.DMA((pieces + 2,)),
        ],
        compiler_params=pltpu.CompilerParams(vmem_limit_bytes=60 * 2**20),
        name="write",
    )(*arrays)


def local(n, m, normed, out_cotangent, segments, band_mask, query_weight, key_value_weight, out_weight):
    tok, width = normed.shape
    qc = query_weight.shape[1]
    kv_heads = key_value_weight.shape[1]
    pair = 2 * HEAD_DIM
    kvc = kv_heads * pair
    wkv = key_value_weight.reshape(width * kv_heads, pair)
    blocks = tok // BLOCK
    ch = width // m
    pw = width // n
    sum_seq = n % 2 == 0 and n * 128 <= width and width % (n * 128) == 0
    chips = n // 2
    dma = pltpu.SemaphoreType.DMA
    vmem = pltpu.VMEM
    relay = n == 8 and m == 4 and kv_heads == 2 and tok == 4 * BLOCK and sum_seq
    scratch = [
        vmem((tok, qc), bf16),
        vmem((width * kv_heads, pair), bf16),
        vmem((256 * kv_heads, pair), f32),
        vmem((tok, width), bf16),
        vmem((tok, width), bf16),
        vmem((width, qc), bf16),
        vmem((width, kvc), bf16),
        vmem((qc, width), bf16),
        vmem((tok, qc), bf16),
        vmem((tok, qc), bf16),
        vmem((tok + 2 * MARGIN, kvc), bf16),
        vmem((blocks + 4, BLOCK, BLOCK), jnp.int32),
        vmem((blocks, WINDOW, BLOCK), f32),
        vmem((tok + 2 * MARGIN, kvc), f32),
        vmem((2, kv_heads, MARGIN, pair), bf16),
        vmem((2, kv_heads, MARGIN, pair), bf16),
        vmem((tok, qc), bf16),
        vmem((tok, kvc), bf16),
        vmem((m, tok, ch), bf16),
        vmem((m + 1, tok, ch), bf16),
        dma((5,)),
        dma((1 + n,)),
        dma((2,)),
        dma((2,)),
        dma((2, kv_heads)),
        dma((2, kv_heads)),
        dma((m,)),
        dma((m + 1,)),
    ]
    if sum_seq:
        kvg_shape = (width * kv_heads, pair)
        if not relay:
            scratch += [
                vmem((2, chips, kvc, pw), bf16),
                vmem((chips, kvc, pw), f32),
                vmem((chips, kvc, pw), bf16),
                vmem((chips, kvc, pw), bf16),
                vmem((chips, pw * kv_heads, pair), bf16),
                vmem((kvc, pw), f32),
                vmem((pw * kv_heads, pair), f32),
                vmem((pw * kv_heads, pair), bf16),
                vmem((chips, pw * kv_heads, pair), bf16),
                dma, dma, dma((chips,)), dma((chips,)), dma((chips,)), dma((chips,)), dma, dma,
            ]
    else:
        kvg_shape = (tok, kvc)
    ag = AHEAD
    held = ag * BLOCK
    relay_scratch = [
        vmem((tok, qc), bf16),
        vmem((width * kv_heads, pair), bf16),
        vmem((256 * kv_heads, pair), f32),
        vmem((tok, width), bf16),
        vmem((tok, width), bf16),
        vmem((width, qc + kvc), bf16),
        vmem((qc, width), bf16),
        vmem((tok, qc), bf16),
        vmem((tok, qc), bf16),
        vmem((tok + 2 * MARGIN, kvc), bf16),
        vmem((blocks + 4, BLOCK, BLOCK), jnp.int32),
        vmem((blocks, WINDOW, BLOCK), f32),
        vmem((tok + 2 * MARGIN, kvc), f32),
        vmem((2, kv_heads, MARGIN, pair), bf16),
        vmem((2, kv_heads, MARGIN, pair), bf16),
        vmem((tok, qc + kvc), bf16),
        vmem((6, max(chips, 1), 2, max(ch // n, 8), qc + kvc), bf16),
        vmem((tok, qc + kvc), bf16),
        vmem((2, tok, qc + kvc), bf16),
        vmem((2, max(tok - held, BLOCK), ch), bf16),
        vmem((2, max(tok - held, BLOCK), ch), bf16),
        vmem((tok, ch), bf16),
        vmem((tok, ch), bf16),
        vmem((6, MARGIN, ch), f32),
        vmem((2, chips, kvc, pw), bf16),
        vmem((chips, kvc, pw), f32),
        vmem((chips, kvc, pw), bf16),
        vmem((chips, kvc, pw), bf16),
        vmem((chips, pw * kv_heads, pair), bf16),
        vmem((kvc, pw), f32),
        vmem((pw * kv_heads, pair), f32),
        vmem((pw * kv_heads, pair), bf16),
        vmem((chips, pw * kv_heads, pair), bf16),
        dma((5,)),
        dma((1 + n,)),
        dma((2,)),
        dma((2,)),
        dma((2, kv_heads)),
        dma((2, kv_heads)),
        dma, dma, dma((chips,)), dma((chips,)), dma((chips,)), dma((chips,)), dma, dma,
        dma((2, 3)), dma((2, 3)),
        dma((4, 2)), dma((4, 2)),
        dma((2, 3)), dma((2, 3)),
        dma((2, 3)), dma((2, 3)),
        dma((3, 4)), dma((3, 4)),
        dma((kv_heads, blocks)), dma((kv_heads, blocks)),
        dma((kv_heads, 2)), dma((kv_heads, 2)),
        dma((2, kv_heads, blocks)), dma((2, kv_heads, blocks)),
        dma((3, kv_heads)), dma((3, kv_heads)),
        dma((2, blocks)), dma((2, blocks)),
        dma((blocks,)), dma((blocks,)),
        dma((2,)), dma((2,)),
    ]
    if relay:
        scratch = relay_scratch
        body = functools.partial(relay_kernel, n, ag)
    else:
        body = functools.partial(fused_kernel, n, m, sum_seq)
    context, input_grad, other = pl.pallas_call(
        body,
        out_shape=[
            jax.ShapeDtypeStruct((tok, qc), bf16),
            jax.ShapeDtypeStruct((tok, ch), bf16),
            jax.ShapeDtypeStruct(kvg_shape, bf16),
        ],
        in_specs=[ANY] * 5 + [VMEM, SMEM],
        out_specs=[ANY, VMEM, ANY],
        scratch_shapes=scratch,
        compiler_params=pltpu.CompilerParams(
            vmem_limit_bytes=56 * 2**20, collective_id=0, has_side_effects=True
        ),
        name="fused",
    )(normed, out_cotangent, query_weight, wkv, out_weight, segments.reshape(-1, BLOCK), band_mask)
    if sum_seq:
        context, input_grad, kv_grad = written(context, input_grad, other)
    else:
        kv_grad = lax.dot_general(normed, other, (((0,), (0,)), ((), ())), preferred_element_type=f32)
        kv_grad = lax.psum(kv_grad, "seq")
    return context, input_grad, kv_grad.reshape(width, kv_heads, pair)


def solution(mesh):
    placed = (
        P("seq", None),
        P("seq", None),
        P(),
        P("seq", None),
        P(None, "mp"),
        P(None, "mp", None),
        P("mp", None),
    )
    return jax.shard_map(
        functools.partial(local, mesh.shape["seq"], mesh.shape["mp"]),
        mesh=mesh,
        in_specs=placed,
        out_specs=(P("seq", "mp"), P("seq", "mp"), P(None, "mp", None)),
        check_vma=False,
    )
```

```python
import functools

import jax
import jax.numpy as jnp
from jax import lax
from jax.experimental import pallas as pl
from jax.experimental.pallas import tpu as pltpu
from jax.sharding import PartitionSpec as P

QUERY_HEADS = 32
KEY_VALUE_HEADS = 8
GROUP = QUERY_HEADS // KEY_VALUE_HEADS
HEAD_DIM = 64
BLOCK = 128
MARGIN = 2 * BLOCK
WINDOW = BLOCK + 2 * MARGIN
SCALE = 0.125
AHEAD = 2

MESH = pl.DeviceIdType.MESH
NT = (((1,), (1,)), ((), ()))
f32 = jnp.float32
bf16 = jnp.bfloat16
ANY = pl.BlockSpec(memory_space=pl.ANY)
VMEM = pl.BlockSpec(memory_space=pltpu.VMEM)
SMEM = pl.BlockSpec(memory_space=pltpu.SMEM)


def side_by_side(x):
    return jnp.concatenate([x[h * HEAD_DIM : (h + 1) * HEAD_DIM] for h in range(GROUP)], axis=1)


def stacked(x):
    return jnp.concatenate([x[:, h * BLOCK : (h + 1) * BLOCK] for h in range(GROUP)], axis=0)


def fused_kernel(n, m, sum_seq, x_hbm, oc_hbm, wq_hbm, wkv_hbm, wo_hbm, seg_ref, band_ref,
                 ctx_hbm, ig_ref, kvg_hbm, ctx_ref, raw, wide_raw, x_ref, oc_ref, wq_ref, wkv_ref, wo_ref, q_ref, dc_ref,
                 kvx, kdocs, bias, grad, halo, hin, dq_ref, dkv, part, inb, ls, os, ks, kr, hs, hr, rs, rr,
                 *rest):
    if sum_seq:
        (gt, gsum, sib, quart, got, mine, mix, piece, sib2,
         ss, sr, qs, qr, gs, gr, fs, fr) = rest
    tok, kvc = dkv.shape
    blocks = tok // BLOCK
    kv_heads = kvc // (2 * HEAD_DIM)
    wide = GROUP * HEAD_DIM
    loads = [
        pltpu.make_async_copy(src, dst, ls.at[i])
        for i, (src, dst) in enumerate(
            ((wkv_hbm, raw), (x_hbm, x_ref), (wq_hbm, wq_ref), (oc_hbm, oc_ref), (wo_hbm, wo_ref))
        )
    ]
    for cp in loads:
        cp.start()
    ch = part.shape[2]
    me = lax.axis_index("seq")
    z = lax.axis_index("mp")
    core = me % 2
    sibling = me + 1 - 2 * core
    chip = me // 2
    chips = n // 2

    def seq_dev(i):
        return (i, z)

    def mp_dev(i):
        return (me, i)

    barrier = pltpu.get_barrier_semaphore()
    has_left, has_right = me > 0, me < n - 1
    has_down, has_up = z > 0, z < m - 1

    def greet(dev):
        pl.semaphore_signal(barrier, inc=1, device_id=dev, device_id_type=MESH)

    for there, dev in (
        (has_left, seq_dev(me - 1)),
        (has_right, seq_dev(me + 1)),
        (has_down, mp_dev(z - 1)),
        (has_up, mp_dev(z + 1)),
    ):
        @pl.when(there)
        def _():
            greet(dev)
    if sum_seq:
        for k in range(1, chips):
            greet(seq_dev(((chip + k) % chips) * 2 + core))
    peers = chips - 1 if sum_seq else 0
    for there in (has_left, has_right, has_down, has_up):
        peers = peers + there.astype(jnp.int32)
    pl.semaphore_wait(barrier, peers)

    def remote(src, dst, send, recv, dev):
        return pltpu.make_async_remote_copy(
            src_ref=src, dst_ref=dst, send_sem=send, recv_sem=recv, device_id=dev,
            device_id_type=MESH)

    loads[0].wait()
    span = wide_raw.shape[0] // kv_heads

    @pl.loop(0, wkv_ref.shape[0] // span)
    def _(i):
        wide_raw[...] = raw[pl.ds(pl.multiple_of(i * span * kv_heads, 256), span * kv_heads), :].astype(f32)
        for g in range(kv_heads):
            wkv_ref[pl.ds(pl.multiple_of(i * span, 256), span), g * 128 : (g + 1) * 128] = (
                wide_raw[pl.ds(g, span, stride=kv_heads), :].astype(bf16)
            )

    loads[1].wait()

    @pl.loop(0, tok // 256)
    def _(i):
        r = pl.ds(pl.multiple_of(i * 256, 256), 256)
        ro = pl.ds(pl.multiple_of(i * 256 + MARGIN, 256), 256)
        kvx[ro, :] = jnp.dot(x_ref[r, :], wkv_ref[...], preferred_element_type=f32).astype(bf16)

    before, after = pl.ds(0, MARGIN), pl.ds(MARGIN + tok, MARGIN)
    kv_left = remote(kvx.at[pl.ds(MARGIN, MARGIN)], kvx.at[after], ks.at[0], kr.at[0], seq_dev(me - 1))
    kv_right = remote(kvx.at[pl.ds(tok, MARGIN)], kvx.at[before], ks.at[1], kr.at[1], seq_dev(me + 1))
    pl.when(has_left)(kv_left.start)
    pl.when(has_right)(kv_right.start)

    for kb in range(blocks + 4):
        row = me * blocks + kb - 2
        inside = (row >= 0) & (row < n * blocks)
        docs = seg_ref[pl.ds(jnp.clip(row, 0, n * blocks - 1), 1), :]
        docs = jnp.where(inside, docs, -1)
        kdocs[kb] = jnp.transpose(jnp.broadcast_to(docs, (BLOCK, BLOCK)))

    @pl.loop(0, blocks)
    def _(b):
        qdoc = seg_ref[pl.ds(me * blocks + b, 1), :]
        for o in range(5):
            same = kdocs[b + o] == qdoc
            if o != 2:
                same = same & (band_ref[b, o if o < 2 else o - 1] == 1)
            bias[b, o * BLOCK : (o + 1) * BLOCK, :] = jnp.where(same, 0.0, -1e30).astype(f32)

    grad[...] = jnp.zeros_like(grad)
    loads[2].wait()

    @pl.loop(0, tok // 256)
    def _(i):
        r = pl.ds(pl.multiple_of(i * 256, 256), 256)
        q_ref[r, :] = jnp.dot(x_ref[r, :], wq_ref[...], preferred_element_type=f32).astype(bf16)

    loads[3].wait()
    loads[4].wait()

    @pl.loop(0, tok // 256)
    def _(i):
        r = pl.ds(pl.multiple_of(i * 256, 256), 256)
        dc_ref[r, :] = lax.dot_general(
            oc_ref[r, :], wo_ref[...], NT, preferred_element_type=f32
        ).astype(bf16)

    @pl.when(jnp.logical_not(has_left))
    def _():
        kvx[before, :] = jnp.zeros((MARGIN, kvc), bf16)
        for g in range(kv_heads):
            hin[1, g] = jnp.zeros(hin.shape[2:], bf16)

    @pl.when(jnp.logical_not(has_right))
    def _():
        kvx[after, :] = jnp.zeros((MARGIN, kvc), bf16)
        for g in range(kv_heads):
            hin[0, g] = jnp.zeros(hin.shape[2:], bf16)

    pl.when(has_left)(kv_right.wait_recv)
    pl.when(has_right)(kv_left.wait_recv)

    halos = []
    for g in range(kv_heads):
        cols = slice(g * wide, (g + 1) * wide)
        kcols = slice(g * 2 * HEAD_DIM, (g + 1) * 2 * HEAD_DIM)

        @pl.loop(0, blocks)
        def _(b):
            first = pl.multiple_of(b * BLOCK, BLOCK)
            qt = side_by_side(jnp.transpose(q_ref[pl.ds(first, BLOCK), cols] * SCALE))
            dct = side_by_side(jnp.transpose(dc_ref[pl.ds(first, BLOCK), cols]))
            zero = jnp.zeros_like(qt)
            qz = jnp.concatenate([qt, zero], axis=0)
            dcz = jnp.concatenate([zero, dct], axis=0)
            kv = kvx[pl.ds(first, WINDOW), kcols]
            kvt = jnp.transpose(kv)
            s = jnp.dot(kv, qz, preferred_element_type=f32)
            s = s + jnp.concatenate([bias[b]] * GROUP, axis=1)
            p = jnp.exp(s - jnp.max(s, axis=0, keepdims=True))
            w = p * (1.0 / jnp.sum(p, axis=0, keepdims=True))
            wh = w.astype(bf16)
            ctx = jnp.dot(kvt[HEAD_DIM:], wh, preferred_element_type=f32).astype(bf16)
            delta = jnp.sum(dct.astype(f32) * ctx.astype(f32), axis=0, keepdims=True)
            dp = jnp.dot(kv, dcz, preferred_element_type=f32)
            ds = (w * (dp - delta)).astype(bf16)
            dq = jnp.dot(kvt[:HEAD_DIM], ds, preferred_element_type=f32) * SCALE
            ctx_ref[pl.ds(first, BLOCK), cols] = jnp.transpose(stacked(ctx))
            dq_ref[pl.ds(first, BLOCK), cols] = jnp.transpose(stacked(dq.astype(bf16)))
            d_kv = lax.dot_general(ds, qz, NT, preferred_element_type=f32)
            d_kv = d_kv + lax.dot_general(wh, dcz, NT, preferred_element_type=f32)
            grad[pl.ds(first, WINDOW), kcols] += d_kv

        halo[0, g] = grad[:MARGIN, kcols].astype(bf16)
        halo[1, g] = grad[MARGIN + tok :, kcols].astype(bf16)
        to_left = remote(halo.at[0, g], hin.at[0, g], hs.at[0, g], hr.at[0, g], seq_dev(me - 1))
        to_right = remote(halo.at[1, g], hin.at[1, g], hs.at[1, g], hr.at[1, g], seq_dev(me + 1))
        pl.when(has_left)(to_left.start)
        pl.when(has_right)(to_right.start)
        halos.append((to_left, to_right))

    leave = [pltpu.make_async_copy(ctx_ref, ctx_hbm, os.at[0])]
    leave[0].start()
    zero = jnp.zeros((tok - MARGIN, 2 * HEAD_DIM), f32)
    for g, (to_left, to_right) in enumerate(halos):
        kcols = slice(g * 2 * HEAD_DIM, (g + 1) * 2 * HEAD_DIM)
        pl.when(has_left)(to_right.wait_recv)
        pl.when(has_right)(to_left.wait_recv)
        dkv[:, kcols] = (
            grad[MARGIN : MARGIN + tok, kcols]
            + jnp.concatenate([hin[1, g].astype(f32), zero], axis=0)
            + jnp.concatenate([zero, hin[0, g].astype(f32)], axis=0)
        ).astype(bf16)

    def to_up(c):
        return remote(part.at[c], inb.at[c], rs.at[c], rr.at[c], mp_dev(z + 1))

    def to_down(c):
        slot = jnp.where(c == z - 1, m, c)
        return remote(part.at[c], inb.at[slot], rs.at[c], rr.at[slot], mp_dev(z - 1))

    low = z < m // 2

    @pl.loop(0, m)
    def _(t):
        c = jnp.where(low, m - 1 - t, t)
        rows = pl.ds(pl.multiple_of(c * ch, ch), ch)

        @pl.loop(0, tok // 256)
        def _(i):
            r = pl.ds(pl.multiple_of(i * 256, 256), 256)
            part[c, r, :] = (
                lax.dot_general(dq_ref[r, :], wq_ref[rows, :], NT, preferred_element_type=f32)
                + lax.dot_general(dkv[r, :], wkv_ref[rows, :], NT, preferred_element_type=f32)
            ).astype(bf16)

        @pl.when((z == 0) & (c > z))
        def _():
            to_up(c).start()

        @pl.when((z == m - 1) & (c < z))
        def _():
            to_down(c).start()

    def arrived(slot):
        remote(part.at[0], inb.at[slot], rs.at[0], rr.at[slot], mp_dev(z)).wait_recv()

    def add_in(c, slot):
        arrived(slot)

        @pl.loop(0, tok // 128)
        def _(i):
            r = pl.ds(pl.multiple_of(i * 128, 128), 128)
            part[c, r, :] = (part[c, r, :].astype(f32) + inb[slot, r, :].astype(f32)).astype(bf16)

    inner = (z > 0) & (z < m - 1)

    def up_step(c):
        @pl.when(inner & (c > z))
        def _():
            add_in(c, c)
            to_up(c).start()

    def down_step(c):
        @pl.when(inner & (c < z))
        def _():
            add_in(c, c)
            to_down(c).start()

    def chain_steps(first, last):
        @pl.when(low)
        def _():
            @pl.loop(first, last)
            def _(t):
                up_step(m - 1 - t)
                down_step(t)

        @pl.when(jnp.logical_not(low))
        def _():
            @pl.loop(first, last)
            def _(t):
                down_step(t)
                up_step(m - 1 - t)

    if sum_seq:
        pw = gt.shape[3]
        pr = pw * kv_heads
        dkvt = jnp.transpose(dkv[...])
        for k in range(2):
            half = (1 - core) if k == 0 else core

            @pl.loop(0, chips)
            def _(j):
                cols = pl.ds(pl.multiple_of((2 * j + half) * pw, pw), pw)
                prod = jnp.dot(dkvt, x_ref[:, cols], preferred_element_type=f32)
                if k == 0:
                    gt[0, j] = prod.astype(bf16)
                else:
                    gsum[j] = prod

            if k == 0:
                swap = remote(gt.at[0], sib, ss, sr, seq_dev(sibling))
                swap.start()
        swap.wait_recv()

        def other(k):
            return (chip + k) % chips

        sends = []
        for k in range(1, chips):
            j = other(k)
            gt[1, j] = (gsum[j] + sib[j].astype(f32)).astype(bf16)
            cp = remote(gt.at[1, j], quart.at[k], qs.at[k], qr.at[k], seq_dev(j * 2 + core))
            cp.start()
            sends.append(cp)
        mine[...] = gsum[chip] + sib[chip].astype(f32)
        swap.wait_send()

        @pl.when(low)
        def _():
            up_step(m - 1)

        @pl.when(jnp.logical_not(low))
        def _():
            down_step(0)

        for cp in sends:
            cp.wait_recv()
        for k in range(1, chips):
            mine[...] += quart[k].astype(f32)
        for cp in sends:
            cp.wait_send()
        done = jnp.transpose(mine[...])
        for g in range(kv_heads):
            kcols = slice(g * 2 * HEAD_DIM, (g + 1) * 2 * HEAD_DIM)
            mix[pl.ds(g, pw, stride=kv_heads), :] = done[:, kcols]
        piece[...] = mix[...].astype(bf16)
        sends = []
        for k in range(1, chips):
            cp = remote(piece, got.at[k], gs.at[k], gr.at[k], seq_dev(other(k) * 2 + core))
            cp.start()
            sends.append(cp)

        @pl.when(low)
        def _():
            down_step(0)

        @pl.when(jnp.logical_not(low))
        def _():
            up_step(m - 1)

        chain_steps(1, m)
        got[0] = piece[...]
        for cp in sends:
            cp.wait()
        swap = remote(got, sib2, fs, fr, seq_dev(sibling))
        swap.start()
        for k in range(chips):
            src = (chip + chips - k) % chips
            rows = pl.ds(pl.multiple_of((2 * src + core) * pr, pr), pr)
            leave.append(pltpu.make_async_copy(got.at[k], kvg_hbm.at[rows], os.at[1 + k]))
            leave[-1].start()
        swap.wait_recv()
        for k in range(chips):
            src = (chip + chips - k) % chips
            rows = pl.ds(pl.multiple_of((2 * src + 1 - core) * pr, pr), pr)
            leave.append(pltpu.make_async_copy(sib2.at[k], kvg_hbm.at[rows], os.at[1 + chips + k]))
            leave[-1].start()
        swap.wait_send()
    else:
        leave.append(pltpu.make_async_copy(dkv, kvg_hbm, os.at[1]))
        leave[1].start()
        chain_steps(0, m)

    @pl.when(has_down)
    def _():
        arrived(z)

    @pl.when(jnp.logical_not(has_down))
    def _():
        inb[0] = jnp.zeros(inb.shape[1:], bf16)

    @pl.when(has_up)
    def _():
        arrived(m)

    @pl.when(jnp.logical_not(has_up))
    def _():
        inb[m] = jnp.zeros(inb.shape[1:], bf16)

    @pl.loop(0, tok // 128)
    def _(i):
        r = pl.ds(pl.multiple_of(i * 128, 128), 128)
        ig_ref[r, :] = (
            part[z, r, :].astype(f32) + inb[z, r, :].astype(f32) + inb[m, r, :].astype(f32)
        ).astype(bf16)

    @pl.loop(0, m)
    def _(c):
        @pl.when(c > z)
        def _():
            to_up(c).wait_send()

        @pl.when(c < z)
        def _():
            to_down(c).wait_send()

    for cp in leave:
        cp.wait()
    pl.when(has_left)(kv_left.wait_send)
    pl.when(has_right)(kv_right.wait_send)
    for to_left, to_right in halos:
        pl.when(has_left)(to_left.wait_send)
        pl.when(has_right)(to_right.wait_send)


def relay_kernel(n, ag, x_hbm, oc_hbm, wq_hbm, wkv_hbm, wo_hbm, seg_ref, band_ref,
                 ctx_ref, ig_ref, kvg_ref, raw, wide_raw, x_ref, oc_ref, wall, wo_ref, q_ref, dc_ref,
                 kvx, kdocs, bias, grad, halo, hin, dall, wx, dout, dx, snd, rcv, tout, rin, part,
                 gt, gsum, sib, quart, got, mine, mix, piece, sib2,
                 ls, ks, kr, hs, hr, ss, sr, qs, qr, gs, gr, fs, fr,
                 zhs, zhr, zas, zar, pls, plr, pfs, pfr, pss, psr,
                 oqs, oqr, oks, okr, xqs, xqr, xks, xkr, rss, rsr, tos, tor, fas, far):
    tok, qc = q_ref.shape
    kvc = kvx.shape[1]
    ch = wall.shape[0] // 4
    blocks = tok // BLOCK
    kv_heads = kvc // (2 * HEAD_DIM)
    wide = GROUP * HEAD_DIM
    pair = 2 * HEAD_DIM
    held = ag * BLOCK
    me = lax.axis_index("seq")
    z = lax.axis_index("mp")
    core = me % 2
    sibling = me + 1 - 2 * core
    chip = me // 2
    chips = n // 2
    pr = ch // n
    outer = (z == 0) | (z == 3)
    inner = jnp.logical_not(outer)
    partner = jnp.where(outer, jnp.where(z == 0, 1, 2), jnp.where(z == 1, 0, 3))
    facing = 3 - z
    facing_partner = 3 - partner

    loads = [
        pltpu.make_async_copy(src, dst, ls.at[i])
        for i, (src, dst) in enumerate((
            (wkv_hbm, raw),
            (x_hbm, x_ref),
            (wq_hbm, wall.at[:, pl.ds(0, qc)]),
            (oc_hbm, oc_ref),
            (wo_hbm, wo_ref),
        ))
    ]
    for cp in loads:
        cp.start()

    def seq_dev(i):
        return (i, z)

    def mp_dev(i):
        return (me, i)

    barrier = pltpu.get_barrier_semaphore()
    has_left, has_right = me > 0, me < n - 1
    has_down, has_up = z > 0, z < 3

    def greet(dev):
        pl.semaphore_signal(barrier, inc=1, device_id=dev, device_id_type=MESH)

    for there, dev in (
        (has_left, seq_dev(me - 1)),
        (has_right, seq_dev(me + 1)),
        (has_down, mp_dev(z - 1)),
        (has_up, mp_dev(z + 1)),
    ):
        @pl.when(there)
        def _():
            greet(dev)
    for k in range(1, chips):
        greet(seq_dev(((chip + k) % chips) * 2 + core))
    peers = chips - 1
    for there in (has_left, has_right, has_down, has_up):
        peers = peers + there.astype(jnp.int32)
    pl.semaphore_wait(barrier, peers)

    def remote(src, dst, send, recv, dev):
        return pltpu.make_async_remote_copy(
            src_ref=src, dst_ref=dst, send_sem=send, recv_sem=recv, device_id=dev,
            device_id_type=MESH)

    qcols, kvcols = pl.ds(0, qc), pl.ds(qc, kvc)

    def rows_of(c):
        return pl.ds(pl.multiple_of(c * ch + me * pr, pr), pr)

    sent_chunks = (facing_partner, facing)
    zh = [[], []]
    for j, c in enumerate(sent_chunks):
        zh[0].append(remote(wq_hbm.at[rows_of(c), :], wx.at[j, chip, core, :, qcols], zhs.at[0, j], zhr.at[0, j], mp_dev(partner)))
        zh[1].append(remote(wall.at[rows_of(c), kvcols], wx.at[j, chip, core, :, kvcols], zhs.at[1, j], zhr.at[1, j], mp_dev(partner)))
    za = [[], [], []]
    if ag:
        za.append([])
        for j, c in enumerate((facing_partner, facing)):
            za[0].append(remote(wq_hbm.at[rows_of(c), :], wx.at[(2, 4)[j], chip, core, :, qcols], zas.at[0, j], zar.at[0, j], mp_dev(facing)))
            za[1].append(remote(wall.at[rows_of(c), kvcols], wx.at[(2, 4)[j], chip, core, :, kvcols], zas.at[1, j], zar.at[1, j], mp_dev(facing)))
            for i, cols in enumerate((qcols, kvcols)):
                za[2 + i].append(remote(
                    wx.at[1 - j, chip, core, :, cols], wx.at[(3, 5)[j], chip, core, :, cols],
                    zas.at[2 + i, j], zar.at[2 + i, j], mp_dev(facing)))

    def each(cps, what):
        for cp in cps:
            getattr(cp, what)()

    @pl.when(outer)
    def _():
        each(zh[0], "start")

    @pl.when(inner)
    def _():
        each(za[0], "start")

    xchip, ychip = chip + 1 - 2 * (chip % 2), (chip + 2) % chips
    dchip = (xchip + 2) % chips
    sets = ((0, 2), (2, 2), (4, 2))
    half = pr // 2
    to_x, to_y, via_x, via_y, to_sib = [], [], [], [], []
    for i, (first, count) in enumerate(sets):
        ksl = pl.ds(first, count)
        own = wx.at[ksl, chip, core]
        to_x.append(remote(own, own, pls.at[0, i], plr.at[0, i], seq_dev(xchip * 2 + core)))
        to_y.append(remote(own, own, pls.at[1, i], plr.at[1, i], seq_dev(ychip * 2 + core)))
        lo = wx.at[ksl, xchip, core, pl.ds(0, half)]
        hi = wx.at[ksl, ychip, core, pl.ds(half, half)]
        via_y.append(remote(lo, lo, pfs.at[0, i], pfr.at[0, i], seq_dev(ychip * 2 + core)))
        via_x.append(remote(hi, hi, pfs.at[1, i], pfr.at[1, i], seq_dev(xchip * 2 + core)))
        row = []
        for j, c in enumerate((chip, xchip, ychip, dchip)):
            block = wx.at[ksl, c, core]
            row.append(remote(block, block, pss.at[i, j], psr.at[i, j], seq_dev(sibling)))
        to_sib.append(row)

    def plane_start(i):
        to_x[i].start()
        to_y[i].start()
        to_sib[i][0].start()

    def plane_wait_x(i):
        first, count = sets[i]
        dst = wx.at[pl.ds(first, count), xchip, core]
        remote(dst, dst, pls.at[0, i], plr.at[0, i], seq_dev(sibling)).wait_recv()

    def plane_wait_y(i):
        first, count = sets[i]
        dst = wx.at[pl.ds(first, count), ychip, core]
        remote(dst, dst, pls.at[1, i], plr.at[1, i], seq_dev(sibling)).wait_recv()

    def plane_relay(i):
        plane_wait_x(i)
        via_y[i].start()
        to_sib[i][1].start()
        plane_wait_y(i)
        via_x[i].start()
        to_sib[i][2].start()

    def plane_pair(i):
        first, count = sets[i]
        for f, s in enumerate((pl.ds(0, half), pl.ds(half, half))):
            dst = wx.at[pl.ds(first, count), dchip, core, s]
            remote(dst, dst, pfs.at[f, i], pfr.at[f, i], seq_dev(sibling)).wait_recv()
        to_sib[i][3].start()

    def plane_done(i):
        first, count = sets[i]
        for j, c in enumerate((chip, xchip, ychip, dchip)):
            dst = wx.at[pl.ds(first, count), c, 1 - core]
            remote(dst, dst, pss.at[i, j], psr.at[i, j], seq_dev(sibling)).wait_recv()

    loads[0].wait()
    span = wide_raw.shape[0] // kv_heads

    @pl.loop(0, wall.shape[0] // span)
    def _(i):
        wide_raw[...] = raw[pl.ds(pl.multiple_of(i * span * kv_heads, 256), span * kv_heads), :].astype(f32)
        for g in range(kv_heads):
            wall[pl.ds(pl.multiple_of(i * span, 256), span), qc + g * 128 : qc + (g + 1) * 128] = (
                wide_raw[pl.ds(g, span, stride=kv_heads), :].astype(bf16)
            )

    @pl.when(outer)
    def _():
        each(zh[1], "start")

    @pl.when(inner)
    def _():
        each(za[1], "start")

    loads[1].wait()

    @pl.loop(0, tok // 256)
    def _(i):
        r = pl.ds(pl.multiple_of(i * 256, 256), 256)
        ro = pl.ds(pl.multiple_of(i * 256 + MARGIN, 256), 256)
        kvx[ro, :] = jnp.dot(x_ref[r, :], wall[:, qc:], preferred_element_type=f32).astype(bf16)

    before, after = pl.ds(0, MARGIN), pl.ds(MARGIN + tok, MARGIN)
    kv_left = remote(kvx.at[pl.ds(MARGIN, MARGIN)], kvx.at[after], ks.at[0], kr.at[0], seq_dev(me - 1))
    kv_right = remote(kvx.at[pl.ds(tok, MARGIN)], kvx.at[before], ks.at[1], kr.at[1], seq_dev(me + 1))
    pl.when(has_left)(kv_left.start)
    pl.when(has_right)(kv_right.start)

    for kb in range(blocks + 4):
        row = me * blocks + kb - 2
        inside = (row >= 0) & (row < n * blocks)
        docs = seg_ref[pl.ds(jnp.clip(row, 0, n * blocks - 1), 1), :]
        docs = jnp.where(inside, docs, -1)
        kdocs[kb] = jnp.transpose(jnp.broadcast_to(docs, (BLOCK, BLOCK)))

    @pl.loop(0, blocks)
    def _(b):
        qdoc = seg_ref[pl.ds(me * blocks + b, 1), :]
        for o in range(5):
            same = kdocs[b + o] == qdoc
            if o != 2:
                same = same & (band_ref[b, o if o < 2 else o - 1] == 1)
            bias[b, o * BLOCK : (o + 1) * BLOCK, :] = jnp.where(same, 0.0, -1e30).astype(f32)

    grad[...] = jnp.zeros_like(grad)
    loads[2].wait()

    @pl.when(inner)
    def _():
        each(zh[0], "wait_recv")
        each(za[2], "start")

    @pl.loop(0, tok // 256)
    def _(i):
        r = pl.ds(pl.multiple_of(i * 256, 256), 256)
        q_ref[r, :] = jnp.dot(x_ref[r, :], wall[:, :qc], preferred_element_type=f32).astype(bf16)

    @pl.when(inner)
    def _():
        each(zh[1], "wait_recv")
        each(za[3], "start")
        plane_start(0)

    loads[3].wait()
    loads[4].wait()

    @pl.loop(0, tok // 256)
    def _(i):
        r = pl.ds(pl.multiple_of(i * 256, 256), 256)
        dc_ref[r, :] = lax.dot_general(
            oc_ref[r, :], wo_ref[...], NT, preferred_element_type=f32
        ).astype(bf16)

    @pl.when(jnp.logical_not(has_left))
    def _():
        kvx[before, :] = jnp.zeros((MARGIN, kvc), bf16)
        for g in range(kv_heads):
            hin[1, g] = jnp.zeros(hin.shape[2:], bf16)

    @pl.when(jnp.logical_not(has_right))
    def _():
        kvx[after, :] = jnp.zeros((MARGIN, kvc), bf16)
        for g in range(kv_heads):
            hin[0, g] = jnp.zeros(hin.shape[2:], bf16)

    pl.when(has_left)(kv_right.wait_recv)
    pl.when(has_right)(kv_left.wait_recv)

    def block_rows(b):
        return pl.ds(pl.multiple_of(b * BLOCK, BLOCK), BLOCK)

    def dq_out(g, b):
        at = (block_rows(b), pl.ds(g * wide, wide))
        return remote(dall.at[at], dout.at[at], oqs.at[g, b], oqr.at[g, b], mp_dev(partner))

    def dq_across(which, g, b):
        at = (block_rows(b), pl.ds(g * wide, wide))
        src = dall.at[at] if which == 0 else dout.at[at]
        return remote(src, dx.at[(which,) + at], xqs.at[which, g, b], xqr.at[which, g, b], mp_dev(facing))

    def dkv_cols(g):
        return pl.ds(qc + g * pair, pair)

    def dkv_out(g, early):
        rows = pl.ds(0, held) if early else pl.ds(held, tok - held)
        at = (rows, dkv_cols(g))
        i = 1 if early else 0
        return remote(dall.at[at], dout.at[at], oks.at[g, i], okr.at[g, i], mp_dev(partner))

    def dkv_across(which, g):
        at = (pl.ds(0, held), dkv_cols(g))
        src = dall.at[at] if which == 0 else dout.at[at]
        return remote(src, dx.at[(which,) + at], xks.at[which, g], xkr.at[which, g], mp_dev(facing))

    def dkv_rest_across(g):
        at = (pl.ds(held, tok - held), dkv_cols(g))
        return remote(dout.at[at], dx.at[(1,) + at], xks.at[2, g], xkr.at[2, g], mp_dev(facing))

    def halo_left(g):
        return remote(halo.at[0, g], hin.at[0, g], hs.at[0, g], hr.at[0, g], seq_dev(me - 1))

    def halo_right(g):
        return remote(halo.at[1, g], hin.at[1, g], hs.at[1, g], hr.at[1, g], seq_dev(me + 1))

    def finish_late(g):
        pl.when(has_right)(halo_left(g).wait_recv)
        dall[held:, qc + g * pair : qc + (g + 1) * pair] = (
            grad[MARGIN + held : MARGIN + tok, g * pair : (g + 1) * pair] + hin[0, g].astype(f32)
        ).astype(bf16)
        pl.when(outer)(dkv_out(g, False).start)

    def finish_early(g):
        pl.when(has_left)(halo_right(g).wait_recv)
        dall[:held, qc + g * pair : qc + (g + 1) * pair] = (
            grad[MARGIN : MARGIN + held, g * pair : (g + 1) * pair] + hin[1, g].astype(f32)
        ).astype(bf16)
        pl.when(outer)(dkv_out(g, True).start)
        pl.when(inner)(dkv_across(0, g).start)

    for g in range(kv_heads):
        cols = slice(g * wide, (g + 1) * wide)
        kcols = slice(g * pair, (g + 1) * pair)

        def attend(b):
            first = pl.multiple_of(b * BLOCK, BLOCK)
            qt = side_by_side(jnp.transpose(q_ref[pl.ds(first, BLOCK), cols] * SCALE))
            dct = side_by_side(jnp.transpose(dc_ref[pl.ds(first, BLOCK), cols]))
            zero = jnp.zeros_like(qt)
            qz = jnp.concatenate([qt, zero], axis=0)
            dcz = jnp.concatenate([zero, dct], axis=0)
            kv = kvx[pl.ds(first, WINDOW), kcols]
            kvt = jnp.transpose(kv)
            s = jnp.dot(kv, qz, preferred_element_type=f32)
            s = s + jnp.concatenate([bias[b]] * GROUP, axis=1)
            p = jnp.exp(s - jnp.max(s, axis=0, keepdims=True))
            w = p * (1.0 / jnp.sum(p, axis=0, keepdims=True))
            wh = w.astype(bf16)
            ctx = jnp.dot(kvt[HEAD_DIM:], wh, preferred_element_type=f32).astype(bf16)
            delta = jnp.sum(dct.astype(f32) * ctx.astype(f32), axis=0, keepdims=True)
            dp = jnp.dot(kv, dcz, preferred_element_type=f32)
            ds = (w * (dp - delta)).astype(bf16)
            dq = jnp.dot(kvt[:HEAD_DIM], ds, preferred_element_type=f32) * SCALE
            ctx_ref[pl.ds(first, BLOCK), cols] = jnp.transpose(stacked(ctx))
            dall[pl.ds(first, BLOCK), cols] = jnp.transpose(stacked(dq.astype(bf16)))
            d_kv = lax.dot_general(ds, qz, NT, preferred_element_type=f32)
            d_kv = d_kv + lax.dot_general(wh, dcz, NT, preferred_element_type=f32)
            grad[pl.ds(first, WINDOW), kcols] += d_kv

        @pl.loop(0, blocks // 2)
        def _(pair_index):
            for b in (2 * pair_index, 2 * pair_index + 1):
                attend(b)

            first_pair = pair_index == 0

            @pl.when(outer)
            def _():
                for b in (2 * pair_index, 2 * pair_index + 1):
                    dq_out(g, b).start()

            @pl.when(first_pair)
            def _():
                halo[0, g] = grad[:MARGIN, kcols].astype(bf16)
                pl.when(has_left)(halo_left(g).start)

            @pl.when(inner & first_pair)
            def _():
                for b in range(2):
                    dq_across(0, g, b).start()
                if g == 0:
                    each(za[0] + za[1] + za[2] + za[3], "wait_recv")
                    plane_start(1)
                if g == 1:
                    plane_relay(1)

            @pl.when(inner & jnp.logical_not(first_pair))
            def _():
                for b in range(2):
                    dq_out(g, b).wait_recv()
                    dq_across(1, g, b).start()
                if g == 0:
                    plane_relay(0)
                if g == 1:
                    plane_pair(0)

            if g == 1:
                @pl.when(first_pair)
                def _():
                    finish_early(0)
                    finish_late(0)

        halo[1, g] = grad[MARGIN + tok :, kcols].astype(bf16)
        pl.when(has_right)(halo_right(g).start)

    def chunk(c):
        return pl.ds(pl.multiple_of(c * ch, ch), ch)

    def times_own(r, c):
        return lax.dot_general(dall[r, :], wall[chunk(c), :], NT, preferred_element_type=f32)

    def times_sent(d, k):
        return lax.dot_general(d, wx[k].reshape(ch, qc + kvc), NT, preferred_element_type=f32)

    summed = tok - held
    last = kv_heads - 1

    def sum_piece(slot, i):
        at = (slot, pl.ds(i * BLOCK, BLOCK))
        return remote(snd.at[at], rcv.at[at], rss.at[slot, i], rsr.at[slot, i], mp_dev(facing))

    def out_piece(i):
        at = block_rows(i)
        return remote(tout.at[at], rin.at[at], tos.at[i], tor.at[i], mp_dev(partner))

    early, late = slice(0, held), slice(held, tok)
    cut = qc + kvc - pair

    finish_late(1)

    @pl.when(inner)
    def _():
        dkv_out(0, True).wait_recv()
        dkv_across(1, 0).start()
        for j, c in enumerate((facing_partner, facing, partner, z)):
            part[j] = times_own(late, c)

    @pl.when(outer)
    def _():
        tout[late, :] = times_own(late, partner).astype(bf16)
        part[3] = times_own(late, z)

    finish_early(1)

    @pl.when(inner)
    def _():
        plane_start(2)
        plane_pair(1)
        part[4] = times_own(early, partner)
        part[5] = times_own(early, z)

    @pl.when(outer)
    def _():
        tout[early, :] = times_own(early, partner).astype(bf16)
        part[5] = times_own(early, z)
        dkv_out(last, False).wait_send()
        dkv_out(last, True).wait_send()
        for i in range(blocks):
            out_piece(i).start()

    pw = gt.shape[3]
    gr_rows = pw * kv_heads
    dkvt = jnp.transpose(dall[:, qc:])
    for k in range(2):
        own_half = (1 - core) if k == 0 else core

        @pl.loop(0, chips)
        def _(j):
            cols = pl.ds(pl.multiple_of((2 * j + own_half) * pw, pw), pw)
            prod = jnp.dot(dkvt, x_ref[:, cols], preferred_element_type=f32)
            if k == 0:
                gt[0, j] = prod.astype(bf16)
            else:
                gsum[j] = prod

        if k == 0:
            swap = remote(gt.at[0], sib, ss, sr, seq_dev(sibling))
            swap.start()

    def times_cut(d, k):
        return lax.dot_general(
            d, wx[k, :, :, :, :cut].reshape(ch, cut), NT, preferred_element_type=f32)

    def rest_on():
        src = dx.at[1, :, pl.ds(cut, pair)]
        return remote(src, src, fas.at[0], far.at[0], mp_dev(partner))

    def rest_rows_on():
        src = wx.at[3, :, :, :, pl.ds(cut, pair)]
        return remote(src, src, fas.at[1], far.at[1], mp_dev(partner))

    @pl.when(inner)
    def _():
        for g in range(last):
            dkv_out(g, False).wait_recv()
        plane_done(0)
        for b in range(ag, blocks):
            for g in range(kv_heads):
                dq_out(g, b).wait_recv()
            i = b - ag
            r = slice(b * BLOCK, (b + 1) * BLOCK)
            snd[1, i * BLOCK : (i + 1) * BLOCK, :] = (
                part[0, i * BLOCK : (i + 1) * BLOCK, :] + times_cut(dout[r, :cut], 1)
            ).astype(bf16)
            sum_piece(1, i).start()
        plane_done(1)
        rest_rows_on().start()
        for which in range(2):
            for g in range(kv_heads):
                for b in range(ag):
                    dq_across(which, g, b).wait_recv()
                if which == 0 or g < last:
                    dkv_across(which, g).wait_recv()
        tout[early, :] = (
            part[4] + times_sent(dx[0, early, :], 2) + times_cut(dx[1, early, :cut], 3)
        ).astype(bf16)
        for i in range(ag):
            out_piece(i).start()

    swap.wait_recv()

    def other(k):
        return (chip + k) % chips

    sends = []
    for k in range(1, chips):
        j = other(k)
        gt[1, j] = (gsum[j] + sib[j].astype(f32)).astype(bf16)
        cp = remote(gt.at[1, j], quart.at[k], qs.at[k], qr.at[k], seq_dev(j * 2 + core))
        cp.start()
        sends.append(cp)
    mine[...] = gsum[chip] + sib[chip].astype(f32)
    swap.wait_send()

    @pl.when(inner)
    def _():
        plane_relay(2)
        dkv_out(last, False).wait_recv()
        dkv_rest_across(last).start()
        dkv_out(last, True).wait_recv()
        dkv_across(1, last).start()
        snd[0] = (part[1] + times_sent(dout[late, :], 0)).astype(bf16)
        for i in range(blocks - ag):
            sum_piece(0, i).start()

    @pl.when(inner)
    def _():
        for i in range(summed // BLOCK):
            r = slice(held + i * BLOCK, held + (i + 1) * BLOCK)
            p = slice(i * BLOCK, (i + 1) * BLOCK)
            sum_piece(1, i).wait_recv()
            tout[r, :] = (part[2, p, :] + rcv[1, p, :].astype(f32)).astype(bf16)
            out_piece(ag + i).start()

    for cp in sends:
        cp.wait_recv()
    for k in range(1, chips):
        mine[...] += quart[k].astype(f32)
    for cp in sends:
        cp.wait_send()
    done = jnp.transpose(mine[...])
    for g in range(kv_heads):
        kcols = slice(g * pair, (g + 1) * pair)
        mix[pl.ds(g, pw, stride=kv_heads), :] = done[:, kcols]
    piece[...] = mix[...].astype(bf16)
    sends = []
    for k in range(1, chips):
        cp = remote(piece, got.at[k], gs.at[k], gr.at[k], seq_dev(other(k) * 2 + core))
        cp.start()
        sends.append(cp)

    @pl.when(inner)
    def _():
        dkv_across(1, last).wait_recv()
        dkv_rest_across(last).wait_recv()
        rest_on().start()
        plane_pair(2)
        plane_done(2)
        for i in range(ag):
            out_piece(i).wait_recv()
        ig_ref[early, :] = (
            part[5] + rin[early, :].astype(f32)
            + times_sent(dx[0, early, :], 4) + times_sent(dx[1, early, :], 5)
        ).astype(bf16)

    got[0] = piece[...]
    for cp in sends:
        cp.wait()
    swap = remote(got, sib2, fs, fr, seq_dev(sibling))
    swap.start()
    for k in range(chips):
        src = (chip + chips - k) % chips
        kvg_ref[pl.ds(pl.multiple_of((2 * src + core) * gr_rows, gr_rows), gr_rows), :] = got[k]
    swap.wait_recv()
    for k in range(chips):
        src = (chip + chips - k) % chips
        kvg_ref[pl.ds(pl.multiple_of((2 * src + 1 - core) * gr_rows, gr_rows), gr_rows), :] = sib2[k]
    swap.wait_send()

    @pl.when(inner)
    def _():
        for i in range(ag, blocks):
            out_piece(i).wait_recv()
        for i in range(summed // BLOCK):
            sum_piece(0, i).wait_recv()
        ig_ref[late, :] = (part[3] + rin[late, :].astype(f32) + rcv[0].astype(f32)).astype(bf16)

    @pl.when(outer)
    def _():
        rest_rows_on().wait_recv()
        for i in range(blocks):
            out_piece(i).wait_recv()
        rest_on().wait_recv()
        for r, mine_part in ((early, part[5]), (late, part[3])):
            far_part = lax.dot_general(
                dx[1, r, cut:], wx[3, :, :, :, cut:].reshape(ch, pair), NT, preferred_element_type=f32)
            ig_ref[r, :] = (mine_part + far_part + rin[r, :].astype(f32)).astype(bf16)

    @pl.when(outer)
    def _():
        for g in range(kv_heads):
            for b in range(blocks):
                dq_out(g, b).wait_send()
            if g < last:
                dkv_out(g, False).wait_send()
                dkv_out(g, True).wait_send()
        each(zh[0], "wait_send")
        each(zh[1], "wait_send")

    @pl.when(inner)
    def _():
        for which in range(2 if ag else 0):
            for g in range(kv_heads):
                for b in range(ag):
                    dq_across(which, g, b).wait_send()
                dkv_across(which, g).wait_send()
        dkv_rest_across(last).wait_send()
        rest_on().wait_send()
        rest_rows_on().wait_send()
        for slot in range(2):
            for i in range(blocks - ag):
                sum_piece(slot, i).wait_send()
        for group in za:
            each(group, "wait_send")
        for group in (to_x, to_y, via_x, via_y, *to_sib):
            each(group, "wait_send")

    for i in range(blocks):
        out_piece(i).wait_send()
    pl.when(has_left)(kv_left.wait_send)
    pl.when(has_right)(kv_right.wait_send)
    for g in range(kv_heads):
        pl.when(has_left)(halo_left(g).wait_send)
        pl.when(has_right)(halo_right(g).wait_send)


def write_kernel(ctx_hbm, ig_hbm, kvg_hbm, ctx_out, ig_out, kvg_out, half, full, ctx_mid, ig_mid, ins, outs):
    pieces, rows = half.shape[0], half.shape[1]
    loads, stores = [], []
    for i in range(pieces):
        loads.append(pltpu.make_async_copy(kvg_hbm.at[pl.ds(i * rows, rows)], half.at[i], ins.at[i]))
        stores.append(pltpu.make_async_copy(full.at[i], kvg_out.at[pl.ds(i * rows, rows)], outs.at[i]))
        loads[i].start()
    for i, (src, mid, dst) in enumerate(((ctx_hbm, ctx_mid, ctx_out), (ig_hbm, ig_mid, ig_out))):
        loads.append(pltpu.make_async_copy(src, mid, ins.at[pieces + i]))
        stores.append(pltpu.make_async_copy(mid, dst, outs.at[pieces + i]))
        loads[-1].start()
    for i in range(pieces):
        loads[i].wait()
        full[i] = half[i].astype(f32)
        stores[i].start()
    for i in range(pieces, pieces + 2):
        loads[i].wait()
        stores[i].start()
    for cp in stores:
        cp.wait()


def store_kernel(ctx_ref, ig_ref, kvg_ref, ctx_out, ig_out, kvg_out, full, outs):
    pieces, rows = full.shape[0], full.shape[1]
    stores = [
        pltpu.make_async_copy(ctx_ref, ctx_out, outs.at[pieces]),
        pltpu.make_async_copy(ig_ref, ig_out, outs.at[pieces + 1]),
    ]
    for cp in stores:
        cp.start()
    for i in range(pieces):
        full[i] = kvg_ref[i * rows : (i + 1) * rows, :].astype(f32)
        stores.append(pltpu.make_async_copy(full.at[i], kvg_out.at[pl.ds(i * rows, rows)], outs.at[i]))
        stores[-1].start()
    for cp in stores:
        cp.wait()


def stored(*arrays):
    pieces = 8
    rows, lanes = arrays[2].shape[0] // pieces, arrays[2].shape[1]
    return pl.pallas_call(
        store_kernel,
        out_shape=[
            jax.ShapeDtypeStruct(a.shape, t) for a, t in zip(arrays, (bf16, bf16, f32))
        ],
        in_specs=[VMEM] * 3,
        out_specs=[ANY] * 3,
        scratch_shapes=[
            pltpu.VMEM((pieces, rows, lanes), f32),
            pltpu.SemaphoreType.DMA((pieces + 2,)),
        ],
        compiler_params=pltpu.CompilerParams(vmem_limit_bytes=30 * 2**20),
        name="store",
    )(*arrays)


def written(*arrays):
    pieces = 4
    rows, lanes = arrays[2].shape[0] // pieces, arrays[2].shape[1]
    return pl.pallas_call(
        write_kernel,
        out_shape=[
            jax.ShapeDtypeStruct(a.shape, t) for a, t in zip(arrays, (bf16, bf16, f32))
        ],
        in_specs=[ANY] * 3,
        out_specs=[ANY] * 3,
        scratch_shapes=[
            pltpu.VMEM((pieces, rows, lanes), bf16),
            pltpu.VMEM((pieces, rows, lanes), f32),
            pltpu.VMEM(arrays[0].shape, bf16),
            pltpu.VMEM(arrays[1].shape, bf16),
            pltpu.SemaphoreType.DMA((pieces + 2,)),
            pltpu.SemaphoreType.DMA((pieces + 2,)),
        ],
        compiler_params=pltpu.CompilerParams(vmem_limit_bytes=60 * 2**20),
        name="write",
    )(*arrays)


def local(n, m, normed, out_cotangent, segments, band_mask, query_weight, key_value_weight, out_weight):
    tok, width = normed.shape
    qc = query_weight.shape[1]
    kv_heads = key_value_weight.shape[1]
    pair = 2 * HEAD_DIM
    kvc = kv_heads * pair
    wkv = key_value_weight.reshape(width * kv_heads, pair)
    blocks = tok // BLOCK
    ch = width // m
    pw = width // n
    sum_seq = n % 2 == 0 and n * 128 <= width and width % (n * 128) == 0
    chips = n // 2
    dma = pltpu.SemaphoreType.DMA
    vmem = pltpu.VMEM
    relay = n == 8 and m == 4 and kv_heads == 2 and tok == 4 * BLOCK and sum_seq
    scratch = [
        vmem((tok, qc), bf16),
        vmem((width * kv_heads, pair), bf16),
        vmem((256 * kv_heads, pair), f32),
        vmem((tok, width), bf16),
        vmem((tok, width), bf16),
        vmem((width, qc), bf16),
        vmem((width, kvc), bf16),
        vmem((qc, width), bf16),
        vmem((tok, qc), bf16),
        vmem((tok, qc), bf16),
        vmem((tok + 2 * MARGIN, kvc), bf16),
        vmem((blocks + 4, BLOCK, BLOCK), jnp.int32),
        vmem((blocks, WINDOW, BLOCK), f32),
        vmem((tok + 2 * MARGIN, kvc), f32),
        vmem((2, kv_heads, MARGIN, pair), bf16),
        vmem((2, kv_heads, MARGIN, pair), bf16),
        vmem((tok, qc), bf16),
        vmem((tok, kvc), bf16),
        vmem((m, tok, ch), bf16),
        vmem((m + 1, tok, ch), bf16),
        dma((5,)),
        dma((1 + n,)),
        dma((2,)),
        dma((2,)),
        dma((2, kv_heads)),
        dma((2, kv_heads)),
        dma((m,)),
        dma((m + 1,)),
    ]
    if sum_seq:
        kvg_shape = (width * kv_heads, pair)
        if not relay:
            scratch += [
                vmem((2, chips, kvc, pw), bf16),
                vmem((chips, kvc, pw), f32),
                vmem((chips, kvc, pw), bf16),
                vmem((chips, kvc, pw), bf16),
                vmem((chips, pw * kv_heads, pair), bf16),
                vmem((kvc, pw), f32),
                vmem((pw * kv_heads, pair), f32),
                vmem((pw * kv_heads, pair), bf16),
                vmem((chips, pw * kv_heads, pair), bf16),
                dma, dma, dma((chips,)), dma((chips,)), dma((chips,)), dma((chips,)), dma, dma,
            ]
    else:
        kvg_shape = (tok, kvc)
    ag = AHEAD
    held = ag * BLOCK
    relay_scratch = [
        vmem((width * kv_heads, pair), bf16),
        vmem((256 * kv_heads, pair), f32),
        vmem((tok, width), bf16),
        vmem((tok, width), bf16),
        vmem((width, qc + kvc), bf16),
        vmem((qc, width), bf16),
        vmem((tok, qc), bf16),
        vmem((tok, qc), bf16),
        vmem((tok + 2 * MARGIN, kvc), bf16),
        vmem((blocks + 4, BLOCK, BLOCK), jnp.int32),
        vmem((blocks, WINDOW, BLOCK), f32),
        vmem((tok + 2 * MARGIN, kvc), f32),
        vmem((2, kv_heads, MARGIN, pair), bf16),
        vmem((2, kv_heads, MARGIN, pair), bf16),
        vmem((tok, qc + kvc), bf16),
        vmem((6, max(chips, 1), 2, max(ch // n, 8), qc + kvc), bf16),
        vmem((tok, qc + kvc), bf16),
        vmem((2, tok, qc + kvc), bf16),
        vmem((2, max(tok - held, BLOCK), ch), bf16),
        vmem((2, max(tok - held, BLOCK), ch), bf16),
        vmem((tok, ch), bf16),
        vmem((tok, ch), bf16),
        vmem((6, MARGIN, ch), f32),
        vmem((2, chips, kvc, pw), bf16),
        vmem((chips, kvc, pw), f32),
        vmem((chips, kvc, pw), bf16),
        vmem((chips, kvc, pw), bf16),
        vmem((chips, pw * kv_heads, pair), bf16),
        vmem((kvc, pw), f32),
        vmem((pw * kv_heads, pair), f32),
        vmem((pw * kv_heads, pair), bf16),
        vmem((chips, pw * kv_heads, pair), bf16),
        dma((5,)),
        dma((2,)),
        dma((2,)),
        dma((2, kv_heads)),
        dma((2, kv_heads)),
        dma, dma, dma((chips,)), dma((chips,)), dma((chips,)), dma((chips,)), dma, dma,
        dma((2, 2)), dma((2, 2)),
        dma((4, 2)), dma((4, 2)),
        dma((2, 3)), dma((2, 3)),
        dma((2, 3)), dma((2, 3)),
        dma((3, 4)), dma((3, 4)),
        dma((kv_heads, blocks)), dma((kv_heads, blocks)),
        dma((kv_heads, 2)), dma((kv_heads, 2)),
        dma((2, kv_heads, ag)), dma((2, kv_heads, ag)),
        dma((3, kv_heads)), dma((3, kv_heads)),
        dma((2, blocks - ag)), dma((2, blocks - ag)),
        dma((blocks,)), dma((blocks,)),
        dma((2,)), dma((2,)),
    ]
    if relay:
        scratch = relay_scratch
        body = functools.partial(relay_kernel, n, ag)
        shapes = [vmem((tok, qc), bf16), vmem((tok, ch), bf16), vmem(kvg_shape, bf16)]
        out_specs = [VMEM] * 3
    else:
        body = functools.partial(fused_kernel, n, m, sum_seq)
        shapes = [
            jax.ShapeDtypeStruct((tok, qc), bf16),
            jax.ShapeDtypeStruct((tok, ch), bf16),
            jax.ShapeDtypeStruct(kvg_shape, bf16),
        ]
        out_specs = [ANY, VMEM, ANY]
    context, input_grad, other = pl.pallas_call(
        body,
        out_shape=shapes,
        in_specs=[ANY] * 5 + [VMEM, SMEM],
        out_specs=out_specs,
        scratch_shapes=scratch,
        compiler_params=pltpu.CompilerParams(
            vmem_limit_bytes=56 * 2**20, collective_id=0, has_side_effects=True
        ),
        name="fused",
    )(normed, out_cotangent, query_weight, wkv, out_weight, segments.reshape(-1, BLOCK), band_mask)
    if relay:
        context, input_grad, kv_grad = stored(context, input_grad, other)
    elif sum_seq:
        context, input_grad, kv_grad = written(context, input_grad, other)
    else:
        kv_grad = lax.dot_general(normed, other, (((0,), (0,)), ((), ())), preferred_element_type=f32)
        kv_grad = lax.psum(kv_grad, "seq")
    return context, input_grad, kv_grad.reshape(width, kv_heads, pair)


def solution(mesh):
    placed = (
        P("seq", None),
        P("seq", None),
        P(),
        P("seq", None),
        P(None, "mp"),
        P(None, "mp", None),
        P("mp", None),
    )
    return jax.shard_map(
        functools.partial(local, mesh.shape["seq"], mesh.shape["mp"]),
        mesh=mesh,
        in_specs=placed,
        out_specs=(P("seq", "mp"), P("seq", "mp"), P(None, "mp", None)),
        check_vma=False,
    )
```

```python
import functools

import jax
import jax.numpy as jnp
from jax import lax
from jax.experimental import pallas as pl
from jax.experimental.pallas import tpu as pltpu
from jax.sharding import PartitionSpec as P

QUERY_HEADS = 32
KEY_VALUE_HEADS = 8
GROUP = QUERY_HEADS // KEY_VALUE_HEADS
HEAD_DIM = 64
BLOCK = 128
MARGIN = 2 * BLOCK
WINDOW = BLOCK + 2 * MARGIN
SCALE = 0.125
AHEAD = 2

MESH = pl.DeviceIdType.MESH
NT = (((1,), (1,)), ((), ()))
f32 = jnp.float32
bf16 = jnp.bfloat16
ANY = pl.BlockSpec(memory_space=pl.ANY)
VMEM = pl.BlockSpec(memory_space=pltpu.VMEM)
SMEM = pl.BlockSpec(memory_space=pltpu.SMEM)


def side_by_side(x):
    return jnp.concatenate([x[h * HEAD_DIM : (h + 1) * HEAD_DIM] for h in range(GROUP)], axis=1)


def stacked(x):
    return jnp.concatenate([x[:, h * BLOCK : (h + 1) * BLOCK] for h in range(GROUP)], axis=0)


def fused_kernel(n, m, sum_seq, x_hbm, oc_hbm, wq_hbm, wkv_hbm, wo_hbm, seg_ref, band_ref,
                 ctx_hbm, ig_ref, kvg_hbm, ctx_ref, raw, wide_raw, x_ref, oc_ref, wq_ref, wkv_ref, wo_ref, q_ref, dc_ref,
                 kvx, kdocs, bias, grad, halo, hin, dq_ref, dkv, part, inb, ls, os, ks, kr, hs, hr, rs, rr,
                 *rest):
    if sum_seq:
        (gt, gsum, sib, quart, got, mine, mix, piece, sib2,
         ss, sr, qs, qr, gs, gr, fs, fr) = rest
    tok, kvc = dkv.shape
    blocks = tok // BLOCK
    kv_heads = kvc // (2 * HEAD_DIM)
    wide = GROUP * HEAD_DIM
    loads = [
        pltpu.make_async_copy(src, dst, ls.at[i])
        for i, (src, dst) in enumerate(
            ((wkv_hbm, raw), (x_hbm, x_ref), (wq_hbm, wq_ref), (oc_hbm, oc_ref), (wo_hbm, wo_ref))
        )
    ]
    for cp in loads:
        cp.start()
    ch = part.shape[2]
    me = lax.axis_index("seq")
    z = lax.axis_index("mp")
    core = me % 2
    sibling = me + 1 - 2 * core
    chip = me // 2
    chips = n // 2

    def seq_dev(i):
        return (i, z)

    def mp_dev(i):
        return (me, i)

    barrier = pltpu.get_barrier_semaphore()
    has_left, has_right = me > 0, me < n - 1
    has_down, has_up = z > 0, z < m - 1

    def greet(dev):
        pl.semaphore_signal(barrier, inc=1, device_id=dev, device_id_type=MESH)

    for there, dev in (
        (has_left, seq_dev(me - 1)),
        (has_right, seq_dev(me + 1)),
        (has_down, mp_dev(z - 1)),
        (has_up, mp_dev(z + 1)),
    ):
        @pl.when(there)
        def _():
            greet(dev)
    if sum_seq:
        for k in range(1, chips):
            greet(seq_dev(((chip + k) % chips) * 2 + core))
    peers = chips - 1 if sum_seq else 0
    for there in (has_left, has_right, has_down, has_up):
        peers = peers + there.astype(jnp.int32)
    pl.semaphore_wait(barrier, peers)

    def remote(src, dst, send, recv, dev):
        return pltpu.make_async_remote_copy(
            src_ref=src, dst_ref=dst, send_sem=send, recv_sem=recv, device_id=dev,
            device_id_type=MESH)

    loads[0].wait()
    span = wide_raw.shape[0] // kv_heads

    @pl.loop(0, wkv_ref.shape[0] // span)
    def _(i):
        wide_raw[...] = raw[pl.ds(pl.multiple_of(i * span * kv_heads, 256), span * kv_heads), :].astype(f32)
        for g in range(kv_heads):
            wkv_ref[pl.ds(pl.multiple_of(i * span, 256), span), g * 128 : (g + 1) * 128] = (
                wide_raw[pl.ds(g, span, stride=kv_heads), :].astype(bf16)
            )

    loads[1].wait()

    @pl.loop(0, tok // 256)
    def _(i):
        r = pl.ds(pl.multiple_of(i * 256, 256), 256)
        ro = pl.ds(pl.multiple_of(i * 256 + MARGIN, 256), 256)
        kvx[ro, :] = jnp.dot(x_ref[r, :], wkv_ref[...], preferred_element_type=f32).astype(bf16)

    before, after = pl.ds(0, MARGIN), pl.ds(MARGIN + tok, MARGIN)
    kv_left = remote(kvx.at[pl.ds(MARGIN, MARGIN)], kvx.at[after], ks.at[0], kr.at[0], seq_dev(me - 1))
    kv_right = remote(kvx.at[pl.ds(tok, MARGIN)], kvx.at[before], ks.at[1], kr.at[1], seq_dev(me + 1))
    pl.when(has_left)(kv_left.start)
    pl.when(has_right)(kv_right.start)

    for kb in range(blocks + 4):
        row = me * blocks + kb - 2
        inside = (row >= 0) & (row < n * blocks)
        docs = seg_ref[pl.ds(jnp.clip(row, 0, n * blocks - 1), 1), :]
        docs = jnp.where(inside, docs, -1)
        kdocs[kb] = jnp.transpose(jnp.broadcast_to(docs, (BLOCK, BLOCK)))

    @pl.loop(0, blocks)
    def _(b):
        qdoc = seg_ref[pl.ds(me * blocks + b, 1), :]
        for o in range(5):
            same = kdocs[b + o] == qdoc
            if o != 2:
                same = same & (band_ref[b, o if o < 2 else o - 1] == 1)
            bias[b, o * BLOCK : (o + 1) * BLOCK, :] = jnp.where(same, 0.0, -1e30).astype(f32)

    grad[...] = jnp.zeros_like(grad)
    loads[2].wait()

    @pl.loop(0, tok // 256)
    def _(i):
        r = pl.ds(pl.multiple_of(i * 256, 256), 256)
        q_ref[r, :] = jnp.dot(x_ref[r, :], wq_ref[...], preferred_element_type=f32).astype(bf16)

    loads[3].wait()
    loads[4].wait()

    @pl.loop(0, tok // 256)
    def _(i):
        r = pl.ds(pl.multiple_of(i * 256, 256), 256)
        dc_ref[r, :] = lax.dot_general(
            oc_ref[r, :], wo_ref[...], NT, preferred_element_type=f32
        ).astype(bf16)

    @pl.when(jnp.logical_not(has_left))
    def _():
        kvx[before, :] = jnp.zeros((MARGIN, kvc), bf16)
        for g in range(kv_heads):
            hin[1, g] = jnp.zeros(hin.shape[2:], bf16)

    @pl.when(jnp.logical_not(has_right))
    def _():
        kvx[after, :] = jnp.zeros((MARGIN, kvc), bf16)
        for g in range(kv_heads):
            hin[0, g] = jnp.zeros(hin.shape[2:], bf16)

    pl.when(has_left)(kv_right.wait_recv)
    pl.when(has_right)(kv_left.wait_recv)

    halos = []
    for g in range(kv_heads):
        cols = slice(g * wide, (g + 1) * wide)
        kcols = slice(g * 2 * HEAD_DIM, (g + 1) * 2 * HEAD_DIM)

        @pl.loop(0, blocks)
        def _(b):
            first = pl.multiple_of(b * BLOCK, BLOCK)
            qt = side_by_side(jnp.transpose(q_ref[pl.ds(first, BLOCK), cols] * SCALE))
            dct = side_by_side(jnp.transpose(dc_ref[pl.ds(first, BLOCK), cols]))
            zero = jnp.zeros_like(qt)
            qz = jnp.concatenate([qt, zero], axis=0)
            dcz = jnp.concatenate([zero, dct], axis=0)
            kv = kvx[pl.ds(first, WINDOW), kcols]
            kvt = jnp.transpose(kv)
            s = jnp.dot(kv, qz, preferred_element_type=f32)
            s = s + jnp.concatenate([bias[b]] * GROUP, axis=1)
            p = jnp.exp(s - jnp.max(s, axis=0, keepdims=True))
            w = p * (1.0 / jnp.sum(p, axis=0, keepdims=True))
            wh = w.astype(bf16)
            ctx = jnp.dot(kvt[HEAD_DIM:], wh, preferred_element_type=f32).astype(bf16)
            delta = jnp.sum(dct.astype(f32) * ctx.astype(f32), axis=0, keepdims=True)
            dp = jnp.dot(kv, dcz, preferred_element_type=f32)
            ds = (w * (dp - delta)).astype(bf16)
            dq = jnp.dot(kvt[:HEAD_DIM], ds, preferred_element_type=f32) * SCALE
            ctx_ref[pl.ds(first, BLOCK), cols] = jnp.transpose(stacked(ctx))
            dq_ref[pl.ds(first, BLOCK), cols] = jnp.transpose(stacked(dq.astype(bf16)))
            d_kv = lax.dot_general(ds, qz, NT, preferred_element_type=f32)
            d_kv = d_kv + lax.dot_general(wh, dcz, NT, preferred_element_type=f32)
            grad[pl.ds(first, WINDOW), kcols] += d_kv

        halo[0, g] = grad[:MARGIN, kcols].astype(bf16)
        halo[1, g] = grad[MARGIN + tok :, kcols].astype(bf16)
        to_left = remote(halo.at[0, g], hin.at[0, g], hs.at[0, g], hr.at[0, g], seq_dev(me - 1))
        to_right = remote(halo.at[1, g], hin.at[1, g], hs.at[1, g], hr.at[1, g], seq_dev(me + 1))
        pl.when(has_left)(to_left.start)
        pl.when(has_right)(to_right.start)
        halos.append((to_left, to_right))

    leave = [pltpu.make_async_copy(ctx_ref, ctx_hbm, os.at[0])]
    leave[0].start()
    zero = jnp.zeros((tok - MARGIN, 2 * HEAD_DIM), f32)
    for g, (to_left, to_right) in enumerate(halos):
        kcols = slice(g * 2 * HEAD_DIM, (g + 1) * 2 * HEAD_DIM)
        pl.when(has_left)(to_right.wait_recv)
        pl.when(has_right)(to_left.wait_recv)
        dkv[:, kcols] = (
            grad[MARGIN : MARGIN + tok, kcols]
            + jnp.concatenate([hin[1, g].astype(f32), zero], axis=0)
            + jnp.concatenate([zero, hin[0, g].astype(f32)], axis=0)
        ).astype(bf16)

    def to_up(c):
        return remote(part.at[c], inb.at[c], rs.at[c], rr.at[c], mp_dev(z + 1))

    def to_down(c):
        slot = jnp.where(c == z - 1, m, c)
        return remote(part.at[c], inb.at[slot], rs.at[c], rr.at[slot], mp_dev(z - 1))

    low = z < m // 2

    @pl.loop(0, m)
    def _(t):
        c = jnp.where(low, m - 1 - t, t)
        rows = pl.ds(pl.multiple_of(c * ch, ch), ch)

        @pl.loop(0, tok // 256)
        def _(i):
            r = pl.ds(pl.multiple_of(i * 256, 256), 256)
            part[c, r, :] = (
                lax.dot_general(dq_ref[r, :], wq_ref[rows, :], NT, preferred_element_type=f32)
                + lax.dot_general(dkv[r, :], wkv_ref[rows, :], NT, preferred_element_type=f32)
            ).astype(bf16)

        @pl.when((z == 0) & (c > z))
        def _():
            to_up(c).start()

        @pl.when((z == m - 1) & (c < z))
        def _():
            to_down(c).start()

    def arrived(slot):
        remote(part.at[0], inb.at[slot], rs.at[0], rr.at[slot], mp_dev(z)).wait_recv()

    def add_in(c, slot):
        arrived(slot)

        @pl.loop(0, tok // 128)
        def _(i):
            r = pl.ds(pl.multiple_of(i * 128, 128), 128)
            part[c, r, :] = (part[c, r, :].astype(f32) + inb[slot, r, :].astype(f32)).astype(bf16)

    inner = (z > 0) & (z < m - 1)

    def up_step(c):
        @pl.when(inner & (c > z))
        def _():
            add_in(c, c)
            to_up(c).start()

    def down_step(c):
        @pl.when(inner & (c < z))
        def _():
            add_in(c, c)
            to_down(c).start()

    def chain_steps(first, last):
        @pl.when(low)
        def _():
            @pl.loop(first, last)
            def _(t):
                up_step(m - 1 - t)
                down_step(t)

        @pl.when(jnp.logical_not(low))
        def _():
            @pl.loop(first, last)
            def _(t):
                down_step(t)
                up_step(m - 1 - t)

    if sum_seq:
        pw = gt.shape[3]
        pr = pw * kv_heads
        dkvt = jnp.transpose(dkv[...])
        for k in range(2):
            half = (1 - core) if k == 0 else core

            @pl.loop(0, chips)
            def _(j):
                cols = pl.ds(pl.multiple_of((2 * j + half) * pw, pw), pw)
                prod = jnp.dot(dkvt, x_ref[:, cols], preferred_element_type=f32)
                if k == 0:
                    gt[0, j] = prod.astype(bf16)
                else:
                    gsum[j] = prod

            if k == 0:
                swap = remote(gt.at[0], sib, ss, sr, seq_dev(sibling))
                swap.start()
        swap.wait_recv()

        def other(k):
            return (chip + k) % chips

        sends = []
        for k in range(1, chips):
            j = other(k)
            gt[1, j] = (gsum[j] + sib[j].astype(f32)).astype(bf16)
            cp = remote(gt.at[1, j], quart.at[k], qs.at[k], qr.at[k], seq_dev(j * 2 + core))
            cp.start()
            sends.append(cp)
        mine[...] = gsum[chip] + sib[chip].astype(f32)
        swap.wait_send()

        @pl.when(low)
        def _():
            up_step(m - 1)

        @pl.when(jnp.logical_not(low))
        def _():
            down_step(0)

        for cp in sends:
            cp.wait_recv()
        for k in range(1, chips):
            mine[...] += quart[k].astype(f32)
        for cp in sends:
            cp.wait_send()
        done = jnp.transpose(mine[...])
        for g in range(kv_heads):
            kcols = slice(g * 2 * HEAD_DIM, (g + 1) * 2 * HEAD_DIM)
            mix[pl.ds(g, pw, stride=kv_heads), :] = done[:, kcols]
        piece[...] = mix[...].astype(bf16)
        sends = []
        for k in range(1, chips):
            cp = remote(piece, got.at[k], gs.at[k], gr.at[k], seq_dev(other(k) * 2 + core))
            cp.start()
            sends.append(cp)

        @pl.when(low)
        def _():
            down_step(0)

        @pl.when(jnp.logical_not(low))
        def _():
            up_step(m - 1)

        chain_steps(1, m)
        got[0] = piece[...]
        for cp in sends:
            cp.wait()
        swap = remote(got, sib2, fs, fr, seq_dev(sibling))
        swap.start()
        for k in range(chips):
            src = (chip + chips - k) % chips
            rows = pl.ds(pl.multiple_of((2 * src + core) * pr, pr), pr)
            leave.append(pltpu.make_async_copy(got.at[k], kvg_hbm.at[rows], os.at[1 + k]))
            leave[-1].start()
        swap.wait_recv()
        for k in range(chips):
            src = (chip + chips - k) % chips
            rows = pl.ds(pl.multiple_of((2 * src + 1 - core) * pr, pr), pr)
            leave.append(pltpu.make_async_copy(sib2.at[k], kvg_hbm.at[rows], os.at[1 + chips + k]))
            leave[-1].start()
        swap.wait_send()
    else:
        leave.append(pltpu.make_async_copy(dkv, kvg_hbm, os.at[1]))
        leave[1].start()
        chain_steps(0, m)

    @pl.when(has_down)
    def _():
        arrived(z)

    @pl.when(jnp.logical_not(has_down))
    def _():
        inb[0] = jnp.zeros(inb.shape[1:], bf16)

    @pl.when(has_up)
    def _():
        arrived(m)

    @pl.when(jnp.logical_not(has_up))
    def _():
        inb[m] = jnp.zeros(inb.shape[1:], bf16)

    @pl.loop(0, tok // 128)
    def _(i):
        r = pl.ds(pl.multiple_of(i * 128, 128), 128)
        ig_ref[r, :] = (
            part[z, r, :].astype(f32) + inb[z, r, :].astype(f32) + inb[m, r, :].astype(f32)
        ).astype(bf16)

    @pl.loop(0, m)
    def _(c):
        @pl.when(c > z)
        def _():
            to_up(c).wait_send()

        @pl.when(c < z)
        def _():
            to_down(c).wait_send()

    for cp in leave:
        cp.wait()
    pl.when(has_left)(kv_left.wait_send)
    pl.when(has_right)(kv_right.wait_send)
    for to_left, to_right in halos:
        pl.when(has_left)(to_left.wait_send)
        pl.when(has_right)(to_right.wait_send)


def relay_kernel(n, ag, x_hbm, oc_hbm, wq_hbm, wkv_hbm, wo_hbm, seg_ref, band_ref,
                 ctx_ref, ig_ref, kvg_ref, raw, wide_raw, x_ref, oc_ref, wall, wo_ref, q_ref, dc_ref,
                 kvx, kdocs, bias, grad, halo, hin, dall, wx, dout, dx, snd, rcv, tout, rin, part,
                 gt, gsum, sib, quart, got, mine, mix, piece, sib2,
                 ls, ks, kr, hs, hr, ss, sr, qs, qr, gs, gr, fs, fr,
                 zhs, zhr, zas, zar, pls, plr, pfs, pfr, pss, psr,
                 oqs, oqr, oks, okr, xqs, xqr, xks, xkr, rss, rsr, tos, tor, fas, far):
    tok, qc = q_ref.shape
    kvc = kvx.shape[1]
    ch = wall.shape[0] // 4
    blocks = tok // BLOCK
    kv_heads = kvc // (2 * HEAD_DIM)
    wide = GROUP * HEAD_DIM
    pair = 2 * HEAD_DIM
    held = ag * BLOCK
    me = lax.axis_index("seq")
    z = lax.axis_index("mp")
    core = me % 2
    sibling = me + 1 - 2 * core
    chip = me // 2
    chips = n // 2
    pr = ch // n
    outer = (z == 0) | (z == 3)
    inner = jnp.logical_not(outer)
    partner = jnp.where(outer, jnp.where(z == 0, 1, 2), jnp.where(z == 1, 0, 3))
    facing = 3 - z
    facing_partner = 3 - partner

    loads = [
        pltpu.make_async_copy(src, dst, ls.at[i])
        for i, (src, dst) in enumerate((
            (wkv_hbm, raw),
            (x_hbm, x_ref),
            (wq_hbm, wall.at[:, pl.ds(0, qc)]),
            (oc_hbm, oc_ref),
            (wo_hbm, wo_ref),
        ))
    ]
    for cp in loads:
        cp.start()

    def seq_dev(i):
        return (i, z)

    def mp_dev(i):
        return (me, i)

    barrier = pltpu.get_barrier_semaphore()
    has_left, has_right = me > 0, me < n - 1
    has_down, has_up = z > 0, z < 3

    def greet(dev):
        pl.semaphore_signal(barrier, inc=1, device_id=dev, device_id_type=MESH)

    for there, dev in (
        (has_left, seq_dev(me - 1)),
        (has_right, seq_dev(me + 1)),
        (has_down, mp_dev(z - 1)),
        (has_up, mp_dev(z + 1)),
    ):
        @pl.when(there)
        def _():
            greet(dev)
    for k in range(1, chips):
        greet(seq_dev(((chip + k) % chips) * 2 + core))
    peers = chips - 1
    for there in (has_left, has_right, has_down, has_up):
        peers = peers + there.astype(jnp.int32)
    pl.semaphore_wait(barrier, peers)

    def remote(src, dst, send, recv, dev):
        return pltpu.make_async_remote_copy(
            src_ref=src, dst_ref=dst, send_sem=send, recv_sem=recv, device_id=dev,
            device_id_type=MESH)

    qcols, kvcols = pl.ds(0, qc), pl.ds(qc, kvc)

    def rows_of(c):
        return pl.ds(pl.multiple_of(c * ch + me * pr, pr), pr)

    sent_chunks = (facing_partner, facing)
    zh = [[], []]
    for j, c in enumerate(sent_chunks):
        zh[0].append(remote(wq_hbm.at[rows_of(c), :], wx.at[j, chip, core, :, qcols], zhs.at[0, j], zhr.at[0, j], mp_dev(partner)))
        zh[1].append(remote(wall.at[rows_of(c), kvcols], wx.at[j, chip, core, :, kvcols], zhs.at[1, j], zhr.at[1, j], mp_dev(partner)))
    za = [[], [], []]
    if ag:
        za.append([])
        for j, c in enumerate((facing_partner, facing)):
            za[0].append(remote(wq_hbm.at[rows_of(c), :], wx.at[(2, 4)[j], chip, core, :, qcols], zas.at[0, j], zar.at[0, j], mp_dev(facing)))
            za[1].append(remote(wall.at[rows_of(c), kvcols], wx.at[(2, 4)[j], chip, core, :, kvcols], zas.at[1, j], zar.at[1, j], mp_dev(facing)))
            for i, cols in enumerate((qcols, kvcols)):
                za[2 + i].append(remote(
                    wx.at[1 - j, chip, core, :, cols], wx.at[(3, 5)[j], chip, core, :, cols],
                    zas.at[2 + i, j], zar.at[2 + i, j], mp_dev(facing)))

    def each(cps, what):
        for cp in cps:
            getattr(cp, what)()

    @pl.when(outer)
    def _():
        each(zh[0], "start")

    @pl.when(inner)
    def _():
        each(za[0], "start")

    xchip, ychip = chip + 1 - 2 * (chip % 2), (chip + 2) % chips
    dchip = (xchip + 2) % chips
    sets = ((0, 2), (2, 2), (4, 2))
    half = pr // 2
    to_x, to_y, via_x, via_y, to_sib = [], [], [], [], []
    for i, (first, count) in enumerate(sets):
        ksl = pl.ds(first, count)
        own = wx.at[ksl, chip, core]
        to_x.append(remote(own, own, pls.at[0, i], plr.at[0, i], seq_dev(xchip * 2 + core)))
        to_y.append(remote(own, own, pls.at[1, i], plr.at[1, i], seq_dev(ychip * 2 + core)))
        lo = wx.at[ksl, xchip, core, pl.ds(0, half)]
        hi = wx.at[ksl, ychip, core, pl.ds(half, half)]
        via_y.append(remote(lo, lo, pfs.at[0, i], pfr.at[0, i], seq_dev(ychip * 2 + core)))
        via_x.append(remote(hi, hi, pfs.at[1, i], pfr.at[1, i], seq_dev(xchip * 2 + core)))
        row = []
        for j, c in enumerate((chip, xchip, ychip, dchip)):
            block = wx.at[ksl, c, core]
            row.append(remote(block, block, pss.at[i, j], psr.at[i, j], seq_dev(sibling)))
        to_sib.append(row)

    def plane_start(i):
        to_x[i].start()
        to_y[i].start()
        to_sib[i][0].start()

    def plane_wait_x(i):
        first, count = sets[i]
        dst = wx.at[pl.ds(first, count), xchip, core]
        remote(dst, dst, pls.at[0, i], plr.at[0, i], seq_dev(sibling)).wait_recv()

    def plane_wait_y(i):
        first, count = sets[i]
        dst = wx.at[pl.ds(first, count), ychip, core]
        remote(dst, dst, pls.at[1, i], plr.at[1, i], seq_dev(sibling)).wait_recv()

    def plane_relay(i):
        plane_wait_x(i)
        via_y[i].start()
        to_sib[i][1].start()
        plane_wait_y(i)
        via_x[i].start()
        to_sib[i][2].start()

    def plane_pair(i):
        first, count = sets[i]
        for f, s in enumerate((pl.ds(0, half), pl.ds(half, half))):
            dst = wx.at[pl.ds(first, count), dchip, core, s]
            remote(dst, dst, pfs.at[f, i], pfr.at[f, i], seq_dev(sibling)).wait_recv()
        to_sib[i][3].start()

    def plane_done(i):
        first, count = sets[i]
        for j, c in enumerate((chip, xchip, ychip, dchip)):
            dst = wx.at[pl.ds(first, count), c, 1 - core]
            remote(dst, dst, pss.at[i, j], psr.at[i, j], seq_dev(sibling)).wait_recv()

    loads[0].wait()
    span = wide_raw.shape[0] // kv_heads

    @pl.loop(0, wall.shape[0] // span)
    def _(i):
        wide_raw[...] = raw[pl.ds(pl.multiple_of(i * span * kv_heads, 256), span * kv_heads), :].astype(f32)
        for g in range(kv_heads):
            wall[pl.ds(pl.multiple_of(i * span, 256), span), qc + g * 128 : qc + (g + 1) * 128] = (
                wide_raw[pl.ds(g, span, stride=kv_heads), :].astype(bf16)
            )

    @pl.when(outer)
    def _():
        each(zh[1], "start")

    @pl.when(inner)
    def _():
        each(za[1], "start")

    loads[1].wait()

    @pl.loop(0, tok // 256)
    def _(i):
        r = pl.ds(pl.multiple_of(i * 256, 256), 256)
        ro = pl.ds(pl.multiple_of(i * 256 + MARGIN, 256), 256)
        kvx[ro, :] = jnp.dot(x_ref[r, :], wall[:, qc:], preferred_element_type=f32).astype(bf16)

    before, after = pl.ds(0, MARGIN), pl.ds(MARGIN + tok, MARGIN)
    kv_left = remote(kvx.at[pl.ds(MARGIN, MARGIN)], kvx.at[after], ks.at[0], kr.at[0], seq_dev(me - 1))
    kv_right = remote(kvx.at[pl.ds(tok, MARGIN)], kvx.at[before], ks.at[1], kr.at[1], seq_dev(me + 1))
    pl.when(has_left)(kv_left.start)
    pl.when(has_right)(kv_right.start)

    for kb in range(blocks + 4):
        row = me * blocks + kb - 2
        inside = (row >= 0) & (row < n * blocks)
        docs = seg_ref[pl.ds(jnp.clip(row, 0, n * blocks - 1), 1), :]
        docs = jnp.where(inside, docs, -1)
        kdocs[kb] = jnp.transpose(jnp.broadcast_to(docs, (BLOCK, BLOCK)))

    @pl.loop(0, blocks)
    def _(b):
        qdoc = seg_ref[pl.ds(me * blocks + b, 1), :]
        for o in range(5):
            same = kdocs[b + o] == qdoc
            if o != 2:
                same = same & (band_ref[b, o if o < 2 else o - 1] == 1)
            bias[b, o * BLOCK : (o + 1) * BLOCK, :] = jnp.where(same, 0.0, -1e30).astype(f32)

    grad[...] = jnp.zeros_like(grad)
    loads[2].wait()

    @pl.when(inner)
    def _():
        each(zh[0], "wait_recv")
        each(za[2], "start")

    @pl.loop(0, tok // 256)
    def _(i):
        r = pl.ds(pl.multiple_of(i * 256, 256), 256)
        q_ref[r, :] = jnp.dot(x_ref[r, :], wall[:, :qc], preferred_element_type=f32).astype(bf16)

    @pl.when(inner)
    def _():
        each(zh[1], "wait_recv")
        each(za[3], "start")
        plane_start(0)

    loads[3].wait()
    loads[4].wait()

    @pl.loop(0, tok // 256)
    def _(i):
        r = pl.ds(pl.multiple_of(i * 256, 256), 256)
        dc_ref[r, :] = lax.dot_general(
            oc_ref[r, :], wo_ref[...], NT, preferred_element_type=f32
        ).astype(bf16)

    @pl.when(jnp.logical_not(has_left))
    def _():
        kvx[before, :] = jnp.zeros((MARGIN, kvc), bf16)
        for g in range(kv_heads):
            hin[1, g] = jnp.zeros(hin.shape[2:], bf16)

    @pl.when(jnp.logical_not(has_right))
    def _():
        kvx[after, :] = jnp.zeros((MARGIN, kvc), bf16)
        for g in range(kv_heads):
            hin[0, g] = jnp.zeros(hin.shape[2:], bf16)

    pl.when(has_left)(kv_right.wait_recv)
    pl.when(has_right)(kv_left.wait_recv)

    def block_rows(b):
        return pl.ds(pl.multiple_of(b * BLOCK, BLOCK), BLOCK)

    def dq_out(g, b):
        at = (block_rows(b), pl.ds(g * wide, wide))
        return remote(dall.at[at], dout.at[at], oqs.at[g, b], oqr.at[g, b], mp_dev(partner))

    def dq_across(which, g, b):
        at = (block_rows(b), pl.ds(g * wide, wide))
        src = dall.at[at] if which == 0 else dout.at[at]
        return remote(src, dx.at[(which,) + at], xqs.at[which, g, b], xqr.at[which, g, b], mp_dev(facing))

    def dkv_cols(g):
        return pl.ds(qc + g * pair, pair)

    def dkv_out(g, early):
        rows = pl.ds(0, held) if early else pl.ds(held, tok - held)
        at = (rows, dkv_cols(g))
        i = 1 if early else 0
        return remote(dall.at[at], dout.at[at], oks.at[g, i], okr.at[g, i], mp_dev(partner))

    def dkv_across(which, g):
        at = (pl.ds(0, held), dkv_cols(g))
        src = dall.at[at] if which == 0 else dout.at[at]
        return remote(src, dx.at[(which,) + at], xks.at[which, g], xkr.at[which, g], mp_dev(facing))

    def dkv_rest_across(g):
        at = (pl.ds(held, BLOCK), dkv_cols(g))
        return remote(dout.at[at], dx.at[(1,) + at], xks.at[2, g], xkr.at[2, g], mp_dev(facing))

    def halo_left(g):
        return remote(halo.at[0, g], hin.at[0, g], hs.at[0, g], hr.at[0, g], seq_dev(me - 1))

    def halo_right(g):
        return remote(halo.at[1, g], hin.at[1, g], hs.at[1, g], hr.at[1, g], seq_dev(me + 1))

    def finish_late(g):
        pl.when(has_right)(halo_left(g).wait_recv)
        dall[held:, qc + g * pair : qc + (g + 1) * pair] = (
            grad[MARGIN + held : MARGIN + tok, g * pair : (g + 1) * pair] + hin[0, g].astype(f32)
        ).astype(bf16)
        pl.when(outer)(dkv_out(g, False).start)

    def finish_early(g):
        pl.when(has_left)(halo_right(g).wait_recv)
        dall[:held, qc + g * pair : qc + (g + 1) * pair] = (
            grad[MARGIN : MARGIN + held, g * pair : (g + 1) * pair] + hin[1, g].astype(f32)
        ).astype(bf16)
        pl.when(outer)(dkv_out(g, True).start)
        pl.when(inner)(dkv_across(0, g).start)

    for g in range(kv_heads):
        cols = slice(g * wide, (g + 1) * wide)
        kcols = slice(g * pair, (g + 1) * pair)

        def attend(b):
            first = pl.multiple_of(b * BLOCK, BLOCK)
            qt = side_by_side(jnp.transpose(q_ref[pl.ds(first, BLOCK), cols] * SCALE))
            dct = side_by_side(jnp.transpose(dc_ref[pl.ds(first, BLOCK), cols]))
            zero = jnp.zeros_like(qt)
            qz = jnp.concatenate([qt, zero], axis=0)
            dcz = jnp.concatenate([zero, dct], axis=0)
            kv = kvx[pl.ds(first, WINDOW), kcols]
            kvt = jnp.transpose(kv)
            s = jnp.dot(kv, qz, preferred_element_type=f32)
            s = s + jnp.concatenate([bias[b]] * GROUP, axis=1)
            p = jnp.exp(s - jnp.max(s, axis=0, keepdims=True))
            w = p * (1.0 / jnp.sum(p, axis=0, keepdims=True))
            wh = w.astype(bf16)
            ctx = jnp.dot(kvt[HEAD_DIM:], wh, preferred_element_type=f32).astype(bf16)
            delta = jnp.sum(dct.astype(f32) * ctx.astype(f32), axis=0, keepdims=True)
            dp = jnp.dot(kv, dcz, preferred_element_type=f32)
            ds = (w * (dp - delta)).astype(bf16)
            dq = jnp.dot(kvt[:HEAD_DIM], ds, preferred_element_type=f32) * SCALE
            ctx_ref[pl.ds(first, BLOCK), cols] = jnp.transpose(stacked(ctx))
            dall[pl.ds(first, BLOCK), cols] = jnp.transpose(stacked(dq.astype(bf16)))
            d_kv = lax.dot_general(ds, qz, NT, preferred_element_type=f32)
            d_kv = d_kv + lax.dot_general(wh, dcz, NT, preferred_element_type=f32)
            grad[pl.ds(first, WINDOW), kcols] += d_kv

        @pl.loop(0, blocks // 2)
        def _(pair_index):
            for b in (2 * pair_index, 2 * pair_index + 1):
                attend(b)

            first_pair = pair_index == 0

            @pl.when(outer)
            def _():
                for b in (2 * pair_index, 2 * pair_index + 1):
                    dq_out(g, b).start()

            @pl.when(first_pair)
            def _():
                halo[0, g] = grad[:MARGIN, kcols].astype(bf16)
                pl.when(has_left)(halo_left(g).start)

            @pl.when(inner & first_pair)
            def _():
                for b in range(2):
                    dq_across(0, g, b).start()
                if g == 0:
                    each(za[0] + za[1] + za[2] + za[3], "wait_recv")
                    plane_start(1)
                if g == 1:
                    plane_relay(1)

            @pl.when(inner & jnp.logical_not(first_pair))
            def _():
                for b in range(2):
                    dq_out(g, b).wait_recv()
                    dq_across(1, g, b).start()
                if g == 0:
                    plane_relay(0)
                if g == 1:
                    plane_pair(0)

            if g == 1:
                @pl.when(first_pair)
                def _():
                    finish_early(0)
                    finish_late(0)

        halo[1, g] = grad[MARGIN + tok :, kcols].astype(bf16)
        pl.when(has_right)(halo_right(g).start)

    def chunk(c):
        return pl.ds(pl.multiple_of(c * ch, ch), ch)

    def times_own(r, c):
        return lax.dot_general(dall[r, :], wall[chunk(c), :], NT, preferred_element_type=f32)

    def times_sent(d, k):
        return lax.dot_general(d, wx[k].reshape(ch, qc + kvc), NT, preferred_element_type=f32)

    summed = tok - held
    last = kv_heads - 1

    def sum_piece(slot, i):
        at = (slot, pl.ds(i * BLOCK, BLOCK))
        return remote(snd.at[at], rcv.at[at], rss.at[slot, i], rsr.at[slot, i], mp_dev(facing))

    def out_piece(i):
        at = block_rows(i)
        return remote(tout.at[at], rin.at[at], tos.at[i], tor.at[i], mp_dev(partner))

    early, late = slice(0, held), slice(held, tok)
    cut = qc + kvc - pair

    finish_late(1)

    @pl.when(inner)
    def _():
        dkv_out(0, True).wait_recv()
        dkv_across(1, 0).start()
        for j, c in enumerate((facing_partner, facing, partner, z)):
            part[j] = times_own(late, c)

    @pl.when(outer)
    def _():
        tout[late, :] = times_own(late, partner).astype(bf16)
        part[3] = times_own(late, z)

    finish_early(1)

    @pl.when(inner)
    def _():
        plane_start(2)
        plane_pair(1)
        part[4] = times_own(early, partner)
        part[5] = times_own(early, z)

    @pl.when(outer)
    def _():
        tout[early, :] = times_own(early, partner).astype(bf16)
        part[5] = times_own(early, z)
        dkv_out(last, False).wait_send()
        dkv_out(last, True).wait_send()
        for i in range(blocks):
            out_piece(i).start()

    pw = gt.shape[3]
    gr_rows = pw * kv_heads
    dkvt = jnp.transpose(dall[:, qc:])
    for k in range(2):
        own_half = (1 - core) if k == 0 else core

        @pl.loop(0, chips)
        def _(j):
            cols = pl.ds(pl.multiple_of((2 * j + own_half) * pw, pw), pw)
            prod = jnp.dot(dkvt, x_ref[:, cols], preferred_element_type=f32)
            if k == 0:
                gt[0, j] = prod.astype(bf16)
            else:
                gsum[j] = prod

        if k == 0:
            swap = remote(gt.at[0], sib, ss, sr, seq_dev(sibling))
            swap.start()

    swap.wait_recv()

    def other(k):
        return (chip + k) % chips

    sends = []
    for k in range(1, chips):
        j = other(k)
        gt[1, j] = (gsum[j] + sib[j].astype(f32)).astype(bf16)
        cp = remote(gt.at[1, j], quart.at[k], qs.at[k], qr.at[k], seq_dev(j * 2 + core))
        cp.start()
        sends.append(cp)
    mine[...] = gsum[chip] + sib[chip].astype(f32)
    swap.wait_send()

    def times_cut(d, k):
        return lax.dot_general(
            d, wx[k, :, :, :, :cut].reshape(ch, cut), NT, preferred_element_type=f32)

    def rest_on():
        src = dx.at[1, pl.ds(0, held + BLOCK), pl.ds(cut, pair)]
        return remote(src, src, fas.at[0], far.at[0], mp_dev(partner))

    def rest_rows_on():
        src = wx.at[3, :, :, :, pl.ds(cut, pair)]
        return remote(src, src, fas.at[1], far.at[1], mp_dev(partner))

    @pl.when(inner)
    def _():
        for g in range(last):
            dkv_out(g, False).wait_recv()
        plane_done(0)
        for b in range(ag, ag + 1):
            for g in range(kv_heads):
                dq_out(g, b).wait_recv()
            i = b - ag
            r = slice(b * BLOCK, (b + 1) * BLOCK)
            snd[1, i * BLOCK : (i + 1) * BLOCK, :] = (
                part[0, i * BLOCK : (i + 1) * BLOCK, :] + times_cut(dout[r, :cut], 1)
            ).astype(bf16)
            sum_piece(1, i).start()
        plane_done(1)
        rest_rows_on().start()
        for which in range(2):
            for g in range(kv_heads):
                for b in range(ag):
                    dq_across(which, g, b).wait_recv()
                if which == 0 or g < last:
                    dkv_across(which, g).wait_recv()
        tout[early, :] = (
            part[4] + times_sent(dx[0, early, :], 2) + times_cut(dx[1, early, :cut], 3)
        ).astype(bf16)
        for i in range(ag):
            out_piece(i).start()

    @pl.when(inner)
    def _():
        plane_relay(2)
        for b in range(ag + 1, blocks):
            for g in range(kv_heads):
                dq_out(g, b).wait_recv()
        dkv_out(last, False).wait_recv()
        for b in range(ag + 1, blocks):
            i = b - ag
            r = slice(b * BLOCK, (b + 1) * BLOCK)
            snd[1, i * BLOCK : (i + 1) * BLOCK, :] = (
                part[0, i * BLOCK : (i + 1) * BLOCK, :] + times_sent(dout[r, :], 1)
            ).astype(bf16)
            sum_piece(1, i).start()
        dkv_rest_across(last).start()
        dkv_out(last, True).wait_recv()
        dkv_across(1, last).start()
        snd[0] = (part[1] + times_sent(dout[late, :], 0)).astype(bf16)
        for i in range(blocks - ag):
            sum_piece(0, i).start()

    @pl.when(inner)
    def _():
        for i in range(summed // BLOCK):
            r = slice(held + i * BLOCK, held + (i + 1) * BLOCK)
            p = slice(i * BLOCK, (i + 1) * BLOCK)
            sum_piece(1, i).wait_recv()
            tout[r, :] = (part[2, p, :] + rcv[1, p, :].astype(f32)).astype(bf16)
            out_piece(ag + i).start()

    for cp in sends:
        cp.wait_recv()
    for k in range(1, chips):
        mine[...] += quart[k].astype(f32)
    for cp in sends:
        cp.wait_send()
    done = jnp.transpose(mine[...])
    for g in range(kv_heads):
        kcols = slice(g * pair, (g + 1) * pair)
        mix[pl.ds(g, pw, stride=kv_heads), :] = done[:, kcols]
    piece[...] = mix[...].astype(bf16)
    sends = []
    for k in range(1, chips):
        cp = remote(piece, got.at[k], gs.at[k], gr.at[k], seq_dev(other(k) * 2 + core))
        cp.start()
        sends.append(cp)

    @pl.when(inner)
    def _():
        dkv_across(1, last).wait_recv()
        dkv_rest_across(last).wait_recv()
        rest_on().start()
        plane_pair(2)
        plane_done(2)
        for i in range(ag):
            out_piece(i).wait_recv()
        ig_ref[early, :] = (
            part[5] + rin[early, :].astype(f32)
            + times_sent(dx[0, early, :], 4) + times_sent(dx[1, early, :], 5)
        ).astype(bf16)

    got[0] = piece[...]
    swaps = []
    for j in range(chips):
        if j:
            sends[j - 1].wait()
        swaps.append(remote(got.at[j], sib2.at[j], fs.at[j], fr.at[j], seq_dev(sibling)))
        swaps[-1].start()
        src = (chip + chips - j) % chips
        kvg_ref[pl.ds(pl.multiple_of((2 * src + core) * gr_rows, gr_rows), gr_rows), :] = got[j]
    for j in range(chips):
        swaps[j].wait_recv()
        src = (chip + chips - j) % chips
        kvg_ref[pl.ds(pl.multiple_of((2 * src + 1 - core) * gr_rows, gr_rows), gr_rows), :] = sib2[j]
    for cp in swaps:
        cp.wait_send()

    @pl.when(inner)
    def _():
        for i in range(ag, blocks):
            out_piece(i).wait_recv()
        for i in range(summed // BLOCK):
            sum_piece(0, i).wait_recv()
        ig_ref[late, :] = (part[3] + rin[late, :].astype(f32) + rcv[0].astype(f32)).astype(bf16)

    @pl.when(outer)
    def _():
        rest_rows_on().wait_recv()
        for i in range(blocks):
            out_piece(i).wait_recv()
        rest_on().wait_recv()
        tail = slice(held + BLOCK, tok)
        ig_ref[tail, :] = (part[3, BLOCK:, :] + rin[tail, :].astype(f32)).astype(bf16)
        for r, mine_part in ((early, part[5]), (slice(held, held + BLOCK), part[3, :BLOCK, :])):
            far_part = lax.dot_general(
                dx[1, r, cut:], wx[3, :, :, :, cut:].reshape(ch, pair), NT, preferred_element_type=f32)
            ig_ref[r, :] = (mine_part + far_part + rin[r, :].astype(f32)).astype(bf16)

    @pl.when(outer)
    def _():
        for g in range(kv_heads):
            for b in range(blocks):
                dq_out(g, b).wait_send()
            if g < last:
                dkv_out(g, False).wait_send()
                dkv_out(g, True).wait_send()
        each(zh[0], "wait_send")
        each(zh[1], "wait_send")

    @pl.when(inner)
    def _():
        for which in range(2 if ag else 0):
            for g in range(kv_heads):
                for b in range(ag):
                    dq_across(which, g, b).wait_send()
                dkv_across(which, g).wait_send()
        dkv_rest_across(last).wait_send()
        rest_on().wait_send()
        rest_rows_on().wait_send()
        for slot in range(2):
            for i in range(blocks - ag):
                sum_piece(slot, i).wait_send()
        for group in za:
            each(group, "wait_send")
        for group in (to_x, to_y, via_x, via_y, *to_sib):
            each(group, "wait_send")

    for i in range(blocks):
        out_piece(i).wait_send()
    pl.when(has_left)(kv_left.wait_send)
    pl.when(has_right)(kv_right.wait_send)
    for g in range(kv_heads):
        pl.when(has_left)(halo_left(g).wait_send)
        pl.when(has_right)(halo_right(g).wait_send)


def write_kernel(ctx_hbm, ig_hbm, kvg_hbm, ctx_out, ig_out, kvg_out, half, full, ctx_mid, ig_mid, ins, outs):
    pieces, rows = half.shape[0], half.shape[1]
    loads, stores = [], []
    for i in range(pieces):
        loads.append(pltpu.make_async_copy(kvg_hbm.at[pl.ds(i * rows, rows)], half.at[i], ins.at[i]))
        stores.append(pltpu.make_async_copy(full.at[i], kvg_out.at[pl.ds(i * rows, rows)], outs.at[i]))
        loads[i].start()
    for i, (src, mid, dst) in enumerate(((ctx_hbm, ctx_mid, ctx_out), (ig_hbm, ig_mid, ig_out))):
        loads.append(pltpu.make_async_copy(src, mid, ins.at[pieces + i]))
        stores.append(pltpu.make_async_copy(mid, dst, outs.at[pieces + i]))
        loads[-1].start()
    for i in range(pieces):
        loads[i].wait()
        full[i] = half[i].astype(f32)
        stores[i].start()
    for i in range(pieces, pieces + 2):
        loads[i].wait()
        stores[i].start()
    for cp in stores:
        cp.wait()


def store_kernel(ctx_ref, ig_ref, kvg_ref, ctx_out, ig_out, kvg_out, full, outs):
    pieces, rows = full.shape[0], full.shape[1]
    stores = [
        pltpu.make_async_copy(ctx_ref, ctx_out, outs.at[pieces]),
        pltpu.make_async_copy(ig_ref, ig_out, outs.at[pieces + 1]),
    ]
    for cp in stores:
        cp.start()
    for i in range(pieces):
        full[i] = kvg_ref[i * rows : (i + 1) * rows, :].astype(f32)
        stores.append(pltpu.make_async_copy(full.at[i], kvg_out.at[pl.ds(i * rows, rows)], outs.at[i]))
        stores[-1].start()
    for cp in stores:
        cp.wait()


def stored(*arrays):
    pieces = 8
    rows, lanes = arrays[2].shape[0] // pieces, arrays[2].shape[1]
    return pl.pallas_call(
        store_kernel,
        out_shape=[
            jax.ShapeDtypeStruct(a.shape, t) for a, t in zip(arrays, (bf16, bf16, f32))
        ],
        in_specs=[VMEM] * 3,
        out_specs=[ANY] * 3,
        scratch_shapes=[
            pltpu.VMEM((pieces, rows, lanes), f32),
            pltpu.SemaphoreType.DMA((pieces + 2,)),
        ],
        compiler_params=pltpu.CompilerParams(vmem_limit_bytes=30 * 2**20),
        name="store",
    )(*arrays)


def written(*arrays):
    pieces = 4
    rows, lanes = arrays[2].shape[0] // pieces, arrays[2].shape[1]
    return pl.pallas_call(
        write_kernel,
        out_shape=[
            jax.ShapeDtypeStruct(a.shape, t) for a, t in zip(arrays, (bf16, bf16, f32))
        ],
        in_specs=[ANY] * 3,
        out_specs=[ANY] * 3,
        scratch_shapes=[
            pltpu.VMEM((pieces, rows, lanes), bf16),
            pltpu.VMEM((pieces, rows, lanes), f32),
            pltpu.VMEM(arrays[0].shape, bf16),
            pltpu.VMEM(arrays[1].shape, bf16),
            pltpu.SemaphoreType.DMA((pieces + 2,)),
            pltpu.SemaphoreType.DMA((pieces + 2,)),
        ],
        compiler_params=pltpu.CompilerParams(vmem_limit_bytes=60 * 2**20),
        name="write",
    )(*arrays)


def local(n, m, normed, out_cotangent, segments, band_mask, query_weight, key_value_weight, out_weight):
    tok, width = normed.shape
    qc = query_weight.shape[1]
    kv_heads = key_value_weight.shape[1]
    pair = 2 * HEAD_DIM
    kvc = kv_heads * pair
    wkv = key_value_weight.reshape(width * kv_heads, pair)
    blocks = tok // BLOCK
    ch = width // m
    pw = width // n
    sum_seq = n % 2 == 0 and n * 128 <= width and width % (n * 128) == 0
    chips = n // 2
    dma = pltpu.SemaphoreType.DMA
    vmem = pltpu.VMEM
    relay = n == 8 and m == 4 and kv_heads == 2 and tok == 4 * BLOCK and sum_seq
    scratch = [
        vmem((tok, qc), bf16),
        vmem((width * kv_heads, pair), bf16),
        vmem((256 * kv_heads, pair), f32),
        vmem((tok, width), bf16),
        vmem((tok, width), bf16),
        vmem((width, qc), bf16),
        vmem((width, kvc), bf16),
        vmem((qc, width), bf16),
        vmem((tok, qc), bf16),
        vmem((tok, qc), bf16),
        vmem((tok + 2 * MARGIN, kvc), bf16),
        vmem((blocks + 4, BLOCK, BLOCK), jnp.int32),
        vmem((blocks, WINDOW, BLOCK), f32),
        vmem((tok + 2 * MARGIN, kvc), f32),
        vmem((2, kv_heads, MARGIN, pair), bf16),
        vmem((2, kv_heads, MARGIN, pair), bf16),
        vmem((tok, qc), bf16),
        vmem((tok, kvc), bf16),
        vmem((m, tok, ch), bf16),
        vmem((m + 1, tok, ch), bf16),
        dma((5,)),
        dma((1 + n,)),
        dma((2,)),
        dma((2,)),
        dma((2, kv_heads)),
        dma((2, kv_heads)),
        dma((m,)),
        dma((m + 1,)),
    ]
    if sum_seq:
        kvg_shape = (width * kv_heads, pair)
        if not relay:
            scratch += [
                vmem((2, chips, kvc, pw), bf16),
                vmem((chips, kvc, pw), f32),
                vmem((chips, kvc, pw), bf16),
                vmem((chips, kvc, pw), bf16),
                vmem((chips, pw * kv_heads, pair), bf16),
                vmem((kvc, pw), f32),
                vmem((pw * kv_heads, pair), f32),
                vmem((pw * kv_heads, pair), bf16),
                vmem((chips, pw * kv_heads, pair), bf16),
                dma, dma, dma((chips,)), dma((chips,)), dma((chips,)), dma((chips,)), dma, dma,
            ]
    else:
        kvg_shape = (tok, kvc)
    ag = AHEAD
    held = ag * BLOCK
    relay_scratch = [
        vmem((width * kv_heads, pair), bf16),
        vmem((256 * kv_heads, pair), f32),
        vmem((tok, width), bf16),
        vmem((tok, width), bf16),
        vmem((width, qc + kvc), bf16),
        vmem((qc, width), bf16),
        vmem((tok, qc), bf16),
        vmem((tok, qc), bf16),
        vmem((tok + 2 * MARGIN, kvc), bf16),
        vmem((blocks + 4, BLOCK, BLOCK), jnp.int32),
        vmem((blocks, WINDOW, BLOCK), f32),
        vmem((tok + 2 * MARGIN, kvc), f32),
        vmem((2, kv_heads, MARGIN, pair), bf16),
        vmem((2, kv_heads, MARGIN, pair), bf16),
        vmem((tok, qc + kvc), bf16),
        vmem((6, max(chips, 1), 2, max(ch // n, 8), qc + kvc), bf16),
        vmem((tok, qc + kvc), bf16),
        vmem((2, tok, qc + kvc), bf16),
        vmem((2, max(tok - held, BLOCK), ch), bf16),
        vmem((2, max(tok - held, BLOCK), ch), bf16),
        vmem((tok, ch), bf16),
        vmem((tok, ch), bf16),
        vmem((6, MARGIN, ch), f32),
        vmem((2, chips, kvc, pw), bf16),
        vmem((chips, kvc, pw), f32),
        vmem((chips, kvc, pw), bf16),
        vmem((chips, kvc, pw), bf16),
        vmem((chips, pw * kv_heads, pair), bf16),
        vmem((kvc, pw), f32),
        vmem((pw * kv_heads, pair), f32),
        vmem((pw * kv_heads, pair), bf16),
        vmem((chips, pw * kv_heads, pair), bf16),
        dma((5,)),
        dma((2,)),
        dma((2,)),
        dma((2, kv_heads)),
        dma((2, kv_heads)),
        dma, dma, dma((chips,)), dma((chips,)), dma((chips,)), dma((chips,)), dma((chips,)), dma((chips,)),
        dma((2, 2)), dma((2, 2)),
        dma((4, 2)), dma((4, 2)),
        dma((2, 3)), dma((2, 3)),
        dma((2, 3)), dma((2, 3)),
        dma((3, 4)), dma((3, 4)),
        dma((kv_heads, blocks)), dma((kv_heads, blocks)),
        dma((kv_heads, 2)), dma((kv_heads, 2)),
        dma((2, kv_heads, ag)), dma((2, kv_heads, ag)),
        dma((3, kv_heads)), dma((3, kv_heads)),
        dma((2, blocks - ag)), dma((2, blocks - ag)),
        dma((blocks,)), dma((blocks,)),
        dma((2,)), dma((2,)),
    ]
    if relay:
        scratch = relay_scratch
        body = functools.partial(relay_kernel, n, ag)
        shapes = [vmem((tok, qc), bf16), vmem((tok, ch), bf16), vmem(kvg_shape, bf16)]
        out_specs = [VMEM] * 3
    else:
        body = functools.partial(fused_kernel, n, m, sum_seq)
        shapes = [
            jax.ShapeDtypeStruct((tok, qc), bf16),
            jax.ShapeDtypeStruct((tok, ch), bf16),
            jax.ShapeDtypeStruct(kvg_shape, bf16),
        ]
        out_specs = [ANY, VMEM, ANY]
    context, input_grad, other = pl.pallas_call(
        body,
        out_shape=shapes,
        in_specs=[ANY] * 5 + [VMEM, SMEM],
        out_specs=out_specs,
        scratch_shapes=scratch,
        compiler_params=pltpu.CompilerParams(
            vmem_limit_bytes=56 * 2**20, collective_id=0, has_side_effects=True
        ),
        name="fused",
    )(normed, out_cotangent, query_weight, wkv, out_weight, segments.reshape(-1, BLOCK), band_mask)
    if relay:
        context, input_grad, kv_grad = stored(context, input_grad, other)
    elif sum_seq:
        context, input_grad, kv_grad = written(context, input_grad, other)
    else:
        kv_grad = lax.dot_general(normed, other, (((0,), (0,)), ((), ())), preferred_element_type=f32)
        kv_grad = lax.psum(kv_grad, "seq")
    return context, input_grad, kv_grad.reshape(width, kv_heads, pair)


def solution(mesh):
    placed = (
        P("seq", None),
        P("seq", None),
        P(),
        P("seq", None),
        P(None, "mp"),
        P(None, "mp", None),
        P("mp", None),
    )
    return jax.shard_map(
        functools.partial(local, mesh.shape["seq"], mesh.shape["mp"]),
        mesh=mesh,
        in_specs=placed,
        out_specs=(P("seq", "mp"), P("seq", "mp"), P(None, "mp", None)),
        check_vma=False,
    )
```

```python
import functools

import jax
import jax.numpy as jnp
from jax import lax
from jax.experimental import pallas as pl
from jax.experimental.pallas import tpu as pltpu
from jax.sharding import PartitionSpec as P

QUERY_HEADS = 32
KEY_VALUE_HEADS = 8
GROUP = QUERY_HEADS // KEY_VALUE_HEADS
HEAD_DIM = 64
BLOCK = 128
MARGIN = 2 * BLOCK
WINDOW = BLOCK + 2 * MARGIN
SCALE = 0.125
AHEAD = 2

MESH = pl.DeviceIdType.MESH
NT = (((1,), (1,)), ((), ()))
f32 = jnp.float32
bf16 = jnp.bfloat16
ANY = pl.BlockSpec(memory_space=pl.ANY)
VMEM = pl.BlockSpec(memory_space=pltpu.VMEM)
SMEM = pl.BlockSpec(memory_space=pltpu.SMEM)


def side_by_side(x):
    return jnp.concatenate([x[h * HEAD_DIM : (h + 1) * HEAD_DIM] for h in range(GROUP)], axis=1)


def stacked(x):
    return jnp.concatenate([x[:, h * BLOCK : (h + 1) * BLOCK] for h in range(GROUP)], axis=0)


def fused_kernel(n, m, sum_seq, x_hbm, oc_hbm, wq_hbm, wkv_hbm, wo_hbm, seg_ref, band_ref,
                 ctx_hbm, ig_ref, kvg_hbm, ctx_ref, raw, wide_raw, x_ref, oc_ref, wq_ref, wkv_ref, wo_ref, q_ref, dc_ref,
                 kvx, kdocs, bias, grad, halo, hin, dq_ref, dkv, part, inb, ls, os, ks, kr, hs, hr, rs, rr,
                 *rest):
    if sum_seq:
        (gt, gsum, sib, quart, got, mine, mix, piece, sib2,
         ss, sr, qs, qr, gs, gr, fs, fr) = rest
    tok, kvc = dkv.shape
    blocks = tok // BLOCK
    kv_heads = kvc // (2 * HEAD_DIM)
    wide = GROUP * HEAD_DIM
    loads = [
        pltpu.make_async_copy(src, dst, ls.at[i])
        for i, (src, dst) in enumerate(
            ((wkv_hbm, raw), (x_hbm, x_ref), (wq_hbm, wq_ref), (oc_hbm, oc_ref), (wo_hbm, wo_ref))
        )
    ]
    for cp in loads:
        cp.start()
    ch = part.shape[2]
    me = lax.axis_index("seq")
    z = lax.axis_index("mp")
    core = me % 2
    sibling = me + 1 - 2 * core
    chip = me // 2
    chips = n // 2

    def seq_dev(i):
        return (i, z)

    def mp_dev(i):
        return (me, i)

    barrier = pltpu.get_barrier_semaphore()
    has_left, has_right = me > 0, me < n - 1
    has_down, has_up = z > 0, z < m - 1

    def greet(dev):
        pl.semaphore_signal(barrier, inc=1, device_id=dev, device_id_type=MESH)

    for there, dev in (
        (has_left, seq_dev(me - 1)),
        (has_right, seq_dev(me + 1)),
        (has_down, mp_dev(z - 1)),
        (has_up, mp_dev(z + 1)),
    ):
        @pl.when(there)
        def _():
            greet(dev)
    if sum_seq:
        for k in range(1, chips):
            greet(seq_dev(((chip + k) % chips) * 2 + core))
    peers = chips - 1 if sum_seq else 0
    for there in (has_left, has_right, has_down, has_up):
        peers = peers + there.astype(jnp.int32)
    pl.semaphore_wait(barrier, peers)

    def remote(src, dst, send, recv, dev):
        return pltpu.make_async_remote_copy(
            src_ref=src, dst_ref=dst, send_sem=send, recv_sem=recv, device_id=dev,
            device_id_type=MESH)

    loads[0].wait()
    span = wide_raw.shape[0] // kv_heads

    @pl.loop(0, wkv_ref.shape[0] // span)
    def _(i):
        wide_raw[...] = raw[pl.ds(pl.multiple_of(i * span * kv_heads, 256), span * kv_heads), :].astype(f32)
        for g in range(kv_heads):
            wkv_ref[pl.ds(pl.multiple_of(i * span, 256), span), g * 128 : (g + 1) * 128] = (
                wide_raw[pl.ds(g, span, stride=kv_heads), :].astype(bf16)
            )

    loads[1].wait()

    @pl.loop(0, tok // 256)
    def _(i):
        r = pl.ds(pl.multiple_of(i * 256, 256), 256)
        ro = pl.ds(pl.multiple_of(i * 256 + MARGIN, 256), 256)
        kvx[ro, :] = jnp.dot(x_ref[r, :], wkv_ref[...], preferred_element_type=f32).astype(bf16)

    before, after = pl.ds(0, MARGIN), pl.ds(MARGIN + tok, MARGIN)
    kv_left = remote(kvx.at[pl.ds(MARGIN, MARGIN)], kvx.at[after], ks.at[0], kr.at[0], seq_dev(me - 1))
    kv_right = remote(kvx.at[pl.ds(tok, MARGIN)], kvx.at[before], ks.at[1], kr.at[1], seq_dev(me + 1))
    pl.when(has_left)(kv_left.start)
    pl.when(has_right)(kv_right.start)

    for kb in range(blocks + 4):
        row = me * blocks + kb - 2
        inside = (row >= 0) & (row < n * blocks)
        docs = seg_ref[pl.ds(jnp.clip(row, 0, n * blocks - 1), 1), :]
        docs = jnp.where(inside, docs, -1)
        kdocs[kb] = jnp.transpose(jnp.broadcast_to(docs, (BLOCK, BLOCK)))

    @pl.loop(0, blocks)
    def _(b):
        qdoc = seg_ref[pl.ds(me * blocks + b, 1), :]
        for o in range(5):
            same = kdocs[b + o] == qdoc
            if o != 2:
                same = same & (band_ref[b, o if o < 2 else o - 1] == 1)
            bias[b, o * BLOCK : (o + 1) * BLOCK, :] = jnp.where(same, 0.0, -1e30).astype(f32)

    grad[...] = jnp.zeros_like(grad)
    loads[2].wait()

    @pl.loop(0, tok // 256)
    def _(i):
        r = pl.ds(pl.multiple_of(i * 256, 256), 256)
        q_ref[r, :] = jnp.dot(x_ref[r, :], wq_ref[...], preferred_element_type=f32).astype(bf16)

    loads[3].wait()
    loads[4].wait()

    @pl.loop(0, tok // 256)
    def _(i):
        r = pl.ds(pl.multiple_of(i * 256, 256), 256)
        dc_ref[r, :] = lax.dot_general(
            oc_ref[r, :], wo_ref[...], NT, preferred_element_type=f32
        ).astype(bf16)

    @pl.when(jnp.logical_not(has_left))
    def _():
        kvx[before, :] = jnp.zeros((MARGIN, kvc), bf16)
        for g in range(kv_heads):
            hin[1, g] = jnp.zeros(hin.shape[2:], bf16)

    @pl.when(jnp.logical_not(has_right))
    def _():
        kvx[after, :] = jnp.zeros((MARGIN, kvc), bf16)
        for g in range(kv_heads):
            hin[0, g] = jnp.zeros(hin.shape[2:], bf16)

    pl.when(has_left)(kv_right.wait_recv)
    pl.when(has_right)(kv_left.wait_recv)

    halos = []
    for g in range(kv_heads):
        cols = slice(g * wide, (g + 1) * wide)
        kcols = slice(g * 2 * HEAD_DIM, (g + 1) * 2 * HEAD_DIM)

        @pl.loop(0, blocks)
        def _(b):
            first = pl.multiple_of(b * BLOCK, BLOCK)
            qt = side_by_side(jnp.transpose(q_ref[pl.ds(first, BLOCK), cols] * SCALE))
            dct = side_by_side(jnp.transpose(dc_ref[pl.ds(first, BLOCK), cols]))
            zero = jnp.zeros_like(qt)
            qz = jnp.concatenate([qt, zero], axis=0)
            dcz = jnp.concatenate([zero, dct], axis=0)
            kv = kvx[pl.ds(first, WINDOW), kcols]
            kvt = jnp.transpose(kv)
            s = jnp.dot(kv, qz, preferred_element_type=f32)
            s = s + jnp.concatenate([bias[b]] * GROUP, axis=1)
            p = jnp.exp(s - jnp.max(s, axis=0, keepdims=True))
            w = p * (1.0 / jnp.sum(p, axis=0, keepdims=True))
            wh = w.astype(bf16)
            ctx = jnp.dot(kvt[HEAD_DIM:], wh, preferred_element_type=f32).astype(bf16)
            delta = jnp.sum(dct.astype(f32) * ctx.astype(f32), axis=0, keepdims=True)
            dp = jnp.dot(kv, dcz, preferred_element_type=f32)
            ds = (w * (dp - delta)).astype(bf16)
            dq = jnp.dot(kvt[:HEAD_DIM], ds, preferred_element_type=f32) * SCALE
            ctx_ref[pl.ds(first, BLOCK), cols] = jnp.transpose(stacked(ctx))
            dq_ref[pl.ds(first, BLOCK), cols] = jnp.transpose(stacked(dq.astype(bf16)))
            d_kv = lax.dot_general(ds, qz, NT, preferred_element_type=f32)
            d_kv = d_kv + lax.dot_general(wh, dcz, NT, preferred_element_type=f32)
            grad[pl.ds(first, WINDOW), kcols] += d_kv

        halo[0, g] = grad[:MARGIN, kcols].astype(bf16)
        halo[1, g] = grad[MARGIN + tok :, kcols].astype(bf16)
        to_left = remote(halo.at[0, g], hin.at[0, g], hs.at[0, g], hr.at[0, g], seq_dev(me - 1))
        to_right = remote(halo.at[1, g], hin.at[1, g], hs.at[1, g], hr.at[1, g], seq_dev(me + 1))
        pl.when(has_left)(to_left.start)
        pl.when(has_right)(to_right.start)
        halos.append((to_left, to_right))

    leave = [pltpu.make_async_copy(ctx_ref, ctx_hbm, os.at[0])]
    leave[0].start()
    zero = jnp.zeros((tok - MARGIN, 2 * HEAD_DIM), f32)
    for g, (to_left, to_right) in enumerate(halos):
        kcols = slice(g * 2 * HEAD_DIM, (g + 1) * 2 * HEAD_DIM)
        pl.when(has_left)(to_right.wait_recv)
        pl.when(has_right)(to_left.wait_recv)
        dkv[:, kcols] = (
            grad[MARGIN : MARGIN + tok, kcols]
            + jnp.concatenate([hin[1, g].astype(f32), zero], axis=0)
            + jnp.concatenate([zero, hin[0, g].astype(f32)], axis=0)
        ).astype(bf16)

    def to_up(c):
        return remote(part.at[c], inb.at[c], rs.at[c], rr.at[c], mp_dev(z + 1))

    def to_down(c):
        slot = jnp.where(c == z - 1, m, c)
        return remote(part.at[c], inb.at[slot], rs.at[c], rr.at[slot], mp_dev(z - 1))

    low = z < m // 2

    @pl.loop(0, m)
    def _(t):
        c = jnp.where(low, m - 1 - t, t)
        rows = pl.ds(pl.multiple_of(c * ch, ch), ch)

        @pl.loop(0, tok // 256)
        def _(i):
            r = pl.ds(pl.multiple_of(i * 256, 256), 256)
            part[c, r, :] = (
                lax.dot_general(dq_ref[r, :], wq_ref[rows, :], NT, preferred_element_type=f32)
                + lax.dot_general(dkv[r, :], wkv_ref[rows, :], NT, preferred_element_type=f32)
            ).astype(bf16)

        @pl.when((z == 0) & (c > z))
        def _():
            to_up(c).start()

        @pl.when((z == m - 1) & (c < z))
        def _():
            to_down(c).start()

    def arrived(slot):
        remote(part.at[0], inb.at[slot], rs.at[0], rr.at[slot], mp_dev(z)).wait_recv()

    def add_in(c, slot):
        arrived(slot)

        @pl.loop(0, tok // 128)
        def _(i):
            r = pl.ds(pl.multiple_of(i * 128, 128), 128)
            part[c, r, :] = (part[c, r, :].astype(f32) + inb[slot, r, :].astype(f32)).astype(bf16)

    inner = (z > 0) & (z < m - 1)

    def up_step(c):
        @pl.when(inner & (c > z))
        def _():
            add_in(c, c)
            to_up(c).start()

    def down_step(c):
        @pl.when(inner & (c < z))
        def _():
            add_in(c, c)
            to_down(c).start()

    def chain_steps(first, last):
        @pl.when(low)
        def _():
            @pl.loop(first, last)
            def _(t):
                up_step(m - 1 - t)
                down_step(t)

        @pl.when(jnp.logical_not(low))
        def _():
            @pl.loop(first, last)
            def _(t):
                down_step(t)
                up_step(m - 1 - t)

    if sum_seq:
        pw = gt.shape[3]
        pr = pw * kv_heads
        dkvt = jnp.transpose(dkv[...])
        for k in range(2):
            half = (1 - core) if k == 0 else core

            @pl.loop(0, chips)
            def _(j):
                cols = pl.ds(pl.multiple_of((2 * j + half) * pw, pw), pw)
                prod = jnp.dot(dkvt, x_ref[:, cols], preferred_element_type=f32)
                if k == 0:
                    gt[0, j] = prod.astype(bf16)
                else:
                    gsum[j] = prod

            if k == 0:
                swap = remote(gt.at[0], sib, ss, sr, seq_dev(sibling))
                swap.start()
        swap.wait_recv()

        def other(k):
            return (chip + k) % chips

        sends = []
        for k in range(1, chips):
            j = other(k)
            gt[1, j] = (gsum[j] + sib[j].astype(f32)).astype(bf16)
            cp = remote(gt.at[1, j], quart.at[k], qs.at[k], qr.at[k], seq_dev(j * 2 + core))
            cp.start()
            sends.append(cp)
        mine[...] = gsum[chip] + sib[chip].astype(f32)
        swap.wait_send()

        @pl.when(low)
        def _():
            up_step(m - 1)

        @pl.when(jnp.logical_not(low))
        def _():
            down_step(0)

        for cp in sends:
            cp.wait_recv()
        for k in range(1, chips):
            mine[...] += quart[k].astype(f32)
        for cp in sends:
            cp.wait_send()
        done = jnp.transpose(mine[...])
        for g in range(kv_heads):
            kcols = slice(g * 2 * HEAD_DIM, (g + 1) * 2 * HEAD_DIM)
            mix[pl.ds(g, pw, stride=kv_heads), :] = done[:, kcols]
        piece[...] = mix[...].astype(bf16)
        sends = []
        for k in range(1, chips):
            cp = remote(piece, got.at[k], gs.at[k], gr.at[k], seq_dev(other(k) * 2 + core))
            cp.start()
            sends.append(cp)

        @pl.when(low)
        def _():
            down_step(0)

        @pl.when(jnp.logical_not(low))
        def _():
            up_step(m - 1)

        chain_steps(1, m)
        got[0] = piece[...]
        for cp in sends:
            cp.wait()
        swap = remote(got, sib2, fs, fr, seq_dev(sibling))
        swap.start()
        for k in range(chips):
            src = (chip + chips - k) % chips
            rows = pl.ds(pl.multiple_of((2 * src + core) * pr, pr), pr)
            leave.append(pltpu.make_async_copy(got.at[k], kvg_hbm.at[rows], os.at[1 + k]))
            leave[-1].start()
        swap.wait_recv()
        for k in range(chips):
            src = (chip + chips - k) % chips
            rows = pl.ds(pl.multiple_of((2 * src + 1 - core) * pr, pr), pr)
            leave.append(pltpu.make_async_copy(sib2.at[k], kvg_hbm.at[rows], os.at[1 + chips + k]))
            leave[-1].start()
        swap.wait_send()
    else:
        leave.append(pltpu.make_async_copy(dkv, kvg_hbm, os.at[1]))
        leave[1].start()
        chain_steps(0, m)

    @pl.when(has_down)
    def _():
        arrived(z)

    @pl.when(jnp.logical_not(has_down))
    def _():
        inb[0] = jnp.zeros(inb.shape[1:], bf16)

    @pl.when(has_up)
    def _():
        arrived(m)

    @pl.when(jnp.logical_not(has_up))
    def _():
        inb[m] = jnp.zeros(inb.shape[1:], bf16)

    @pl.loop(0, tok // 128)
    def _(i):
        r = pl.ds(pl.multiple_of(i * 128, 128), 128)
        ig_ref[r, :] = (
            part[z, r, :].astype(f32) + inb[z, r, :].astype(f32) + inb[m, r, :].astype(f32)
        ).astype(bf16)

    @pl.loop(0, m)
    def _(c):
        @pl.when(c > z)
        def _():
            to_up(c).wait_send()

        @pl.when(c < z)
        def _():
            to_down(c).wait_send()

    for cp in leave:
        cp.wait()
    pl.when(has_left)(kv_left.wait_send)
    pl.when(has_right)(kv_right.wait_send)
    for to_left, to_right in halos:
        pl.when(has_left)(to_left.wait_send)
        pl.when(has_right)(to_right.wait_send)


def relay_kernel(n, ag, x_hbm, oc_hbm, wq_hbm, wkv_hbm, wo_hbm, seg_ref, band_ref,
                 ctx_ref, ig_ref, kvg_ref, raw, wide_raw, x_ref, oc_ref, wall, wo_ref, q_ref, dc_ref,
                 kvx, kdocs, bias, grad, halo, hin, dall, wx, dout, dx, snd, rcv, tout, rin, part,
                 gt, gsum, sib, quart, got, mine, mix, piece, sib2,
                 ls, ks, kr, hs, hr, ss, sr, qs, qr, gs, gr, fs, fr,
                 zhs, zhr, zas, zar, pls, plr, pfs, pfr, pss, psr,
                 oqs, oqr, oks, okr, xqs, xqr, xks, xkr, rss, rsr, tos, tor, fas, far):
    tok, qc = q_ref.shape
    kvc = kvx.shape[1]
    ch = wall.shape[0] // 4
    blocks = tok // BLOCK
    kv_heads = kvc // (2 * HEAD_DIM)
    wide = GROUP * HEAD_DIM
    pair = 2 * HEAD_DIM
    held = ag * BLOCK
    me = lax.axis_index("seq")
    z = lax.axis_index("mp")
    core = me % 2
    sibling = me + 1 - 2 * core
    chip = me // 2
    chips = n // 2
    pr = ch // n
    outer = (z == 0) | (z == 3)
    inner = jnp.logical_not(outer)
    partner = jnp.where(outer, jnp.where(z == 0, 1, 2), jnp.where(z == 1, 0, 3))
    facing = 3 - z
    facing_partner = 3 - partner

    loads = [
        pltpu.make_async_copy(src, dst, ls.at[i])
        for i, (src, dst) in enumerate((
            (wkv_hbm, raw),
            (x_hbm, x_ref),
            (wq_hbm, wall.at[:, pl.ds(0, qc)]),
            (oc_hbm, oc_ref),
            (wo_hbm, wo_ref),
        ))
    ]
    for cp in loads:
        cp.start()

    def seq_dev(i):
        return (i, z)

    def mp_dev(i):
        return (me, i)

    barrier = pltpu.get_barrier_semaphore()
    has_left, has_right = me > 0, me < n - 1
    has_down, has_up = z > 0, z < 3

    def greet(dev):
        pl.semaphore_signal(barrier, inc=1, device_id=dev, device_id_type=MESH)

    for there, dev in (
        (has_left, seq_dev(me - 1)),
        (has_right, seq_dev(me + 1)),
        (has_down, mp_dev(z - 1)),
        (has_up, mp_dev(z + 1)),
    ):
        @pl.when(there)
        def _():
            greet(dev)
    for k in range(1, chips):
        greet(seq_dev(((chip + k) % chips) * 2 + core))
    peers = chips - 1
    for there in (has_left, has_right, has_down, has_up):
        peers = peers + there.astype(jnp.int32)
    pl.semaphore_wait(barrier, peers)

    def remote(src, dst, send, recv, dev):
        return pltpu.make_async_remote_copy(
            src_ref=src, dst_ref=dst, send_sem=send, recv_sem=recv, device_id=dev,
            device_id_type=MESH)

    qcols, kvcols = pl.ds(0, qc), pl.ds(qc, kvc)

    def rows_of(c):
        return pl.ds(pl.multiple_of(c * ch + me * pr, pr), pr)

    sent_chunks = (facing_partner, facing)
    zh = [[], []]
    for j, c in enumerate(sent_chunks):
        zh[0].append(remote(wq_hbm.at[rows_of(c), :], wx.at[j, chip, core, :, qcols], zhs.at[0, j], zhr.at[0, j], mp_dev(partner)))
        zh[1].append(remote(wall.at[rows_of(c), kvcols], wx.at[j, chip, core, :, kvcols], zhs.at[1, j], zhr.at[1, j], mp_dev(partner)))
    za = [[], [], []]
    if ag:
        za.append([])
        for j, c in enumerate((facing_partner, facing)):
            za[0].append(remote(wq_hbm.at[rows_of(c), :], wx.at[(2, 4)[j], chip, core, :, qcols], zas.at[0, j], zar.at[0, j], mp_dev(facing)))
            za[1].append(remote(wall.at[rows_of(c), kvcols], wx.at[(2, 4)[j], chip, core, :, kvcols], zas.at[1, j], zar.at[1, j], mp_dev(facing)))
            for i, cols in enumerate((qcols, kvcols)):
                za[2 + i].append(remote(
                    wx.at[1 - j, chip, core, :, cols], wx.at[(3, 5)[j], chip, core, :, cols],
                    zas.at[2 + i, j], zar.at[2 + i, j], mp_dev(facing)))

    def each(cps, what):
        for cp in cps:
            getattr(cp, what)()

    @pl.when(outer)
    def _():
        each(zh[0], "start")

    @pl.when(inner)
    def _():
        each(za[0], "start")

    xchip, ychip = chip + 1 - 2 * (chip % 2), (chip + 2) % chips
    dchip = (xchip + 2) % chips
    sets = ((0, 2), (2, 2), (4, 2))
    half = pr // 2
    to_x, to_y, via_x, via_y, to_sib = [], [], [], [], []
    for i, (first, count) in enumerate(sets):
        ksl = pl.ds(first, count)
        own = wx.at[ksl, chip, core]
        to_x.append(remote(own, own, pls.at[0, i], plr.at[0, i], seq_dev(xchip * 2 + core)))
        to_y.append(remote(own, own, pls.at[1, i], plr.at[1, i], seq_dev(ychip * 2 + core)))
        lo = wx.at[ksl, xchip, core, pl.ds(0, half)]
        hi = wx.at[ksl, ychip, core, pl.ds(half, half)]
        via_y.append(remote(lo, lo, pfs.at[0, i], pfr.at[0, i], seq_dev(ychip * 2 + core)))
        via_x.append(remote(hi, hi, pfs.at[1, i], pfr.at[1, i], seq_dev(xchip * 2 + core)))
        row = []
        for j, c in enumerate((chip, xchip, ychip, dchip)):
            block = wx.at[ksl, c, core]
            row.append(remote(block, block, pss.at[i, j], psr.at[i, j], seq_dev(sibling)))
        to_sib.append(row)

    def plane_start(i):
        to_x[i].start()
        to_y[i].start()
        to_sib[i][0].start()

    def plane_wait_x(i):
        first, count = sets[i]
        dst = wx.at[pl.ds(first, count), xchip, core]
        remote(dst, dst, pls.at[0, i], plr.at[0, i], seq_dev(sibling)).wait_recv()

    def plane_wait_y(i):
        first, count = sets[i]
        dst = wx.at[pl.ds(first, count), ychip, core]
        remote(dst, dst, pls.at[1, i], plr.at[1, i], seq_dev(sibling)).wait_recv()

    def plane_relay(i):
        plane_wait_x(i)
        via_y[i].start()
        to_sib[i][1].start()
        plane_wait_y(i)
        via_x[i].start()
        to_sib[i][2].start()

    def plane_pair(i):
        first, count = sets[i]
        for f, s in enumerate((pl.ds(0, half), pl.ds(half, half))):
            dst = wx.at[pl.ds(first, count), dchip, core, s]
            remote(dst, dst, pfs.at[f, i], pfr.at[f, i], seq_dev(sibling)).wait_recv()
        to_sib[i][3].start()

    def plane_done(i):
        first, count = sets[i]
        for j, c in enumerate((chip, xchip, ychip, dchip)):
            dst = wx.at[pl.ds(first, count), c, 1 - core]
            remote(dst, dst, pss.at[i, j], psr.at[i, j], seq_dev(sibling)).wait_recv()

    loads[0].wait()
    span = wide_raw.shape[0] // kv_heads

    @pl.loop(0, wall.shape[0] // span)
    def _(i):
        wide_raw[...] = raw[pl.ds(pl.multiple_of(i * span * kv_heads, 256), span * kv_heads), :].astype(f32)
        for g in range(kv_heads):
            wall[pl.ds(pl.multiple_of(i * span, 256), span), qc + g * 128 : qc + (g + 1) * 128] = (
                wide_raw[pl.ds(g, span, stride=kv_heads), :].astype(bf16)
            )

    @pl.when(outer)
    def _():
        each(zh[1], "start")

    @pl.when(inner)
    def _():
        each(za[1], "start")

    loads[1].wait()

    @pl.loop(0, tok // 256)
    def _(i):
        r = pl.ds(pl.multiple_of(i * 256, 256), 256)
        ro = pl.ds(pl.multiple_of(i * 256 + MARGIN, 256), 256)
        kvx[ro, :] = jnp.dot(x_ref[r, :], wall[:, qc:], preferred_element_type=f32).astype(bf16)

    before, after = pl.ds(0, MARGIN), pl.ds(MARGIN + tok, MARGIN)
    kv_left = remote(kvx.at[pl.ds(MARGIN, MARGIN)], kvx.at[after], ks.at[0], kr.at[0], seq_dev(me - 1))
    kv_right = remote(kvx.at[pl.ds(tok, MARGIN)], kvx.at[before], ks.at[1], kr.at[1], seq_dev(me + 1))
    pl.when(has_left)(kv_left.start)
    pl.when(has_right)(kv_right.start)

    for kb in range(blocks + 4):
        row = me * blocks + kb - 2
        inside = (row >= 0) & (row < n * blocks)
        docs = seg_ref[pl.ds(jnp.clip(row, 0, n * blocks - 1), 1), :]
        docs = jnp.where(inside, docs, -1)
        kdocs[kb] = jnp.transpose(jnp.broadcast_to(docs, (BLOCK, BLOCK)))

    @pl.loop(0, blocks)
    def _(b):
        qdoc = seg_ref[pl.ds(me * blocks + b, 1), :]
        for o in range(5):
            same = kdocs[b + o] == qdoc
            if o != 2:
                same = same & (band_ref[b, o if o < 2 else o - 1] == 1)
            bias[b, o * BLOCK : (o + 1) * BLOCK, :] = jnp.where(same, 0.0, -1e30).astype(f32)

    grad[...] = jnp.zeros_like(grad)
    loads[2].wait()

    @pl.when(inner)
    def _():
        each(zh[0], "wait_recv")
        each(za[2], "start")

    @pl.loop(0, tok // 256)
    def _(i):
        r = pl.ds(pl.multiple_of(i * 256, 256), 256)
        q_ref[r, :] = jnp.dot(x_ref[r, :], wall[:, :qc], preferred_element_type=f32).astype(bf16)

    @pl.when(inner)
    def _():
        each(zh[1], "wait_recv")
        each(za[3], "start")
        plane_start(0)

    loads[3].wait()
    loads[4].wait()

    @pl.loop(0, tok // 256)
    def _(i):
        r = pl.ds(pl.multiple_of(i * 256, 256), 256)
        dc_ref[r, :] = lax.dot_general(
            oc_ref[r, :], wo_ref[...], NT, preferred_element_type=f32
        ).astype(bf16)

    @pl.when(jnp.logical_not(has_left))
    def _():
        kvx[before, :] = jnp.zeros((MARGIN, kvc), bf16)
        for g in range(kv_heads):
            hin[1, g] = jnp.zeros(hin.shape[2:], bf16)

    @pl.when(jnp.logical_not(has_right))
    def _():
        kvx[after, :] = jnp.zeros((MARGIN, kvc), bf16)
        for g in range(kv_heads):
            hin[0, g] = jnp.zeros(hin.shape[2:], bf16)

    pl.when(has_left)(kv_right.wait_recv)
    pl.when(has_right)(kv_left.wait_recv)

    def block_rows(b):
        return pl.ds(pl.multiple_of(b * BLOCK, BLOCK), BLOCK)

    def dq_out(g, b):
        at = (block_rows(b), pl.ds(g * wide, wide))
        return remote(dall.at[at], dout.at[at], oqs.at[g, b], oqr.at[g, b], mp_dev(partner))

    def dq_across(which, g, b):
        at = (block_rows(b), pl.ds(g * wide, wide))
        src = dall.at[at] if which == 0 else dout.at[at]
        return remote(src, dx.at[(which,) + at], xqs.at[which, g, b], xqr.at[which, g, b], mp_dev(facing))

    def dkv_cols(g):
        return pl.ds(qc + g * pair, pair)

    def dkv_out(g, early):
        rows = pl.ds(0, held) if early else pl.ds(held, tok - held)
        at = (rows, dkv_cols(g))
        i = 1 if early else 0
        return remote(dall.at[at], dout.at[at], oks.at[g, i], okr.at[g, i], mp_dev(partner))

    def dkv_across(which, g):
        at = (pl.ds(0, held), dkv_cols(g))
        src = dall.at[at] if which == 0 else dout.at[at]
        return remote(src, dx.at[(which,) + at], xks.at[which, g], xkr.at[which, g], mp_dev(facing))

    def dkv_rest_across(g):
        at = (pl.ds(held, BLOCK), dkv_cols(g))
        return remote(dout.at[at], dx.at[(1,) + at], xks.at[2, g], xkr.at[2, g], mp_dev(facing))

    def halo_left(g):
        return remote(halo.at[0, g], hin.at[0, g], hs.at[0, g], hr.at[0, g], seq_dev(me - 1))

    def halo_right(g):
        return remote(halo.at[1, g], hin.at[1, g], hs.at[1, g], hr.at[1, g], seq_dev(me + 1))

    def finish_late(g):
        pl.when(has_right)(halo_left(g).wait_recv)
        dall[held:, qc + g * pair : qc + (g + 1) * pair] = (
            grad[MARGIN + held : MARGIN + tok, g * pair : (g + 1) * pair] + hin[0, g].astype(f32)
        ).astype(bf16)
        pl.when(outer)(dkv_out(g, False).start)

    def finish_early(g):
        pl.when(has_left)(halo_right(g).wait_recv)
        dall[:held, qc + g * pair : qc + (g + 1) * pair] = (
            grad[MARGIN : MARGIN + held, g * pair : (g + 1) * pair] + hin[1, g].astype(f32)
        ).astype(bf16)
        pl.when(outer)(dkv_out(g, True).start)
        pl.when(inner)(dkv_across(0, g).start)

    for g in range(kv_heads):
        cols = slice(g * wide, (g + 1) * wide)
        kcols = slice(g * pair, (g + 1) * pair)

        def attend(b):
            first = pl.multiple_of(b * BLOCK, BLOCK)
            qt = side_by_side(jnp.transpose(q_ref[pl.ds(first, BLOCK), cols] * SCALE))
            dct = side_by_side(jnp.transpose(dc_ref[pl.ds(first, BLOCK), cols]))
            zero = jnp.zeros_like(qt)
            qz = jnp.concatenate([qt, zero], axis=0)
            dcz = jnp.concatenate([zero, dct], axis=0)
            kv = kvx[pl.ds(first, WINDOW), kcols]
            kvt = jnp.transpose(kv)
            s = jnp.dot(kv, qz, preferred_element_type=f32)
            s = s + jnp.concatenate([bias[b]] * GROUP, axis=1)
            p = jnp.exp(s - jnp.max(s, axis=0, keepdims=True))
            w = p * (1.0 / jnp.sum(p, axis=0, keepdims=True))
            wh = w.astype(bf16)
            ctx = jnp.dot(kvt[HEAD_DIM:], wh, preferred_element_type=f32).astype(bf16)
            delta = jnp.sum(dct.astype(f32) * ctx.astype(f32), axis=0, keepdims=True)
            dp = jnp.dot(kv, dcz, preferred_element_type=f32)
            ds = (w * (dp - delta)).astype(bf16)
            dq = jnp.dot(kvt[:HEAD_DIM], ds, preferred_element_type=f32) * SCALE
            ctx_ref[pl.ds(first, BLOCK), cols] = jnp.transpose(stacked(ctx))
            dall[pl.ds(first, BLOCK), cols] = jnp.transpose(stacked(dq.astype(bf16)))
            d_kv = lax.dot_general(ds, qz, NT, preferred_element_type=f32)
            d_kv = d_kv + lax.dot_general(wh, dcz, NT, preferred_element_type=f32)
            grad[pl.ds(first, WINDOW), kcols] += d_kv

        @pl.loop(0, blocks // 2)
        def _(pair_index):
            for b in (2 * pair_index, 2 * pair_index + 1):
                attend(b)

            first_pair = pair_index == 0

            @pl.when(outer)
            def _():
                for b in (2 * pair_index, 2 * pair_index + 1):
                    dq_out(g, b).start()

            @pl.when(first_pair)
            def _():
                halo[0, g] = grad[:MARGIN, kcols].astype(bf16)
                pl.when(has_left)(halo_left(g).start)

            @pl.when(inner & first_pair)
            def _():
                for b in range(2):
                    dq_across(0, g, b).start()
                if g == 0:
                    each(za[0] + za[1] + za[2] + za[3], "wait_recv")
                    plane_start(1)
                if g == 1:
                    plane_relay(1)

            @pl.when(inner & jnp.logical_not(first_pair))
            def _():
                for b in range(2):
                    dq_out(g, b).wait_recv()
                    dq_across(1, g, b).start()
                if g == 0:
                    plane_relay(0)
                if g == 1:
                    plane_pair(0)

            if g == 1:
                @pl.when(first_pair)
                def _():
                    finish_early(0)
                    finish_late(0)

        halo[1, g] = grad[MARGIN + tok :, kcols].astype(bf16)
        pl.when(has_right)(halo_right(g).start)

    def chunk(c):
        return pl.ds(pl.multiple_of(c * ch, ch), ch)

    def times_own(r, c):
        return lax.dot_general(dall[r, :], wall[chunk(c), :], NT, preferred_element_type=f32)

    def times_sent(d, k):
        return lax.dot_general(d, wx[k].reshape(ch, qc + kvc), NT, preferred_element_type=f32)

    summed = tok - held
    last = kv_heads - 1

    def sum_piece(slot, i):
        at = (slot, pl.ds(i * BLOCK, BLOCK))
        return remote(snd.at[at], rcv.at[at], rss.at[slot, i], rsr.at[slot, i], mp_dev(facing))

    def out_piece(i):
        at = block_rows(i)
        return remote(tout.at[at], rin.at[at], tos.at[i], tor.at[i], mp_dev(partner))

    early, late = slice(0, held), slice(held, tok)
    cut = qc + kvc - pair

    finish_late(1)

    @pl.when(inner)
    def _():
        dkv_out(0, True).wait_recv()
        dkv_across(1, 0).start()
        part[0] = times_own(late, facing_partner)

    @pl.when(outer)
    def _():
        tout[late, :] = times_own(late, partner).astype(bf16)

    finish_early(1)

    @pl.when(inner)
    def _():
        plane_start(2)
        plane_pair(1)
        part[4] = times_own(early, partner)

    @pl.when(outer)
    def _():
        tout[early, :] = times_own(early, partner).astype(bf16)
        part[3] = times_own(late, z)
        part[5] = times_own(early, z)
        dkv_out(last, False).wait_send()
        dkv_out(last, True).wait_send()
        for i in range(blocks):
            out_piece(i).start()

    pw = gt.shape[3]
    gr_rows = pw * kv_heads
    dkvt = jnp.transpose(dall[:, qc:])
    for k in range(2):
        own_half = (1 - core) if k == 0 else core

        @pl.loop(0, chips)
        def _(j):
            cols = pl.ds(pl.multiple_of((2 * j + own_half) * pw, pw), pw)
            prod = jnp.dot(dkvt, x_ref[:, cols], preferred_element_type=f32)
            if k == 0:
                gt[0, j] = prod.astype(bf16)
            else:
                gsum[j] = prod

        if k == 0:
            swap = remote(gt.at[0], sib, ss, sr, seq_dev(sibling))
            swap.start()

    swap.wait_recv()

    def other(k):
        return (chip + k) % chips

    sends = []
    for k in range(1, chips):
        j = other(k)
        gt[1, j] = (gsum[j] + sib[j].astype(f32)).astype(bf16)
        cp = remote(gt.at[1, j], quart.at[k], qs.at[k], qr.at[k], seq_dev(j * 2 + core))
        cp.start()
        sends.append(cp)
    mine[...] = gsum[chip] + sib[chip].astype(f32)
    swap.wait_send()

    def times_cut(d, k):
        return lax.dot_general(
            d, wx[k, :, :, :, :cut].reshape(ch, cut), NT, preferred_element_type=f32)

    def rest_on():
        src = dx.at[1, pl.ds(0, held + BLOCK), pl.ds(cut, pair)]
        return remote(src, src, fas.at[0], far.at[0], mp_dev(partner))

    def rest_rows_on():
        src = wx.at[3, :, :, :, pl.ds(cut, pair)]
        return remote(src, src, fas.at[1], far.at[1], mp_dev(partner))

    @pl.when(inner)
    def _():
        for g in range(last):
            dkv_out(g, False).wait_recv()
        plane_done(0)
        for b in range(ag, ag + 1):
            for g in range(kv_heads):
                dq_out(g, b).wait_recv()
            i = b - ag
            r = slice(b * BLOCK, (b + 1) * BLOCK)
            snd[1, i * BLOCK : (i + 1) * BLOCK, :] = (
                part[0, i * BLOCK : (i + 1) * BLOCK, :] + times_cut(dout[r, :cut], 1)
            ).astype(bf16)
            sum_piece(1, i).start()
        plane_done(1)
        rest_rows_on().start()
        for which in range(2):
            for g in range(kv_heads):
                for b in range(ag):
                    dq_across(which, g, b).wait_recv()
                if which == 0 or g < last:
                    dkv_across(which, g).wait_recv()
        tout[early, :] = (
            part[4] + times_sent(dx[0, early, :], 2) + times_cut(dx[1, early, :cut], 3)
        ).astype(bf16)
        for i in range(ag):
            out_piece(i).start()

    @pl.when(inner)
    def _():
        for j, c in ((1, facing), (2, partner), (3, z)):
            part[j] = times_own(late, c)
        part[5] = times_own(early, z)
        plane_relay(2)
        for b in range(ag + 1, blocks):
            for g in range(kv_heads):
                dq_out(g, b).wait_recv()
        dkv_out(last, False).wait_recv()
        for b in range(ag + 1, blocks):
            i = b - ag
            r = slice(b * BLOCK, (b + 1) * BLOCK)
            snd[1, i * BLOCK : (i + 1) * BLOCK, :] = (
                part[0, i * BLOCK : (i + 1) * BLOCK, :] + times_sent(dout[r, :], 1)
            ).astype(bf16)
            sum_piece(1, i).start()
        dkv_rest_across(last).start()
        dkv_out(last, True).wait_recv()
        dkv_across(1, last).start()
        snd[0] = (part[1] + times_sent(dout[late, :], 0)).astype(bf16)
        for i in range(blocks - ag):
            sum_piece(0, i).start()

    @pl.when(inner)
    def _():
        for i in range(summed // BLOCK):
            r = slice(held + i * BLOCK, held + (i + 1) * BLOCK)
            p = slice(i * BLOCK, (i + 1) * BLOCK)
            sum_piece(1, i).wait_recv()
            tout[r, :] = (part[2, p, :] + rcv[1, p, :].astype(f32)).astype(bf16)
            out_piece(ag + i).start()

    for cp in sends:
        cp.wait_recv()
    for k in range(1, chips):
        mine[...] += quart[k].astype(f32)
    for cp in sends:
        cp.wait_send()
    done = jnp.transpose(mine[...])
    for g in range(kv_heads):
        kcols = slice(g * pair, (g + 1) * pair)
        mix[pl.ds(g, pw, stride=kv_heads), :] = done[:, kcols]
    piece[...] = mix[...].astype(bf16)
    sends = []
    for k in range(1, chips):
        cp = remote(piece, got.at[k], gs.at[k], gr.at[k], seq_dev(other(k) * 2 + core))
        cp.start()
        sends.append(cp)

    @pl.when(inner)
    def _():
        dkv_across(1, last).wait_recv()
        dkv_rest_across(last).wait_recv()
        rest_on().start()
        plane_pair(2)
        plane_done(2)
        for i in range(ag):
            out_piece(i).wait_recv()
        ig_ref[early, :] = (
            part[5] + rin[early, :].astype(f32)
            + times_sent(dx[0, early, :], 4) + times_sent(dx[1, early, :], 5)
        ).astype(bf16)

    got[0] = piece[...]
    swaps = []
    for j in range(chips):
        if j:
            sends[j - 1].wait()
        swaps.append(remote(got.at[j], sib2.at[j], fs.at[j], fr.at[j], seq_dev(sibling)))
        swaps[-1].start()
        src = (chip + chips - j) % chips
        kvg_ref[pl.ds(pl.multiple_of((2 * src + core) * gr_rows, gr_rows), gr_rows), :] = got[j]
    for j in range(chips):
        swaps[j].wait_recv()
        src = (chip + chips - j) % chips
        kvg_ref[pl.ds(pl.multiple_of((2 * src + 1 - core) * gr_rows, gr_rows), gr_rows), :] = sib2[j]
    for cp in swaps:
        cp.wait_send()

    @pl.when(inner)
    def _():
        for i in range(ag, blocks):
            out_piece(i).wait_recv()
        for i in range(summed // BLOCK):
            sum_piece(0, i).wait_recv()
        ig_ref[late, :] = (part[3] + rin[late, :].astype(f32) + rcv[0].astype(f32)).astype(bf16)

    @pl.when(outer)
    def _():
        rest_rows_on().wait_recv()
        for i in range(blocks):
            out_piece(i).wait_recv()
        rest_on().wait_recv()
        tail = slice(held + BLOCK, tok)
        ig_ref[tail, :] = (part[3, BLOCK:, :] + rin[tail, :].astype(f32)).astype(bf16)
        for r, mine_part in ((early, part[5]), (slice(held, held + BLOCK), part[3, :BLOCK, :])):
            far_part = lax.dot_general(
                dx[1, r, cut:], wx[3, :, :, :, cut:].reshape(ch, pair), NT, preferred_element_type=f32)
            ig_ref[r, :] = (mine_part + far_part + rin[r, :].astype(f32)).astype(bf16)

    @pl.when(outer)
    def _():
        for g in range(kv_heads):
            for b in range(blocks):
                dq_out(g, b).wait_send()
            if g < last:
                dkv_out(g, False).wait_send()
                dkv_out(g, True).wait_send()
        each(zh[0], "wait_send")
        each(zh[1], "wait_send")

    @pl.when(inner)
    def _():
        for which in range(2 if ag else 0):
            for g in range(kv_heads):
                for b in range(ag):
                    dq_across(which, g, b).wait_send()
                dkv_across(which, g).wait_send()
        dkv_rest_across(last).wait_send()
        rest_on().wait_send()
        rest_rows_on().wait_send()
        for slot in range(2):
            for i in range(blocks - ag):
                sum_piece(slot, i).wait_send()
        for group in za:
            each(group, "wait_send")
        for group in (to_x, to_y, via_x, via_y, *to_sib):
            each(group, "wait_send")

    for i in range(blocks):
        out_piece(i).wait_send()
    pl.when(has_left)(kv_left.wait_send)
    pl.when(has_right)(kv_right.wait_send)
    for g in range(kv_heads):
        pl.when(has_left)(halo_left(g).wait_send)
        pl.when(has_right)(halo_right(g).wait_send)


def write_kernel(ctx_hbm, ig_hbm, kvg_hbm, ctx_out, ig_out, kvg_out, half, full, ctx_mid, ig_mid, ins, outs):
    pieces, rows = half.shape[0], half.shape[1]
    loads, stores = [], []
    for i in range(pieces):
        loads.append(pltpu.make_async_copy(kvg_hbm.at[pl.ds(i * rows, rows)], half.at[i], ins.at[i]))
        stores.append(pltpu.make_async_copy(full.at[i], kvg_out.at[pl.ds(i * rows, rows)], outs.at[i]))
        loads[i].start()
    for i, (src, mid, dst) in enumerate(((ctx_hbm, ctx_mid, ctx_out), (ig_hbm, ig_mid, ig_out))):
        loads.append(pltpu.make_async_copy(src, mid, ins.at[pieces + i]))
        stores.append(pltpu.make_async_copy(mid, dst, outs.at[pieces + i]))
        loads[-1].start()
    for i in range(pieces):
        loads[i].wait()
        full[i] = half[i].astype(f32)
        stores[i].start()
    for i in range(pieces, pieces + 2):
        loads[i].wait()
        stores[i].start()
    for cp in stores:
        cp.wait()


def store_kernel(ctx_ref, ig_ref, kvg_ref, ctx_out, ig_out, kvg_out, full, outs):
    pieces, rows = full.shape[0], full.shape[1]
    stores = [
        pltpu.make_async_copy(ctx_ref, ctx_out, outs.at[pieces]),
        pltpu.make_async_copy(ig_ref, ig_out, outs.at[pieces + 1]),
    ]
    for cp in stores:
        cp.start()
    for i in range(pieces):
        full[i] = kvg_ref[i * rows : (i + 1) * rows, :].astype(f32)
        stores.append(pltpu.make_async_copy(full.at[i], kvg_out.at[pl.ds(i * rows, rows)], outs.at[i]))
        stores[-1].start()
    for cp in stores:
        cp.wait()


def stored(*arrays):
    pieces = 4
    rows, lanes = arrays[2].shape[0] // pieces, arrays[2].shape[1]
    return pl.pallas_call(
        store_kernel,
        out_shape=[
            jax.ShapeDtypeStruct(a.shape, t) for a, t in zip(arrays, (bf16, bf16, f32))
        ],
        in_specs=[VMEM] * 3,
        out_specs=[ANY] * 3,
        scratch_shapes=[
            pltpu.VMEM((pieces, rows, lanes), f32),
            pltpu.SemaphoreType.DMA((pieces + 2,)),
        ],
        compiler_params=pltpu.CompilerParams(vmem_limit_bytes=30 * 2**20),
        name="store",
    )(*arrays)


def written(*arrays):
    pieces = 4
    rows, lanes = arrays[2].shape[0] // pieces, arrays[2].shape[1]
    return pl.pallas_call(
        write_kernel,
        out_shape=[
            jax.ShapeDtypeStruct(a.shape, t) for a, t in zip(arrays, (bf16, bf16, f32))
        ],
        in_specs=[ANY] * 3,
        out_specs=[ANY] * 3,
        scratch_shapes=[
            pltpu.VMEM((pieces, rows, lanes), bf16),
            pltpu.VMEM((pieces, rows, lanes), f32),
            pltpu.VMEM(arrays[0].shape, bf16),
            pltpu.VMEM(arrays[1].shape, bf16),
            pltpu.SemaphoreType.DMA((pieces + 2,)),
            pltpu.SemaphoreType.DMA((pieces + 2,)),
        ],
        compiler_params=pltpu.CompilerParams(vmem_limit_bytes=60 * 2**20),
        name="write",
    )(*arrays)


def local(n, m, normed, out_cotangent, segments, band_mask, query_weight, key_value_weight, out_weight):
    tok, width = normed.shape
    qc = query_weight.shape[1]
    kv_heads = key_value_weight.shape[1]
    pair = 2 * HEAD_DIM
    kvc = kv_heads * pair
    wkv = key_value_weight.reshape(width * kv_heads, pair)
    blocks = tok // BLOCK
    ch = width // m
    pw = width // n
    sum_seq = n % 2 == 0 and n * 128 <= width and width % (n * 128) == 0
    chips = n // 2
    dma = pltpu.SemaphoreType.DMA
    vmem = pltpu.VMEM
    relay = n == 8 and m == 4 and kv_heads == 2 and tok == 4 * BLOCK and sum_seq
    scratch = [
        vmem((tok, qc), bf16),
        vmem((width * kv_heads, pair), bf16),
        vmem((256 * kv_heads, pair), f32),
        vmem((tok, width), bf16),
        vmem((tok, width), bf16),
        vmem((width, qc), bf16),
        vmem((width, kvc), bf16),
        vmem((qc, width), bf16),
        vmem((tok, qc), bf16),
        vmem((tok, qc), bf16),
        vmem((tok + 2 * MARGIN, kvc), bf16),
        vmem((blocks + 4, BLOCK, BLOCK), jnp.int32),
        vmem((blocks, WINDOW, BLOCK), f32),
        vmem((tok + 2 * MARGIN, kvc), f32),
        vmem((2, kv_heads, MARGIN, pair), bf16),
        vmem((2, kv_heads, MARGIN, pair), bf16),
        vmem((tok, qc), bf16),
        vmem((tok, kvc), bf16),
        vmem((m, tok, ch), bf16),
        vmem((m + 1, tok, ch), bf16),
        dma((5,)),
        dma((1 + n,)),
        dma((2,)),
        dma((2,)),
        dma((2, kv_heads)),
        dma((2, kv_heads)),
        dma((m,)),
        dma((m + 1,)),
    ]
    if sum_seq:
        kvg_shape = (width * kv_heads, pair)
        if not relay:
            scratch += [
                vmem((2, chips, kvc, pw), bf16),
                vmem((chips, kvc, pw), f32),
                vmem((chips, kvc, pw), bf16),
                vmem((chips, kvc, pw), bf16),
                vmem((chips, pw * kv_heads, pair), bf16),
                vmem((kvc, pw), f32),
                vmem((pw * kv_heads, pair), f32),
                vmem((pw * kv_heads, pair), bf16),
                vmem((chips, pw * kv_heads, pair), bf16),
                dma, dma, dma((chips,)), dma((chips,)), dma((chips,)), dma((chips,)), dma, dma,
            ]
    else:
        kvg_shape = (tok, kvc)
    ag = AHEAD
    held = ag * BLOCK
    relay_scratch = [
        vmem((width * kv_heads, pair), bf16),
        vmem((256 * kv_heads, pair), f32),
        vmem((tok, width), bf16),
        vmem((tok, width), bf16),
        vmem((width, qc + kvc), bf16),
        vmem((qc, width), bf16),
        vmem((tok, qc), bf16),
        vmem((tok, qc), bf16),
        vmem((tok + 2 * MARGIN, kvc), bf16),
        vmem((blocks + 4, BLOCK, BLOCK), jnp.int32),
        vmem((blocks, WINDOW, BLOCK), f32),
        vmem((tok + 2 * MARGIN, kvc), f32),
        vmem((2, kv_heads, MARGIN, pair), bf16),
        vmem((2, kv_heads, MARGIN, pair), bf16),
        vmem((tok, qc + kvc), bf16),
        vmem((6, max(chips, 1), 2, max(ch // n, 8), qc + kvc), bf16),
        vmem((tok, qc + kvc), bf16),
        vmem((2, tok, qc + kvc), bf16),
        vmem((2, max(tok - held, BLOCK), ch), bf16),
        vmem((2, max(tok - held, BLOCK), ch), bf16),
        vmem((tok, ch), bf16),
        vmem((tok, ch), bf16),
        vmem((6, MARGIN, ch), f32),
        vmem((2, chips, kvc, pw), bf16),
        vmem((chips, kvc, pw), f32),
        vmem((chips, kvc, pw), bf16),
        vmem((chips, kvc, pw), bf16),
        vmem((chips, pw * kv_heads, pair), bf16),
        vmem((kvc, pw), f32),
        vmem((pw * kv_heads, pair), f32),
        vmem((pw * kv_heads, pair), bf16),
        vmem((chips, pw * kv_heads, pair), bf16),
        dma((5,)),
        dma((2,)),
        dma((2,)),
        dma((2, kv_heads)),
        dma((2, kv_heads)),
        dma, dma, dma((chips,)), dma((chips,)), dma((chips,)), dma((chips,)), dma((chips,)), dma((chips,)),
        dma((2, 2)), dma((2, 2)),
        dma((4, 2)), dma((4, 2)),
        dma((2, 3)), dma((2, 3)),
        dma((2, 3)), dma((2, 3)),
        dma((3, 4)), dma((3, 4)),
        dma((kv_heads, blocks)), dma((kv_heads, blocks)),
        dma((kv_heads, 2)), dma((kv_heads, 2)),
        dma((2, kv_heads, ag)), dma((2, kv_heads, ag)),
        dma((3, kv_heads)), dma((3, kv_heads)),
        dma((2, blocks - ag)), dma((2, blocks - ag)),
        dma((blocks,)), dma((blocks,)),
        dma((2,)), dma((2,)),
    ]
    if relay:
        scratch = relay_scratch
        body = functools.partial(relay_kernel, n, ag)
        shapes = [vmem((tok, qc), bf16), vmem((tok, ch), bf16), vmem(kvg_shape, bf16)]
        out_specs = [VMEM] * 3
    else:
        body = functools.partial(fused_kernel, n, m, sum_seq)
        shapes = [
            jax.ShapeDtypeStruct((tok, qc), bf16),
            jax.ShapeDtypeStruct((tok, ch), bf16),
            jax.ShapeDtypeStruct(kvg_shape, bf16),
        ]
        out_specs = [ANY, VMEM, ANY]
    context, input_grad, other = pl.pallas_call(
        body,
        out_shape=shapes,
        in_specs=[ANY] * 5 + [VMEM, SMEM],
        out_specs=out_specs,
        scratch_shapes=scratch,
        compiler_params=pltpu.CompilerParams(
            vmem_limit_bytes=56 * 2**20, collective_id=0, has_side_effects=True
        ),
        name="fused",
    )(normed, out_cotangent, query_weight, wkv, out_weight, segments.reshape(-1, BLOCK), band_mask)
    if relay:
        context, input_grad, kv_grad = stored(context, input_grad, other)
    elif sum_seq:
        context, input_grad, kv_grad = written(context, input_grad, other)
    else:
        kv_grad = lax.dot_general(normed, other, (((0,), (0,)), ((), ())), preferred_element_type=f32)
        kv_grad = lax.psum(kv_grad, "seq")
    return context, input_grad, kv_grad.reshape(width, kv_heads, pair)


def solution(mesh):
    placed = (
        P("seq", None),
        P("seq", None),
        P(),
        P("seq", None),
        P(None, "mp"),
        P(None, "mp", None),
        P("mp", None),
    )
    return jax.shard_map(
        functools.partial(local, mesh.shape["seq"], mesh.shape["mp"]),
        mesh=mesh,
        in_specs=placed,
        out_specs=(P("seq", "mp"), P("seq", "mp"), P(None, "mp", None)),
        check_vma=False,
    )
```
